32 devices in a mesh: grp: 2 (over x), row: 16 (over z, y, core).
Axes of the slice: x: 2, y: 2, z: 4, core: 2. Of those that a mesh axis runs over, the one named last changes fastest.
Arguments:
- features: float32 [8, 32768], P(None, ('grp', 'row')), parts along dimension 1, may hold values from -6 to 6
- lengthscale: float32 [8], replicated, may hold values from 1 to 3
- noise: float32 [32768], P(('grp', 'row')), parts along dimension 0, may hold values from 0.1 to 1
- rhs: float32 [8, 32768], P(None, ('grp', 'row')), parts along dimension 1, may hold values from -15 to 15, as said below
Outputs:
- solution: float32 [8, 32768], P(None, ('grp', 'row')), parts along dimension 1
- residual: float32 [8, 32768], P(None, ('grp', 'row')), parts along dimension 1
The draws below stay inside these ranges and needn't reach their ends.
There are 2 independent parts, one for each index of `grp`. The reference program is written for one: setup_inputs(seed, part) draws one part's arguments, and reference() takes and returns one part's arrays. A program takes and returns all parts, laid end to end along the dimension named above; an argument that names none is the same for every part. Nothing has to cross between parts.
Inputs may be any that keep to these rules, and one draw needn't show every extreme that they name: `rhs`: real values of order one.
All inputs are finite; a program needn't handle non-finite values.
Results may differ from the reference program's by a relative error of at most 0.00013.
Values sent between devices are 32-bit elements; how exact they have to be, the bound alone decides.
No kernel may reach another device: no remote copies, remote signals or barrier semaphores. Data moves between devices by JAX's collectives and lax.ppermute only.
A program may use at most 64 MiB of HBM per device.

```python
import math
import jax
import jax.numpy as jnp
from jax import lax

F = 8
RHS = 8
ITERS = 2
NPTS = 16384


def draw_rhs(key, part):
    key = jax.random.fold_in(key, 7)
    base = jnp.clip(jax.random.normal(key, (RHS, NPTS), jnp.float32), -5.0, 5.0)
    ramp = 1.0 + 2.0 * jnp.arange(NPTS, dtype=jnp.float32) / NPTS
    return (base * ramp[None, :]).astype(jnp.float32)


def steps_of(own_key, extent, cuts, least, top_value):
    factor_of = 1.0
    for position, shards_of in cuts:
        heights = jax.random.uniform(jax.random.fold_in(jax.random.fold_in(own_key, 6), position), (shards_of,), jnp.float32, least / len(cuts), top_value / len(cuts))
        factor_of = factor_of * jnp.repeat(jnp.exp(heights), extent[position] // shards_of).reshape((-1,) + (1,) * (len(extent) - 1 - position))
    return factor_of


def centred(own_key, dims, scale, most, split=(), kind=jnp.bfloat16):
    result = jax.random.normal(own_key, dims, jnp.float32) * scale
    if len(split) > 0:
        result = steps_of(own_key, dims, split, -0.22, 0.18) * result
    return jnp.clip(result, min=-most, max=most).astype(kind)


def setup_inputs(seed: int = 0, part: int = 0) -> dict:
    key_of = jax.random.split(jax.random.key(seed), 5)
    part_keys = jax.random.split(jax.random.fold_in(key_of[4], part), 5)
    features = centred(part_keys[0], (F, NPTS), 1.0, 6.0, ((1, 16),), jnp.float32)
    lengthscale = jnp.clip(jnp.exp(jax.random.uniform(key_of[1], (F,), jnp.float32, math.log(1.0), math.log(3.0))), 1.0, 3.0)
    noise = jnp.clip(jnp.exp(math.log(1.0) - 2.3025851 * jax.random.uniform(part_keys[2], (NPTS,), jnp.float32) ** steps_of(part_keys[2], (NPTS,), ((0, 16),), -0.2, 0.2)), 0.1, 1.0)
    rhs = draw_rhs(jax.random.fold_in(jax.random.fold_in(key_of[4], part), 71), part)
    return dict(features=features, lengthscale=lengthscale, noise=noise, rhs=rhs)


def block_term(mine, mine_sq, pts, dirs):
    pts_sq = lax.optimization_barrier(jnp.sum(pts * pts, axis=0))
    cross = lax.dot_general(mine, pts, (((0,), (0,)), ((), ())), precision=lax.Precision.HIGHEST, preferred_element_type=jnp.float32)
    weight = jnp.exp(-0.5 * (mine_sq[:, None] + pts_sq[None, :] - 2.0 * cross))
    return lax.dot_general(dirs, weight, (((1,), (1,)), ((), ())), precision=lax.Precision.HIGHEST, preferred_element_type=jnp.float32)

def reference(features, lengthscale, noise, rhs):
    scaled = features / lengthscale[:, None]
    scaled_sq = lax.optimization_barrier(jnp.sum(scaled * scaled, axis=0))
    amplitude = 1.0 / math.sqrt(NPTS)
    width = math.gcd(NPTS, 1024)
    count = NPTS // width
    col_blocks = jnp.transpose(scaled.reshape(F, count, width), (1, 0, 2))

    def apply(direc):
        dir_blocks = jnp.transpose(direc.reshape(RHS, count, width), (1, 0, 2))

        def step_fn(carry, block):
            return (carry + block_term(scaled, scaled_sq, block[0], block[1]), None)
        total, unused = lax.scan(step_fn, jnp.zeros((RHS, NPTS), jnp.float32), (col_blocks, dir_blocks))
        return amplitude * total + noise[None, :] * direc
    solution = jnp.zeros_like(rhs)
    residual = rhs
    direc = rhs
    norm_now = lax.optimization_barrier(jnp.sum(residual * residual, axis=1))
    for step in range(ITERS):
        image = apply(direc)
        alpha = norm_now / lax.optimization_barrier(jnp.sum(direc * image, axis=1))
        solution = solution + alpha[:, None] * direc
        residual = residual - alpha[:, None] * image
        if step + 1 < ITERS:
            norm_next = lax.optimization_barrier(jnp.sum(residual * residual, axis=1))
            direc = residual + (norm_next / norm_now)[:, None] * direc
            norm_now = norm_next
    return (solution, residual)
```

```python
import functools
import math

import jax
import jax.numpy as jnp
from jax import lax
from jax.experimental import pallas as pl
from jax.experimental.pallas import tpu as pltpu
from jax.sharding import PartitionSpec as P

ITERS = 2
LOG2E = math.log2(math.e)
DEPTH = 64
TILE = 256
F32 = jnp.float32
BF16 = jnp.bfloat16


def shifted(value, by):
    length = lax.axis_size("row")
    return lax.ppermute(value, "row", [(i, (i + by) % length) for i in range(length)])


def gathered(value):
    return [value] + [shifted(value, by) for by in range(1, lax.axis_size("row"))]


def pieces(value, count):
    parts = []
    for _ in range(count):
        part = value.astype(BF16).astype(F32)
        parts.append(part)
        value = value - part
    return parts


def exponent_rows(points, factor, visiting):
    big, mid, low = pieces(points * factor, 3)
    half_sq = jnp.sum(points * points, axis=0, keepdims=True) * (-0.5 * LOG2E)
    sq_parts = pieces(half_sq, 3)
    row = lax.broadcasted_iota(jnp.int32, points.shape, 0)
    first = 0 if visiting else 3
    tail = jnp.where((row >= 3 - first) & (row < 6 - first), 1.0, 0.0)
    for k, part in enumerate(sq_parts):
        tail = jnp.where(row == first + k, part, tail)
    order = [big, big, big, mid, mid, low] if visiting else [big, mid, low, big, mid, big]
    return jnp.concatenate(order + [tail, jnp.zeros_like(tail)], axis=0)


def operator_loop(yt_ref, own_ref, dirs_ref, acc_ref):
    width = own_ref.shape[1]
    acc_ref[...] = jnp.zeros_like(acc_ref)

    def step(t, carry):
        rows = pl.ds(pl.multiple_of(t * TILE, TILE), TILE)
        lhs = yt_ref[rows, :]
        dirs = dirs_ref[t]
        for c in range(width // TILE):
            cols = slice(c * TILE, (c + 1) * TILE)
            expo = jnp.dot(lhs, own_ref[:, cols], preferred_element_type=F32)
            weight = jnp.exp2(expo)
            high = weight.astype(BF16)
            low = (weight - high.astype(F32)).astype(BF16)
            acc_ref[:, cols] += jnp.dot(
                dirs, high, preferred_element_type=F32
            ) + jnp.dot(dirs, low, preferred_element_type=F32)
        return carry

    lax.fori_loop(0, dirs_ref.shape[0], step, 0)


def put_dirs(dirs_ref, block, value):
    both = jnp.concatenate(pieces(value, 2), axis=0).astype(BF16)
    per = value.shape[1] // TILE
    for k in range(per):
        dirs_ref[block * per + k] = both[:, k * TILE : (k + 1) * TILE]


def prepare_points(scale_ref, blocks, nfeat, yt_ref, own_ref):
    width = blocks[0].shape[1]
    for b, ref in enumerate(blocks):
        points = ref[0:nfeat, :] / scale_ref[...]
        rows = exponent_rows(points, LOG2E, True)
        yt_ref[b * width : (b + 1) * width, :] = rows.T.astype(BF16)
        if b == 0:
            own_ref[...] = exponent_rows(points, 1.0, False).astype(BF16)


def first_kernel(nfeat, amplitude, scale_ref, noise_ref, *refs):
    *blocks, image_ref, yt_ref, own_ref, dirs_ref, acc_ref = refs
    prepare_points(scale_ref, blocks, nfeat, yt_ref, own_ref)
    for b, ref in enumerate(blocks):
        put_dirs(dirs_ref, b, ref[nfeat:, :])
    operator_loop(yt_ref, own_ref, dirs_ref, acc_ref)
    nrhs = image_ref.shape[0]
    total = acc_ref[0:nrhs, :] + acc_ref[nrhs:, :]
    image_ref[...] = amplitude * total + noise_ref[...] * blocks[0][nfeat:, :]


def second_kernel(nfeat, amplitude, count, scale_ref, noise_ref, *refs):
    blocks = refs[:count]
    images = refs[count : 2 * count]
    outs = refs[2 * count :]
    sol_ref, res_ref, dir_ref, image_ref, norm_ref, curv_ref = outs[:6]
    yt_ref, own_ref, dirs_ref, acc_ref = outs[6:]
    prepare_points(scale_ref, blocks, nfeat, yt_ref, own_ref)
    norm = sum(jnp.sum(b[nfeat:, :] * b[nfeat:, :], axis=1, keepdims=True) for b in blocks)
    curv = sum(
        jnp.sum(b[nfeat:, :] * m[...], axis=1, keepdims=True) for b, m in zip(blocks, images)
    )
    alpha = norm / curv
    norm_next = 0.0
    for b, m in zip(blocks, images):
        left = b[nfeat:, :] - alpha * m[...]
        norm_next += jnp.sum(left * left, axis=1, keepdims=True)
    beta = norm_next / norm
    for k, (b, m) in enumerate(zip(blocks, images)):
        direc = (b[nfeat:, :] - alpha * m[...]) + beta * b[nfeat:, :]
        put_dirs(dirs_ref, k, direc)
    rhs = blocks[0][nfeat:, :]
    residual = rhs - alpha * images[0][...]
    direc = residual + beta * rhs
    sol_ref[...] = alpha * rhs
    res_ref[...] = residual
    dir_ref[...] = direc
    operator_loop(yt_ref, own_ref, dirs_ref, acc_ref)
    nrhs = image_ref.shape[0]
    total = acc_ref[0:nrhs, :] + acc_ref[nrhs:, :]
    image = amplitude * total + noise_ref[...] * direc
    image_ref[...] = image
    norm_ref[...] = jnp.broadcast_to(norm_next, norm_ref.shape)
    curv_ref[...] = jnp.broadcast_to(
        jnp.sum(direc * image, axis=1, keepdims=True), curv_ref.shape
    )


def last_kernel(sol_ref, res_ref, dir_ref, image_ref, norm_ref, *refs):
    *curvs, out_sol, out_res = refs
    alpha = norm_ref[:, 0:1] / sum(c[:, 0:1] for c in curvs)
    out_sol[...] = sol_ref[...] + alpha * dir_ref[...]
    out_res[...] = res_ref[...] - alpha * image_ref[...]


def shards(features, lengthscale, noise, rhs):
    nfeat, width = features.shape
    nrhs = rhs.shape[0]
    count = lax.axis_size("row")
    amplitude = 1.0 / math.sqrt(width * count)
    scale = lengthscale[:, None]
    noise = noise[None, :]
    blocks = gathered(jnp.concatenate([features, rhs], axis=0))
    field = jax.ShapeDtypeStruct((nrhs, width), F32)
    small = jax.ShapeDtypeStruct((nrhs, 128), F32)
    scratch = [
        pltpu.VMEM((count * width, DEPTH), BF16),
        pltpu.VMEM((DEPTH, width), BF16),
        pltpu.VMEM((count * width // TILE, 2 * nrhs, TILE), BF16),
        pltpu.VMEM((2 * nrhs, width), F32),
    ]
    entries = count * width * width
    params = pltpu.CompilerParams(
        vmem_limit_bytes=min(16 * 1024 * 1024 + 512 * count * width, 60 * 1024 * 1024)
    )
    cost = pl.CostEstimate(
        flops=2 * entries * (DEPTH + 4 * nrhs),
        bytes_accessed=4 * count * (nfeat + nrhs) * width,
        transcendentals=entries,
    )
    image = pl.pallas_call(
        functools.partial(first_kernel, nfeat, amplitude),
        out_shape=field,
        scratch_shapes=scratch,
        compiler_params=params,
        cost_estimate=cost,
        name="first_operator",
    )(scale, noise, *blocks)
    images = gathered(image)
    sol, res, direc, image, norm, curv = pl.pallas_call(
        functools.partial(second_kernel, nfeat, amplitude, count),
        out_shape=(field, field, field, field, small, small),
        scratch_shapes=scratch,
        compiler_params=params,
        cost_estimate=cost,
        name="second_operator",
    )(scale, noise, *blocks, *images)
    curvs = gathered(curv)
    return pl.pallas_call(
        last_kernel, out_shape=(field, field), name="last_update"
    )(sol, res, direc, image, norm, *curvs)


def solution(mesh):
    in_specs = (P(None, ("grp", "row")), P(), P(("grp", "row")), P(None, ("grp", "row")))
    out_specs = (P(None, ("grp", "row")), P(None, ("grp", "row")))
    return jax.shard_map(shards, mesh=mesh, in_specs=in_specs, out_specs=out_specs, check_vma=False)
```

```python
import functools
import math

import jax
import jax.numpy as jnp
from jax import lax
from jax.experimental import pallas as pl
from jax.experimental.pallas import tpu as pltpu
from jax.sharding import PartitionSpec as P

LOG2E = math.log2(math.e)
DEPTH = 64
TILE = 256
F32 = jnp.float32
BF16 = jnp.bfloat16


def pieces(value, count):
    parts = []
    for _ in range(count):
        part = value.astype(BF16).astype(F32)
        parts.append(part)
        value = value - part
    return parts


def exponent_rows(points, factor, visiting):
    big, mid, low = pieces(points * factor, 3)
    half_sq = jnp.sum(points * points, axis=0, keepdims=True) * (-0.5 * LOG2E)
    sq_parts = pieces(half_sq, 3)
    row = lax.broadcasted_iota(jnp.int32, points.shape, 0)
    first = 0 if visiting else 3
    tail = jnp.where((row >= 3 - first) & (row < 6 - first), 1.0, 0.0)
    for k, part in enumerate(sq_parts):
        tail = jnp.where(row == first + k, part, tail)
    order = [big, big, big, mid, mid, low] if visiting else [big, mid, low, big, mid, big]
    return jnp.concatenate(order + [tail, jnp.zeros_like(tail)], axis=0)


def stacked(value):
    return jnp.concatenate(pieces(value, 2), axis=0).astype(BF16)


def prepare_points(scale_ref, mine_ref, all_ref, nfeat, rows_ref, own_ref):
    own = exponent_rows(mine_ref[0:nfeat, :] / scale_ref[...], 1.0, False)
    own_ref[...] = own.T.astype(BF16)

    def block(b, carry):
        points = all_ref[b, 0:nfeat, :] / scale_ref[...]
        rows_ref[b] = exponent_rows(points, LOG2E, True).astype(BF16)
        return carry

    lax.fori_loop(0, all_ref.shape[0], block, 0)


def operator_loop(rows_ref, own_ref, dirs_ref, acc_ref):
    count, _, width = rows_ref.shape
    acc_ref[...] = jnp.zeros_like(acc_ref)
    chunks = width // TILE

    def step(t, carry):
        b = t // chunks
        at = pl.ds(pl.multiple_of((t % chunks) * TILE, TILE), TILE)
        own = own_ref[at, :]
        total = acc_ref[at, :]
        for c in range(chunks):
            cols = slice(c * TILE, (c + 1) * TILE)
            expo = jnp.dot(own, rows_ref[b, :, cols], preferred_element_type=F32)
            weight = jnp.exp2(expo)
            high = weight.astype(BF16)
            low = (weight - high.astype(F32)).astype(BF16)
            dirs = dirs_ref[b, :, cols]
            for piece in (high, low):
                total = total + lax.dot_general(
                    piece, dirs, (((1,), (1,)), ((), ())), preferred_element_type=F32
                )
        acc_ref[at, :] = total
        return carry

    lax.fori_loop(0, count * chunks, step, 0)


def collected(acc_ref, nrhs):
    total = acc_ref[...].T
    return total[0:nrhs, :] + total[nrhs:, :]


def first_kernel(
    nfeat, amplitude, scale_ref, noise_ref, mine_ref, all_ref,
    image_ref, rows_ref, own_ref, dirs_ref, acc_ref,
):
    prepare_points(scale_ref, mine_ref, all_ref, nfeat, rows_ref, own_ref)

    def block(b, carry):
        dirs_ref[b] = stacked(all_ref[b, nfeat:, :])
        return carry

    lax.fori_loop(0, all_ref.shape[0], block, 0)
    operator_loop(rows_ref, own_ref, dirs_ref, acc_ref)
    total = collected(acc_ref, image_ref.shape[0])
    image_ref[...] = amplitude * total + noise_ref[...] * mine_ref[nfeat:, :]


def second_kernel(
    nfeat, amplitude, scale_ref, noise_ref, mine_ref, all_ref, image0_ref, images_ref,
    sol_ref, res_ref, dir_ref, image_ref, norm_ref, curv_ref,
    rows_ref, own_ref, dirs_ref, acc_ref,
):
    prepare_points(scale_ref, mine_ref, all_ref, nfeat, rows_ref, own_ref)
    count = all_ref.shape[0]
    nrhs = image_ref.shape[0]
    nothing = jnp.zeros((nrhs, image_ref.shape[1]), F32)

    def sums(b, carry):
        rhs = all_ref[b, nfeat:, :]
        return carry[0] + rhs * rhs, carry[1] + rhs * images_ref[b]

    norm, curv = lax.fori_loop(0, count, sums, (nothing, nothing))
    norm = jnp.sum(norm, axis=1, keepdims=True)
    alpha = norm / jnp.sum(curv, axis=1, keepdims=True)

    def next_sum(b, carry):
        left = all_ref[b, nfeat:, :] - alpha * images_ref[b]
        return carry + left * left

    norm_next = jnp.sum(lax.fori_loop(0, count, next_sum, nothing), axis=1, keepdims=True)
    beta = norm_next / norm

    def block(b, carry):
        rhs = all_ref[b, nfeat:, :]
        dirs_ref[b] = stacked((rhs - alpha * images_ref[b]) + beta * rhs)
        return carry

    lax.fori_loop(0, count, block, 0)
    rhs = mine_ref[nfeat:, :]
    residual = rhs - alpha * image0_ref[...]
    direc = residual + beta * rhs
    sol_ref[...] = alpha * rhs
    res_ref[...] = residual
    dir_ref[...] = direc
    operator_loop(rows_ref, own_ref, dirs_ref, acc_ref)
    image = amplitude * collected(acc_ref, nrhs) + noise_ref[...] * direc
    image_ref[...] = image
    norm_ref[...] = jnp.broadcast_to(norm_next, norm_ref.shape)
    curv_ref[...] = jnp.broadcast_to(
        jnp.sum(direc * image, axis=1, keepdims=True), curv_ref.shape
    )


def last_kernel(sol_ref, res_ref, dir_ref, image_ref, norm_ref, curvs_ref, out_sol, out_res):
    curv = jnp.sum(curvs_ref[...], axis=0)[:, 0:1]
    alpha = norm_ref[:, 0:1] / curv
    out_sol[...] = sol_ref[...] + alpha * dir_ref[...]
    out_res[...] = res_ref[...] - alpha * image_ref[...]


def shards(features, lengthscale, noise, rhs):
    nfeat, width = features.shape
    nrhs = rhs.shape[0]
    count = lax.axis_size("row")
    amplitude = 1.0 / math.sqrt(width * count)
    scale = lengthscale[:, None]
    noise = noise[None, :]
    mine = jnp.concatenate([features, rhs], axis=0)
    everything = lax.all_gather(mine, "row")
    field = jax.ShapeDtypeStruct((nrhs, width), F32)
    small = jax.ShapeDtypeStruct((nrhs, 128), F32)
    scratch = [
        pltpu.VMEM((count, DEPTH, width), BF16),
        pltpu.VMEM((width, DEPTH), BF16),
        pltpu.VMEM((count, 2 * nrhs, width), BF16),
        pltpu.VMEM((width, 2 * nrhs), F32),
    ]
    entries = count * width * width
    params = pltpu.CompilerParams(
        vmem_limit_bytes=min(16 * 1024 * 1024 + 512 * count * width, 60 * 1024 * 1024)
    )
    cost = pl.CostEstimate(
        flops=2 * entries * (DEPTH + 4 * nrhs),
        bytes_accessed=4 * count * (nfeat + nrhs) * width,
        transcendentals=entries,
    )
    image = pl.pallas_call(
        functools.partial(first_kernel, nfeat, amplitude),
        out_shape=field,
        scratch_shapes=scratch,
        compiler_params=params,
        cost_estimate=cost,
        name="first_operator",
    )(scale, noise, mine, everything)
    images = lax.all_gather(image, "row")
    sol, res, direc, image, norm, curv = pl.pallas_call(
        functools.partial(second_kernel, nfeat, amplitude),
        out_shape=(field, field, field, field, small, small),
        scratch_shapes=scratch,
        compiler_params=params,
        cost_estimate=cost,
        name="second_operator",
    )(scale, noise, mine, everything, image, images)
    curvs = lax.all_gather(curv, "row")
    return pl.pallas_call(
        last_kernel, out_shape=(field, field), name="last_update"
    )(sol, res, direc, image, norm, curvs)


def solution(mesh):
    in_specs = (P(None, ("grp", "row")), P(), P(("grp", "row")), P(None, ("grp", "row")))
    out_specs = (P(None, ("grp", "row")), P(None, ("grp", "row")))
    return jax.shard_map(shards, mesh=mesh, in_specs=in_specs, out_specs=out_specs, check_vma=False)
```

```python
import functools
import math

import jax
import jax.numpy as jnp
from jax import lax
from jax.experimental import pallas as pl
from jax.experimental.pallas import tpu as pltpu
from jax.sharding import PartitionSpec as P

LOG2E = math.log2(math.e)
DEPTH = 64
TILE = 256
F32 = jnp.float32
BF16 = jnp.bfloat16


def pieces(value, count):
    parts = []
    for _ in range(count):
        part = value.astype(BF16).astype(F32)
        parts.append(part)
        value = value - part
    return parts


def exponent_rows(points, factor, visiting):
    big, mid, low = pieces(points * factor, 3)
    half_sq = jnp.sum(points * points, axis=0, keepdims=True) * (-0.5 * LOG2E)
    sq_parts = pieces(half_sq, 3)
    row = lax.broadcasted_iota(jnp.int32, points.shape, 0)
    first = 0 if visiting else 3
    tail = jnp.where((row >= 3 - first) & (row < 6 - first), 1.0, 0.0)
    for k, part in enumerate(sq_parts):
        tail = jnp.where(row == first + k, part, tail)
    order = [big, big, big, mid, mid, low] if visiting else [big, mid, low, big, mid, big]
    return jnp.concatenate(order + [tail, jnp.zeros_like(tail)], axis=0)


def stacked(value):
    return jnp.concatenate(pieces(value, 2), axis=0).astype(BF16)


def shifted(value, stride, size, by):
    length = lax.axis_size("row")
    pairs = []
    for i in range(length):
        digit = (i // stride) % size
        pairs.append((i, i + ((digit - by) % size - digit) * stride))
    return lax.ppermute(value, "row", pairs)


def gathered(value):
    length = lax.axis_size("row")
    chips = length // 2
    near = 1
    while near * near * 4 <= chips:
        near *= 2
    far = chips // near
    value = value[None]
    stacks = [value] + [shifted(value, 2 * near, far, by) for by in range(1, far)]
    group = jnp.concatenate(stacks, axis=0)
    groups = [group] + [shifted(group, 2, near, by) for by in range(1, near)]
    return stacks, groups[1:] + [shifted(g, 1, 2, 1) for g in groups]


def prepare_points(scale_ref, blocks, nfeat, yt_ref, own_ref):
    width = own_ref.shape[1]
    own_ref[...] = exponent_rows(blocks[0][0, 0:nfeat, :] / scale_ref[...], 1.0, False).astype(BF16)
    base = 0
    for ref in blocks:

        def block(b, carry, ref=ref, base=base):
            rows = exponent_rows(ref[b, 0:nfeat, :] / scale_ref[...], LOG2E, True)
            yt_ref[base + b] = rows.T.astype(BF16)
            return carry

        lax.fori_loop(0, ref.shape[0], block, 0)
        base += ref.shape[0]


def operator_loop(yt_ref, own_ref, dirs_ref, acc_ref):
    count, _, width = dirs_ref.shape
    chunks = width // TILE
    acc_ref[...] = jnp.zeros_like(acc_ref)

    def step(b, carry):
        for c in range(chunks):
            cols = slice(c * TILE, (c + 1) * TILE)
            expo = jnp.dot(yt_ref[b], own_ref[:, cols], preferred_element_type=F32)
            weight = jnp.exp2(expo)
            high = weight.astype(BF16)
            low = (weight - high.astype(F32)).astype(BF16)
            dirs = dirs_ref[b]
            acc_ref[:, cols] += jnp.dot(
                dirs, high, preferred_element_type=F32
            ) + jnp.dot(dirs, low, preferred_element_type=F32)
        return carry

    lax.fori_loop(0, count, step, 0)


def each(stacks, function, carry):
    base = 0
    for refs in zip(*stacks):

        def block(b, carry, refs=refs, base=base):
            return function(base + b, carry, *[r[b] for r in refs])

        carry = lax.fori_loop(0, refs[0].shape[0], block, carry)
        base += refs[0].shape[0]
    return carry


def total_of(acc_ref, nrhs):
    return acc_ref[0:nrhs, :] + acc_ref[nrhs:, :]


def first_kernel(nfeat, amplitude, scale_ref, noise_ref, *refs):
    *blocks, image_ref, yt_ref, own_ref, dirs_ref, acc_ref = refs
    prepare_points(scale_ref, blocks, nfeat, yt_ref, own_ref)

    def block(b, carry, value):
        dirs_ref[b] = stacked(value[nfeat:, :])
        return carry

    each([blocks], block, 0)
    operator_loop(yt_ref, own_ref, dirs_ref, acc_ref)
    total = total_of(acc_ref, image_ref.shape[0])
    image_ref[...] = amplitude * total + noise_ref[...] * blocks[0][0, nfeat:, :]


def second_kernel(nfeat, amplitude, count, scale_ref, noise_ref, *refs):
    blocks = refs[:count]
    images = refs[count : 2 * count]
    outs = refs[2 * count :]
    sol_ref, res_ref, dir_ref, image_ref, norm_ref, curv_ref = outs[:6]
    yt_ref, own_ref, dirs_ref, acc_ref = outs[6:]
    prepare_points(scale_ref, blocks, nfeat, yt_ref, own_ref)
    nrhs = image_ref.shape[0]
    nothing = jnp.zeros(image_ref.shape, F32)

    def sums(b, carry, value, image):
        rhs = value[nfeat:, :]
        return carry[0] + rhs * rhs, carry[1] + rhs * image

    norm, curv = each([blocks, images], sums, (nothing, nothing))
    norm = jnp.sum(norm, axis=1, keepdims=True)
    alpha = norm / jnp.sum(curv, axis=1, keepdims=True)

    def next_sum(b, carry, value, image):
        left = value[nfeat:, :] - alpha * image
        return carry + left * left

    norm_next = jnp.sum(each([blocks, images], next_sum, nothing), axis=1, keepdims=True)
    beta = norm_next / norm

    def block(b, carry, value, image):
        rhs = value[nfeat:, :]
        dirs_ref[b] = stacked((rhs - alpha * image) + beta * rhs)
        return carry

    each([blocks, images], block, 0)
    rhs = blocks[0][0, nfeat:, :]
    residual = rhs - alpha * images[0][0]
    direc = residual + beta * rhs
    sol_ref[...] = alpha * rhs
    res_ref[...] = residual
    dir_ref[...] = direc
    operator_loop(yt_ref, own_ref, dirs_ref, acc_ref)
    image = amplitude * total_of(acc_ref, nrhs) + noise_ref[...] * direc
    image_ref[...] = image
    norm_ref[...] = jnp.broadcast_to(norm_next, norm_ref.shape)
    curv_ref[...] = jnp.broadcast_to(
        jnp.sum(direc * image, axis=1, keepdims=True), curv_ref.shape
    )


def last_kernel(sol_ref, res_ref, dir_ref, image_ref, norm_ref, *refs):
    *curvs, out_sol, out_res = refs
    curv = sum(jnp.sum(c[...], axis=0) for c in curvs)[:, 0:1]
    alpha = norm_ref[:, 0:1] / curv
    out_sol[...] = sol_ref[...] + alpha * dir_ref[...]
    out_res[...] = res_ref[...] - alpha * image_ref[...]


def shards(features, lengthscale, noise, rhs):
    nfeat, width = features.shape
    nrhs = rhs.shape[0]
    count = lax.axis_size("row")
    amplitude = 1.0 / math.sqrt(width * count)
    scale = lengthscale[:, None]
    noise = noise[None, :]
    mine = jnp.concatenate([features, rhs], axis=0)
    blocks = [x for part in gathered(mine) for x in part]
    field = jax.ShapeDtypeStruct((nrhs, width), F32)
    small = jax.ShapeDtypeStruct((nrhs, 128), F32)
    scratch = [
        pltpu.VMEM((count, width, DEPTH), BF16),
        pltpu.VMEM((DEPTH, width), BF16),
        pltpu.VMEM((count, 2 * nrhs, width), BF16),
        pltpu.VMEM((2 * nrhs, width), F32),
    ]
    entries = count * width * width
    params = pltpu.CompilerParams(
        vmem_limit_bytes=min(16 * 1024 * 1024 + 512 * count * width, 60 * 1024 * 1024)
    )
    cost = pl.CostEstimate(
        flops=2 * entries * (DEPTH + 4 * nrhs),
        bytes_accessed=4 * count * (nfeat + nrhs) * width,
        transcendentals=entries,
    )
    image = pl.pallas_call(
        functools.partial(first_kernel, nfeat, amplitude),
        out_shape=field,
        scratch_shapes=scratch,
        compiler_params=params,
        cost_estimate=cost,
        name="first_operator",
    )(scale, noise, *blocks)
    images = [x for part in gathered(image) for x in part]
    sol, res, direc, image, norm, curv = pl.pallas_call(
        functools.partial(second_kernel, nfeat, amplitude, len(blocks)),
        out_shape=(field, field, field, field, small, small),
        scratch_shapes=scratch,
        compiler_params=params,
        cost_estimate=cost,
        name="second_operator",
    )(scale, noise, *blocks, *images)
    curvs = [x for part in gathered(curv) for x in part]
    return pl.pallas_call(
        last_kernel, out_shape=(field, field), name="last_update"
    )(sol, res, direc, image, norm, *curvs)


def solution(mesh):
    in_specs = (P(None, ("grp", "row")), P(), P(("grp", "row")), P(None, ("grp", "row")))
    out_specs = (P(None, ("grp", "row")), P(None, ("grp", "row")))
    return jax.shard_map(shards, mesh=mesh, in_specs=in_specs, out_specs=out_specs, check_vma=False)
```

```python
import functools
import math

import jax
import jax.numpy as jnp
from jax import lax
from jax.experimental import pallas as pl
from jax.experimental.pallas import tpu as pltpu
from jax.sharding import PartitionSpec as P

LOG2E = math.log2(math.e)
DEPTH = 64
TILE = 256
F32 = jnp.float32
BF16 = jnp.bfloat16


def pieces(value, count):
    parts = []
    for _ in range(count):
        part = value.astype(BF16).astype(F32)
        parts.append(part)
        value = value - part
    return parts


def exponent_rows(points, factor, visiting):
    big, mid, low = pieces(points * factor, 3)
    half_sq = jnp.sum(points * points, axis=0, keepdims=True) * (-0.5 * LOG2E)
    sq_parts = pieces(half_sq, 3)
    row = lax.broadcasted_iota(jnp.int32, points.shape, 0)
    first = 0 if visiting else 3
    tail = jnp.where((row >= 3 - first) & (row < 6 - first), 1.0, 0.0)
    for k, part in enumerate(sq_parts):
        tail = jnp.where(row == first + k, part, tail)
    order = [big, big, big, mid, mid, low] if visiting else [big, mid, low, big, mid, big]
    return jnp.concatenate(order + [tail, jnp.zeros_like(tail)], axis=0)


def stacked(value):
    return jnp.concatenate(pieces(value, 2), axis=0).astype(BF16)


def shifted(value, stride, size, by):
    length = lax.axis_size("row")
    pairs = []
    for i in range(length):
        digit = (i // stride) % size
        pairs.append((i, i + ((digit - by) % size - digit) * stride))
    return lax.ppermute(value, "row", pairs)


def digits():
    chips = lax.axis_size("row") // 2
    near = 1
    while near * near * 4 <= chips:
        near *= 2
    return chips // near, near


def gathered(value):
    far, near = digits()
    own = value[None]
    line = [shifted(own, 2 * near, far, by) for by in range(1, far)]
    group = jnp.concatenate([own] + line, axis=0)
    beside = [shifted(group, 2, near, by) for by in range(1, near)]
    across = [shifted(g, 1, 2, 1) for g in [group] + beside]
    return [own], line, beside + across[:1], across[1:]


def summed(value):
    far, near = digits()
    value = sum([shifted(value, 2 * near, far, by) for by in range(1, far)], value)
    quad = [shifted(value, 1, 2, 1)]
    for by in range(1, near):
        beside = shifted(value, 2, near, by)
        quad += [beside, shifted(beside, 1, 2, 1)]
    return sum(quad, value)


def tables():
    far, near = digits()
    place = lax.axis_index("row")
    core = place % 2
    side = (place // 2 % near) // (near // 2)
    picks = jnp.arange(far // 2, dtype=jnp.int32) * 2
    first, second, last_first, last_second = [], [], [], []
    for k in range(near - 1):
        base = k * far
        shift = k + 1
        if 2 * shift == near:
            first.append(base + picks + side)
            second.append(base + picks + 1 - side)
        else:
            whole = base + jnp.arange(far, dtype=jnp.int32)
            (first if 2 * shift < near else second).append(whole)
    base = (near - 1) * far
    first.append(base + picks + core)
    second.append(base + picks + 1 - core)
    for k in range(near - 1):
        last_first.append(k * far + picks + core)
        last_second.append(k * far + picks + 1 - core)
    return [jnp.concatenate(t) for t in (first, second, last_first, last_second)]


def add_block(yt_ref, at, own_ref, dirs, acc_ref):
    for c in range(own_ref.shape[1] // TILE):
        cols = slice(c * TILE, (c + 1) * TILE)
        expo = jnp.dot(yt_ref[at], own_ref[:, cols], preferred_element_type=F32)
        weight = jnp.exp2(expo)
        high = weight.astype(BF16)
        low = (weight - high.astype(F32)).astype(BF16)
        acc_ref[:, cols] += jnp.dot(
            dirs, high, preferred_element_type=F32
        ) + jnp.dot(dirs, low, preferred_element_type=F32)


def folded(acc_ref):
    nrhs = acc_ref.shape[0] // 2
    return acc_ref[0:nrhs, :] + acc_ref[nrhs:, :]


def each(stacks, function):
    base = 0
    for ref in stacks:

        def block(b, carry, ref=ref, base=base):
            function(base + b, ref[b])
            return carry

        if ref.shape[0] == 1:
            block(0, 0)
        else:
            lax.fori_loop(0, ref.shape[0], block, 0)
        base += ref.shape[0]


def over_points(nfeat, nstacks, first, amplitude, *refs):
    scale_ref, *refs = refs
    own_ref = refs.pop(0) if not first else None
    sofar_ref = refs.pop(0) if not first else None
    noise_ref, mine_ref = (refs.pop(0), refs.pop(0)) if amplitude else (None, None)
    stacks = refs[:nstacks]
    refs = refs[nstacks:]
    if first:
        own_ref = refs.pop(0)
        own_ref[...] = exponent_rows(
            stacks[0][0, 0:nfeat, :] / scale_ref[...], 1.0, False
        ).astype(BF16)
    yt_ref, out_ref, dirs_ref, acc_ref = refs

    def prepare(b, value):
        rows = exponent_rows(value[0:nfeat, :] / scale_ref[...], LOG2E, True)
        yt_ref[b] = rows.T.astype(BF16)
        dirs_ref[b] = stacked(value[nfeat:, :])

    each(stacks, prepare)
    acc_ref[...] = jnp.zeros_like(acc_ref)

    def step(b, carry):
        add_block(yt_ref, b, own_ref, dirs_ref[b], acc_ref)
        return carry

    lax.fori_loop(0, yt_ref.shape[0], step, 0)
    total = folded(acc_ref)
    if not first:
        total = total + sofar_ref[...]
    if amplitude:
        total = amplitude * total + noise_ref[...] * mine_ref[0, nfeat:, :]
    out_ref[...] = total


def over_images(nstacks, table, sofar, form, amplitude, *refs):
    refs = list(refs)
    table_ref = refs.pop(0) if table else None
    sofar_ref = refs.pop(0) if sofar else None
    if form:
        once_ref, noise_ref, mine_ref = refs.pop(0), refs.pop(0), refs.pop(0)
    own_ref, yt_ref, *refs = refs
    stacks = refs[:nstacks]
    out_ref, *refs = refs[nstacks:]
    form_ref = refs.pop(0) if form else None
    dirs_ref, acc_ref = refs

    def prepare(b, value):
        dirs_ref[b] = stacked(value)

    each(stacks, prepare)
    acc_ref[...] = jnp.zeros_like(acc_ref)

    def step(s, carry):
        b = table_ref[s] if table else s
        add_block(yt_ref, b, own_ref, dirs_ref[b], acc_ref)
        return carry

    lax.fori_loop(0, table_ref.shape[0] if table else yt_ref.shape[0], step, 0)
    total = folded(acc_ref)
    if sofar:
        total = total + sofar_ref[...]
    if form:
        mine = mine_ref[0]
        twice = once_ref[...] + 2.0 * total
        inner = mine * (amplitude * twice + noise_ref[...] * mine)
        form_ref[...] = jnp.broadcast_to(
            jnp.sum(inner, axis=1, keepdims=True), form_ref.shape
        )
        total = total + once_ref[...]
    out_ref[...] = total


def scalars_kernel(nfeat, count, *refs):
    blocks = refs[:count]
    images = refs[count : 2 * count]
    out_ref = refs[2 * count]
    nothing = jnp.zeros((images[0].shape[1], images[0].shape[2]), F32)

    def walk(function, carry):
        for b_ref, m_ref in zip(blocks, images):

            def block(k, carry, b_ref=b_ref, m_ref=m_ref):
                return function(carry, b_ref[k, nfeat:, :], m_ref[k])

            carry = lax.fori_loop(0, b_ref.shape[0], block, carry)
        return carry

    def total(value):
        return jnp.sum(value, axis=1, keepdims=True)

    norm, curv, square = walk(
        lambda c, r, w: (c[0] + r * r, c[1] + r * w, c[2] + w * w), (nothing,) * 3
    )
    norm, curv, square = total(norm), total(curv), total(square)
    alpha = norm / curv

    def left(carry, r, w):
        rest = r - alpha * w
        return carry + rest * rest

    norm_next = total(walk(left, nothing))
    gain = 1.0 + norm_next / norm
    part = gain * (gain * curv - 2.0 * alpha * square)
    for k, value in enumerate((alpha, gain, norm_next, part)):
        out_ref[k] = jnp.broadcast_to(value, out_ref.shape[1:])


def last_kernel(
    nfeat, amplitude, scalars_ref, form_ref, total_ref, noise_ref, mine_ref, image_ref,
    sol_ref, res_ref,
):
    alpha, gain, norm_next, part = [scalars_ref[k][:, 0:1] for k in range(4)]
    alpha_next = norm_next / (part + alpha * alpha * form_ref[:, 0:1])
    rhs = mine_ref[0, nfeat:, :]
    image = image_ref[0]
    twice = amplitude * total_ref[...] + noise_ref[...] * image
    sol_ref[...] = alpha * rhs + alpha_next * (gain * rhs - alpha * image)
    res_ref[...] = (rhs - alpha * image) - alpha_next * (gain * image - alpha * twice)


def shards(features, lengthscale, noise, rhs):
    nfeat, width = features.shape
    nrhs = rhs.shape[0]
    amplitude = 1.0 / math.sqrt(width * lax.axis_size("row"))
    scale = lengthscale[:, None]
    noise = noise[None, :]
    field = jax.ShapeDtypeStruct((nrhs, width), F32)
    small = jax.ShapeDtypeStruct((nrhs, 128), F32)
    smem = pl.BlockSpec(memory_space=pltpu.SMEM)
    vmem = pl.BlockSpec(memory_space=pltpu.VMEM)

    def call(kernel, blocks, work, out_shape, operands, name, table=False):
        entries = work * width * width
        return pl.pallas_call(
            kernel,
            out_shape=out_shape,
            in_specs=[smem if table and k == 0 else vmem for k in range(len(operands))],
            scratch_shapes=[
                pltpu.VMEM((blocks, 2 * nrhs, width), BF16),
                pltpu.VMEM((2 * nrhs, width), F32),
            ],
            compiler_params=pltpu.CompilerParams(
                vmem_limit_bytes=min(16 * 1024 * 1024 + blocks * 1024 * width, 60 * 1024 * 1024)
            ),
            cost_estimate=pl.CostEstimate(
                flops=2 * entries * 4 * TILE, bytes_accessed=1024 * width, transcendentals=entries
            ),
            name=name,
        )(*operands)

    def amount(stacks):
        return sum(s.shape[0] for s in stacks)

    def points_shape(stacks):
        return jax.ShapeDtypeStruct((amount(stacks), width, DEPTH), BF16)

    groups = gathered(jnp.concatenate([features, rhs], axis=0))
    mine = groups[0][0]
    own_shape = jax.ShapeDtypeStruct((DEPTH, width), BF16)
    own, points, total = call(
        functools.partial(over_points, nfeat, 1, True, None),
        1, 1, (own_shape, points_shape(groups[0]), field), (scale, mine), "own_block",
    )
    prepared = [points]
    for k, stacks in enumerate(groups[1:]):
        final = k == 2
        points, total = call(
            functools.partial(over_points, nfeat, len(stacks), False, amplitude if final else None),
            amount(stacks), amount(stacks), (points_shape(stacks), field),
            (scale, own, total) + ((noise, mine) if final else ()) + tuple(stacks),
            "blocks_%d" % k,
        )
        prepared.append(points)
    images = gathered(total)
    image = images[0][0]

    def again(group, out, name, sofar=(), table=None, form=()):
        stacks = images[group]
        listed = () if table is None else (table,)
        work = amount(stacks) if table is None else table.shape[0]
        return call(
            functools.partial(
                over_images, len(stacks), table is not None, bool(sofar), bool(form), amplitude
            ),
            amount(stacks), work, out,
            listed + tuple(sofar) + tuple(form) + (own, prepared[group]) + tuple(stacks),
            name, table is not None,
        )

    first, second, last_first, last_second = tables()
    once = again(0, field, "own_again")
    once = again(1, field, "line_again", sofar=(once,))
    half = again(2, field, "beside_half", table=first)
    total, form = again(
        3, (field, small), "across_half", sofar=(half,), table=last_first,
        form=(once, noise, image),
    )
    form = summed(form)
    total = again(2, field, "beside_rest", sofar=(total,), table=second)
    total = again(3, field, "across_rest", sofar=(total,), table=last_second)
    flat = [s for g in groups for s in g]
    flat_images = [s for g in images for s in g]
    scalars = pl.pallas_call(
        functools.partial(scalars_kernel, nfeat, len(flat)),
        out_shape=jax.ShapeDtypeStruct((4, nrhs, 128), F32),
        name="scalars",
    )(*flat, *flat_images)
    return pl.pallas_call(
        functools.partial(last_kernel, nfeat, amplitude),
        out_shape=(field, field),
        name="last_update",
    )(scalars, form, total, noise, mine, image)


def solution(mesh):
    in_specs = (P(None, ("grp", "row")), P(), P(("grp", "row")), P(None, ("grp", "row")))
    out_specs = (P(None, ("grp", "row")), P(None, ("grp", "row")))
    return jax.shard_map(shards, mesh=mesh, in_specs=in_specs, out_specs=out_specs, check_vma=False)
```

```python
import functools
import math

import jax
import jax.numpy as jnp
from jax import lax
from jax.experimental import pallas as pl
from jax.experimental.pallas import tpu as pltpu
from jax.sharding import PartitionSpec as P

LOG2E = math.log2(math.e)
DEPTH = 64
TILE = 256
F32 = jnp.float32
BF16 = jnp.bfloat16
F8 = jnp.float8_e4m3fn
LOW_SCALE = 2.0**16
TOP = 256.0


def pieces(value, count):
    parts = []
    for _ in range(count):
        part = value.astype(BF16).astype(F32)
        parts.append(part)
        value = value - part
    return parts


def exponent_rows(points, factor, visiting):
    big, mid, low = pieces(points * factor, 3)
    half_sq = jnp.sum(points * points, axis=0, keepdims=True) * (-0.5 * LOG2E)
    sq_parts = pieces(half_sq, 3)
    row = lax.broadcasted_iota(jnp.int32, points.shape, 0)
    first = 0 if visiting else 3
    tail = jnp.where((row >= 3 - first) & (row < 6 - first), 1.0, 0.0)
    for k, part in enumerate(sq_parts):
        tail = jnp.where(row == first + k, part, tail)
    order = [big, big, big, mid, mid, low] if visiting else [big, mid, low, big, mid, big]
    return jnp.concatenate(order + [tail, jnp.zeros_like(tail)], axis=0)


def stacked(value):
    return jnp.concatenate(pieces(value, 2), axis=0).astype(BF16)


def small_stacked(value):
    top = jnp.maximum(jnp.max(jnp.abs(value), axis=1, keepdims=True), 1e-30)
    part = value * (TOP / top)
    first = part.astype(F8).astype(F32)
    second = part - first
    pad = jnp.zeros_like(value)
    both = jnp.concatenate([first, second, pad, pad], axis=0).astype(F8)
    return both, jnp.broadcast_to(top * (1.0 / (TOP * LOW_SCALE)), (value.shape[0], 128))


def shifted(value, stride, size, by):
    length = lax.axis_size("row")
    pairs = []
    for i in range(length):
        digit = (i // stride) % size
        pairs.append((i, i + ((digit - by) % size - digit) * stride))
    return lax.ppermute(value, "row", pairs)


def digits():
    chips = lax.axis_size("row") // 2
    near = 1
    while near * near * 4 <= chips:
        near *= 2
    return chips // near, near


def gathered(value):
    far, near = digits()
    own = value[None]
    line = [shifted(own, 2 * near, far, by) for by in range(1, far)]
    group = jnp.concatenate([own] + line, axis=0)
    beside = [shifted(group, 2, near, by) for by in range(1, near)]
    across = [shifted(g, 1, 2, 1) for g in [group] + beside]
    return [own], line, beside + across[:1], across[1:]


def along_line(value):
    far, near = digits()
    return [shifted(value, 2 * near, far, by) for by in range(1, far)]


def over_quad(value):
    _, near = digits()
    length = lax.axis_size("row")
    quad = [shifted(value, 1, 2, 1)]
    for by in range(1, near):
        quad.append(shifted(value, 2, near, by))
        pairs = []
        for i in range(length):
            digit = (i // 2) % near
            pairs.append((i, (i + ((digit - by) % near - digit) * 2) ^ 1))
        quad.append(lax.ppermute(value, "row", pairs))
    return quad


def tables():
    far, near = digits()
    place = lax.axis_index("row")
    core = place % 2
    side = (place // 2 % near) // (near // 2)
    picks = jnp.arange(far // 2, dtype=jnp.int32) * 2
    first, second, last_first, last_second = [], [], [], []
    for k in range(near - 1):
        base = k * far
        shift = k + 1
        if 2 * shift == near:
            first.append(base + picks + side)
            second.append(base + picks + 1 - side)
        else:
            whole = base + jnp.arange(far, dtype=jnp.int32)
            (first if 2 * shift < near else second).append(whole)
    base = (near - 1) * far
    first.append(base + picks + core)
    second.append(base + picks + 1 - core)
    for k in range(near - 1):
        last_first.append(k * far + picks + core)
        last_second.append(k * far + picks + 1 - core)
    return [jnp.concatenate(t) for t in (first, second, last_first, last_second)]


def put_dirs(refs, at, value):
    dirs_ref, small_ref, factor_ref = refs
    dirs_ref[at] = stacked(value)
    small_ref[at], factor_ref[at] = small_stacked(value)


def add_block(yt_ref, at, own_ref, dir_refs, b, acc_ref):
    dirs_ref, small_ref, factor_ref = dir_refs
    nrhs = acc_ref.shape[0]
    factor = factor_ref[b][:, 0:1]
    for c in range(own_ref.shape[1] // TILE):
        cols = slice(c * TILE, (c + 1) * TILE)
        expo = jnp.dot(yt_ref[at], own_ref[:, cols], preferred_element_type=F32)
        weight = jnp.exp2(expo)
        high = weight.astype(BF16)
        low = ((weight - high.astype(F32)) * LOW_SCALE).astype(F8)
        big = jnp.dot(dirs_ref[b], high, preferred_element_type=F32)
        rest = jnp.dot(small_ref[b], low, preferred_element_type=F32)
        acc_ref[:, cols] += (big[:nrhs] + big[nrhs:]) + factor * (
            rest[:nrhs] + rest[nrhs : 2 * nrhs]
        )


def each(stacks, function):
    base = 0
    for ref in stacks:

        def block(b, carry, ref=ref, base=base):
            function(base + b, ref[b])
            return carry

        if ref.shape[0] == 1:
            block(0, 0)
        else:
            lax.fori_loop(0, ref.shape[0], block, 0)
        base += ref.shape[0]


def over_points(nfeat, nstacks, first, amplitude, *refs):
    scale_ref, *refs = refs
    own_ref = refs.pop(0) if not first else None
    sofar_ref = refs.pop(0) if not first else None
    noise_ref, mine_ref = (refs.pop(0), refs.pop(0)) if amplitude else (None, None)
    stacks = refs[:nstacks]
    refs = refs[nstacks:]
    if first:
        own_ref = refs.pop(0)
        own_ref[...] = exponent_rows(
            stacks[0][0, 0:nfeat, :] / scale_ref[...], 1.0, False
        ).astype(BF16)
    yt_ref, out_ref, *dir_refs, acc_ref = refs

    def prepare(b, value):
        rows = exponent_rows(value[0:nfeat, :] / scale_ref[...], LOG2E, True)
        yt_ref[b] = rows.T.astype(BF16)
        put_dirs(dir_refs, b, value[nfeat:, :])

    each(stacks, prepare)
    acc_ref[...] = jnp.zeros_like(acc_ref)

    def step(b, carry):
        add_block(yt_ref, b, own_ref, dir_refs, b, acc_ref)
        return carry

    lax.fori_loop(0, yt_ref.shape[0], step, 0)
    total = acc_ref[...]
    if not first:
        total = total + sofar_ref[...]
    if amplitude:
        total = amplitude * total + noise_ref[...] * mine_ref[0, nfeat:, :]
    out_ref[...] = total


def over_images(nstacks, table, sofar, form, amplitude, *refs):
    refs = list(refs)
    table_ref = refs.pop(0) if table else None
    sofar_ref = refs.pop(0) if sofar else None
    if form:
        once_ref, noise_ref, mine_ref = refs.pop(0), refs.pop(0), refs.pop(0)
    own_ref, yt_ref, *refs = refs
    stacks = refs[:nstacks]
    out_ref, *refs = refs[nstacks:]
    form_ref = refs.pop(0) if form else None
    *dir_refs, acc_ref = refs

    def prepare(b, value):
        put_dirs(dir_refs, b, value)

    each(stacks, prepare)
    acc_ref[...] = jnp.zeros_like(acc_ref)

    def step(s, carry):
        b = table_ref[s] if table else s
        add_block(yt_ref, b, own_ref, dir_refs, b, acc_ref)
        return carry

    lax.fori_loop(0, table_ref.shape[0] if table else yt_ref.shape[0], step, 0)
    total = acc_ref[...]
    if sofar:
        total = total + sofar_ref[...]
    if form:
        mine = mine_ref[0]
        twice = once_ref[...] + 2.0 * total
        inner = mine * (amplitude * twice + noise_ref[...] * mine)
        form_ref[...] = jnp.broadcast_to(
            jnp.sum(inner, axis=1, keepdims=True), form_ref.shape
        )
        total = total + once_ref[...]
    out_ref[...] = total


def scalars_kernel(nfeat, count, *refs):
    blocks = refs[:count]
    images = refs[count : 2 * count]
    out_ref = refs[2 * count]
    nothing = jnp.zeros((images[0].shape[1], images[0].shape[2]), F32)

    def walk(function, carry):
        for b_ref, m_ref in zip(blocks, images):

            def block(k, carry, b_ref=b_ref, m_ref=m_ref):
                return function(carry, b_ref[k, nfeat:, :], m_ref[k])

            carry = lax.fori_loop(0, b_ref.shape[0], block, carry)
        return carry

    def total(value):
        return jnp.sum(value, axis=1, keepdims=True)

    norm, curv, square = walk(
        lambda c, r, w: (c[0] + r * r, c[1] + r * w, c[2] + w * w), (nothing,) * 3
    )
    norm, curv, square = total(norm), total(curv), total(square)
    alpha = norm / curv

    def left(carry, r, w):
        rest = r - alpha * w
        return carry + rest * rest

    norm_next = total(walk(left, nothing))
    gain = 1.0 + norm_next / norm
    part = gain * (gain * curv - 2.0 * alpha * square)
    for k, value in enumerate((alpha, gain, norm_next, part)):
        out_ref[k] = jnp.broadcast_to(value, out_ref.shape[1:])


def last_kernel(
    nfeat, amplitude, scalars_ref, form_ref, total_ref, noise_ref, mine_ref, image_ref,
    sol_ref, res_ref,
):
    alpha, gain, norm_next, part = [scalars_ref[k][:, 0:1] for k in range(4)]
    alpha_next = norm_next / (part + alpha * alpha * form_ref[:, 0:1])
    rhs = mine_ref[0, nfeat:, :]
    image = image_ref[0]
    twice = amplitude * total_ref[...] + noise_ref[...] * image
    sol_ref[...] = alpha * rhs + alpha_next * (gain * rhs - alpha * image)
    res_ref[...] = (rhs - alpha * image) - alpha_next * (gain * image - alpha * twice)


def shards(features, lengthscale, noise, rhs):
    nfeat, width = features.shape
    nrhs = rhs.shape[0]
    amplitude = 1.0 / math.sqrt(width * lax.axis_size("row"))
    scale = lengthscale[:, None]
    noise = noise[None, :]
    field = jax.ShapeDtypeStruct((nrhs, width), F32)
    small = jax.ShapeDtypeStruct((nrhs, 128), F32)
    smem = pl.BlockSpec(memory_space=pltpu.SMEM)
    vmem = pl.BlockSpec(memory_space=pltpu.VMEM)

    def call(kernel, blocks, work, out_shape, operands, name, table=False):
        entries = work * width * width
        return pl.pallas_call(
            kernel,
            out_shape=out_shape,
            in_specs=[smem if table and k == 0 else vmem for k in range(len(operands))],
            scratch_shapes=[
                pltpu.VMEM((blocks, 2 * nrhs, width), BF16),
                pltpu.VMEM((blocks, 4 * nrhs, width), F8),
                pltpu.VMEM((blocks, nrhs, 128), F32),
                pltpu.VMEM((nrhs, width), F32),
            ],
            compiler_params=pltpu.CompilerParams(
                vmem_limit_bytes=min(16 * 1024 * 1024 + blocks * 1024 * width, 60 * 1024 * 1024)
            ),
            cost_estimate=pl.CostEstimate(
                flops=2 * entries * 4 * TILE, bytes_accessed=1024 * width, transcendentals=entries
            ),
            name=name,
        )(*operands)

    def amount(stacks):
        return sum(s.shape[0] for s in stacks)

    def points_shape(stacks):
        return jax.ShapeDtypeStruct((amount(stacks), width, DEPTH), BF16)

    groups = gathered(jnp.concatenate([features, rhs], axis=0))
    mine = groups[0][0]
    own_shape = jax.ShapeDtypeStruct((DEPTH, width), BF16)
    own, points, total = call(
        functools.partial(over_points, nfeat, 1, True, None),
        1, 1, (own_shape, points_shape(groups[0]), field), (scale, mine), "own_block",
    )
    prepared = [points]
    for k, stacks in enumerate(groups[1:]):
        final = k == 2
        points, total = call(
            functools.partial(over_points, nfeat, len(stacks), False, amplitude if final else None),
            amount(stacks), amount(stacks), (points_shape(stacks), field),
            (scale, own, total) + ((noise, mine) if final else ()) + tuple(stacks),
            "blocks_%d" % k,
        )
        prepared.append(points)
    images = gathered(total)
    image = images[0][0]

    def again(group, out, name, sofar=(), table=None, form=()):
        stacks = images[group]
        listed = () if table is None else (table,)
        work = amount(stacks) if table is None else table.shape[0]
        return call(
            functools.partial(
                over_images, len(stacks), table is not None, bool(sofar), bool(form), amplitude
            ),
            amount(stacks), work, out,
            listed + tuple(sofar) + tuple(form) + (own, prepared[group]) + tuple(stacks),
            name, table is not None,
        )

    first, second, last_first, last_second = tables()
    once = again(0, field, "own_again")
    once = again(1, field, "line_again", sofar=(once,))
    half = again(2, field, "beside_half", table=first)
    total, form = again(
        3, (field, small), "across_half", sofar=(half,), table=last_first,
        form=(once, noise, image),
    )
    parts = along_line(form)
    total = again(2, field, "beside_rest", sofar=(total,), table=second)
    *parts, total = lax.optimization_barrier((*parts, total))
    form = sum(parts, form)
    parts = over_quad(form)
    total = again(3, field, "across_rest", sofar=(total,), table=last_second)
    *parts, total = lax.optimization_barrier((*parts, total))
    form = sum(parts, form)
    flat = [s for g in groups for s in g]
    flat_images = [s for g in images for s in g]
    scalars = pl.pallas_call(
        functools.partial(scalars_kernel, nfeat, len(flat)),
        out_shape=jax.ShapeDtypeStruct((4, nrhs, 128), F32),
        name="scalars",
    )(*flat, *flat_images)
    return pl.pallas_call(
        functools.partial(last_kernel, nfeat, amplitude),
        out_shape=(field, field),
        name="last_update",
    )(scalars, form, total, noise, mine, image)


def solution(mesh):
    in_specs = (P(None, ("grp", "row")), P(), P(("grp", "row")), P(None, ("grp", "row")))
    out_specs = (P(None, ("grp", "row")), P(None, ("grp", "row")))
    return jax.shard_map(shards, mesh=mesh, in_specs=in_specs, out_specs=out_specs, check_vma=False)
```

```python
import functools
import math

import jax
import jax.numpy as jnp
from jax import lax
from jax.experimental import pallas as pl
from jax.experimental.pallas import tpu as pltpu
from jax.sharding import PartitionSpec as P

LOG2E = math.log2(math.e)
DEPTH = 64
TILE = 256
STRIP = 128
F32 = jnp.float32
BF16 = jnp.bfloat16


def pieces(value, count):
    parts = []
    for _ in range(count):
        part = value.astype(BF16).astype(F32)
        parts.append(part)
        value = value - part
    return parts


def exponent_rows(points, factor, visiting):
    big, mid, low = pieces(points * factor, 3)
    half_sq = jnp.sum(points * points, axis=0, keepdims=True) * (-0.5 * LOG2E)
    sq_parts = pieces(half_sq, 3)
    row = lax.broadcasted_iota(jnp.int32, points.shape, 0)
    first = 0 if visiting else 3
    tail = jnp.where((row >= 3 - first) & (row < 6 - first), 1.0, 0.0)
    for k, part in enumerate(sq_parts):
        tail = jnp.where(row == first + k, part, tail)
    order = [big, big, big, mid, mid, low] if visiting else [big, mid, low, big, mid, big]
    return jnp.concatenate(order + [tail, jnp.zeros_like(tail)], axis=0)


def put_dirs(dirs_ref, at, value):
    both = jnp.concatenate(pieces(value, 2), axis=0).astype(BF16)
    for k in range(value.shape[1] // STRIP):
        part = both[:, k * STRIP : (k + 1) * STRIP]
        dirs_ref[at, :, 2 * k * STRIP : 2 * (k + 1) * STRIP] = jnp.concatenate(
            [part, part], axis=1
        )


def put_own(own_ref, rows):
    for c in range(own_ref.shape[0]):
        own_ref[c] = rows[:, c * TILE : (c + 1) * TILE].astype(BF16)


def shifted(value, stride, size, by):
    length = lax.axis_size("row")
    pairs = []
    for i in range(length):
        digit = (i // stride) % size
        pairs.append((i, i + ((digit - by) % size - digit) * stride))
    return lax.ppermute(value, "row", pairs)


def digits():
    chips = lax.axis_size("row") // 2
    near = 1
    while near * near * 4 <= chips:
        near *= 2
    return chips // near, near


def gathered(value):
    far, near = digits()
    own = value[None]
    line = [shifted(own, 2 * near, far, by) for by in range(1, far)]
    group = jnp.concatenate([own] + line, axis=0)
    beside = [shifted(group, 2, near, by) for by in range(1, near)]
    across = [shifted(g, 1, 2, 1) for g in [group] + beside]
    return [own], line, beside + across[:1], across[1:]


def along_line(value):
    far, near = digits()
    return [shifted(value, 2 * near, far, by) for by in range(1, far)]


def over_quad(value):
    _, near = digits()
    length = lax.axis_size("row")
    quad = [shifted(value, 1, 2, 1)]
    for by in range(1, near):
        quad.append(shifted(value, 2, near, by))
        pairs = []
        for i in range(length):
            digit = (i // 2) % near
            pairs.append((i, (i + ((digit - by) % near - digit) * 2) ^ 1))
        quad.append(lax.ppermute(value, "row", pairs))
    return quad


def tables():
    far, near = digits()
    place = lax.axis_index("row")
    core = place % 2
    side = (place // 2 % near) // (near // 2)
    picks = jnp.arange(far // 2, dtype=jnp.int32) * 2
    first, second, last_first, last_second = [], [], [], []
    for k in range(near - 1):
        base = k * far
        shift = k + 1
        if 2 * shift == near:
            first.append(base + picks + side)
            second.append(base + picks + 1 - side)
        else:
            whole = base + jnp.arange(far, dtype=jnp.int32)
            (first if 2 * shift < near else second).append(whole)
    base = (near - 1) * far
    first.append(base + picks + core)
    second.append(base + picks + 1 - core)
    for k in range(near - 1):
        last_first.append(k * far + picks + core)
        last_second.append(k * far + picks + 1 - core)
    return [jnp.concatenate(t) for t in (first, second, last_first, last_second)]


def add_blocks(yt_ref, own_ref, dirs_ref, acc_ref, count, block):
    acc_ref[...] = jnp.zeros_like(acc_ref)
    chunks = own_ref.shape[0]

    def step(t, carry):
        c = t % chunks
        b = block(t // chunks)
        own = own_ref[c]
        total = acc_ref[c]
        for k in range(yt_ref.shape[1] // STRIP):
            rows = slice(k * STRIP, (k + 1) * STRIP)
            expo = jnp.dot(yt_ref[b, rows, :], own, preferred_element_type=F32)
            weight = jnp.exp2(expo)
            high = weight.astype(BF16)
            low = (weight - high.astype(F32)).astype(BF16)
            total = total + jnp.dot(
                dirs_ref[b, :, 2 * k * STRIP : 2 * (k + 1) * STRIP],
                jnp.concatenate([high, low], axis=0),
                preferred_element_type=F32,
            )
        acc_ref[c] = total
        return carry

    lax.fori_loop(0, count * chunks, step, 0)


def folded(acc_ref):
    nrhs = acc_ref.shape[1] // 2
    return jnp.concatenate(
        [acc_ref[c, 0:nrhs, :] + acc_ref[c, nrhs:, :] for c in range(acc_ref.shape[0])], axis=1
    )


def each(stacks, function):
    base = 0
    for ref in stacks:

        def block(b, carry, ref=ref, base=base):
            function(base + b, ref[b])
            return carry

        if ref.shape[0] == 1:
            block(0, 0)
        else:
            lax.fori_loop(0, ref.shape[0], block, 0)
        base += ref.shape[0]


def over_points(nfeat, nstacks, first, amplitude, *refs):
    scale_ref, *refs = refs
    own_ref = refs.pop(0) if not first else None
    sofar_ref = refs.pop(0) if not first else None
    noise_ref, mine_ref = (refs.pop(0), refs.pop(0)) if amplitude else (None, None)
    stacks = refs[:nstacks]
    refs = refs[nstacks:]
    if first:
        own_ref = refs.pop(0)
        points = stacks[0][0, 0:nfeat, :] / scale_ref[...]
        put_own(own_ref, exponent_rows(points, 1.0, False))
    yt_ref, out_ref, dirs_ref, acc_ref = refs

    def prepare(b, value):
        rows = exponent_rows(value[0:nfeat, :] / scale_ref[...], LOG2E, True)
        yt_ref[b] = rows.T.astype(BF16)
        put_dirs(dirs_ref, b, value[nfeat:, :])

    each(stacks, prepare)
    add_blocks(yt_ref, own_ref, dirs_ref, acc_ref, yt_ref.shape[0], lambda b: b)
    total = folded(acc_ref)
    if not first:
        total = total + sofar_ref[...]
    if amplitude:
        total = amplitude * total + noise_ref[...] * mine_ref[0, nfeat:, :]
    out_ref[...] = total


def over_images(nstacks, table, sofar, form, amplitude, *refs):
    refs = list(refs)
    table_ref = refs.pop(0) if table else None
    sofar_ref = refs.pop(0) if sofar else None
    if form:
        once_ref, noise_ref, mine_ref = refs.pop(0), refs.pop(0), refs.pop(0)
    own_ref, yt_ref, *refs = refs
    stacks = refs[:nstacks]
    out_ref, *refs = refs[nstacks:]
    form_ref = refs.pop(0) if form else None
    dirs_ref, acc_ref = refs

    def prepare(b, value):
        put_dirs(dirs_ref, b, value)

    each(stacks, prepare)
    add_blocks(
        yt_ref, own_ref, dirs_ref, acc_ref,
        table_ref.shape[0] if table else yt_ref.shape[0],
        lambda s: table_ref[s] if table else s,
    )
    total = folded(acc_ref)
    if sofar:
        total = total + sofar_ref[...]
    if form:
        mine = mine_ref[0]
        twice = once_ref[...] + 2.0 * total
        inner = mine * (amplitude * twice + noise_ref[...] * mine)
        form_ref[...] = jnp.broadcast_to(
            jnp.sum(inner, axis=1, keepdims=True), form_ref.shape
        )
        total = total + once_ref[...]
    out_ref[...] = total


def scalars_kernel(nfeat, count, *refs):
    blocks = refs[:count]
    images = refs[count : 2 * count]
    out_ref = refs[2 * count]
    nothing = jnp.zeros((images[0].shape[1], images[0].shape[2]), F32)

    def walk(function, carry):
        for b_ref, m_ref in zip(blocks, images):

            def block(k, carry, b_ref=b_ref, m_ref=m_ref):
                return function(carry, b_ref[k, nfeat:, :], m_ref[k])

            carry = lax.fori_loop(0, b_ref.shape[0], block, carry)
        return carry

    def total(value):
        return jnp.sum(value, axis=1, keepdims=True)

    norm, curv, square = walk(
        lambda c, r, w: (c[0] + r * r, c[1] + r * w, c[2] + w * w), (nothing,) * 3
    )
    norm, curv, square = total(norm), total(curv), total(square)
    alpha = norm / curv

    def left(carry, r, w):
        rest = r - alpha * w
        return carry + rest * rest

    norm_next = total(walk(left, nothing))
    gain = 1.0 + norm_next / norm
    part = gain * (gain * curv - 2.0 * alpha * square)
    for k, value in enumerate((alpha, gain, norm_next, part)):
        out_ref[k] = jnp.broadcast_to(value, out_ref.shape[1:])


def last_kernel(
    nfeat, amplitude, scalars_ref, form_ref, total_ref, noise_ref, mine_ref, image_ref,
    sol_ref, res_ref,
):
    alpha, gain, norm_next, part = [scalars_ref[k][:, 0:1] for k in range(4)]
    alpha_next = norm_next / (part + alpha * alpha * form_ref[:, 0:1])
    rhs = mine_ref[0, nfeat:, :]
    image = image_ref[0]
    twice = amplitude * total_ref[...] + noise_ref[...] * image
    sol_ref[...] = alpha * rhs + alpha_next * (gain * rhs - alpha * image)
    res_ref[...] = (rhs - alpha * image) - alpha_next * (gain * image - alpha * twice)


def shards(features, lengthscale, noise, rhs):
    nfeat, width = features.shape
    nrhs = rhs.shape[0]
    amplitude = 1.0 / math.sqrt(width * lax.axis_size("row"))
    scale = lengthscale[:, None]
    noise = noise[None, :]
    field = jax.ShapeDtypeStruct((nrhs, width), F32)
    small = jax.ShapeDtypeStruct((nrhs, 128), F32)
    smem = pl.BlockSpec(memory_space=pltpu.SMEM)
    vmem = pl.BlockSpec(memory_space=pltpu.VMEM)

    def call(kernel, blocks, work, out_shape, operands, name, table=False):
        entries = work * width * width
        return pl.pallas_call(
            kernel,
            out_shape=out_shape,
            in_specs=[smem if table and k == 0 else vmem for k in range(len(operands))],
            scratch_shapes=[
                pltpu.VMEM((blocks, 2 * nrhs, 2 * width), BF16),
                pltpu.VMEM((width // TILE, 2 * nrhs, TILE), F32),
            ],
            compiler_params=pltpu.CompilerParams(
                vmem_limit_bytes=min(16 * 1024 * 1024 + blocks * 1024 * width, 60 * 1024 * 1024)
            ),
            cost_estimate=pl.CostEstimate(
                flops=2 * entries * 4 * TILE, bytes_accessed=1024 * width, transcendentals=entries
            ),
            name=name,
        )(*operands)

    def amount(stacks):
        return sum(s.shape[0] for s in stacks)

    def points_shape(stacks):
        return jax.ShapeDtypeStruct((amount(stacks), width, DEPTH), BF16)

    groups = gathered(jnp.concatenate([features, rhs], axis=0))
    mine = groups[0][0]
    own_shape = jax.ShapeDtypeStruct((width // TILE, DEPTH, TILE), BF16)
    own, points, total = call(
        functools.partial(over_points, nfeat, 1, True, None),
        1, 1, (own_shape, points_shape(groups[0]), field), (scale, mine), "own_block",
    )
    prepared = [points]
    for k, stacks in enumerate(groups[1:]):
        final = k == 2
        points, total = call(
            functools.partial(over_points, nfeat, len(stacks), False, amplitude if final else None),
            amount(stacks), amount(stacks), (points_shape(stacks), field),
            (scale, own, total) + ((noise, mine) if final else ()) + tuple(stacks),
            "blocks_%d" % k,
        )
        prepared.append(points)
    images = gathered(total)
    image = images[0][0]

    def again(group, out, name, sofar=(), table=None, form=()):
        stacks = images[group]
        listed = () if table is None else (table,)
        work = amount(stacks) if table is None else table.shape[0]
        return call(
            functools.partial(
                over_images, len(stacks), table is not None, bool(sofar), bool(form), amplitude
            ),
            amount(stacks), work, out,
            listed + tuple(sofar) + tuple(form) + (own, prepared[group]) + tuple(stacks),
            name, table is not None,
        )

    first, second, last_first, last_second = tables()
    once = again(0, field, "own_again")
    once = again(1, field, "line_again", sofar=(once,))
    half = again(2, field, "beside_half", table=first)
    total, form = again(
        3, (field, small), "across_half", sofar=(half,), table=last_first,
        form=(once, noise, image),
    )
    parts = along_line(form)
    total = again(2, field, "beside_rest", sofar=(total,), table=second)
    *parts, total = lax.optimization_barrier((*parts, total))
    form = sum(parts, form)
    parts = over_quad(form)
    total = again(3, field, "across_rest", sofar=(total,), table=last_second)
    *parts, total = lax.optimization_barrier((*parts, total))
    form = sum(parts, form)
    flat = [s for g in groups for s in g]
    flat_images = [s for g in images for s in g]
    scalars = pl.pallas_call(
        functools.partial(scalars_kernel, nfeat, len(flat)),
        out_shape=jax.ShapeDtypeStruct((4, nrhs, 128), F32),
        name="scalars",
    )(*flat, *flat_images)
    return pl.pallas_call(
        functools.partial(last_kernel, nfeat, amplitude),
        out_shape=(field, field),
        name="last_update",
    )(scalars, form, total, noise, mine, image)


def solution(mesh):
    in_specs = (P(None, ("grp", "row")), P(), P(("grp", "row")), P(None, ("grp", "row")))
    out_specs = (P(None, ("grp", "row")), P(None, ("grp", "row")))
    return jax.shard_map(shards, mesh=mesh, in_specs=in_specs, out_specs=out_specs, check_vma=False)
```

```python
import functools
import math

import jax
import jax.numpy as jnp
from jax import lax
from jax.experimental import pallas as pl
from jax.experimental.pallas import tpu as pltpu
from jax.sharding import PartitionSpec as P

LOG2E = math.log2(math.e)
DEPTH = 64
TILE = 256
MIB = 1024 * 1024
KEPT_ORDER = (0, 1, 3, 2)
F32 = jnp.float32
BF16 = jnp.bfloat16


def pieces(value, count):
    parts = []
    for _ in range(count):
        part = value.astype(BF16).astype(F32)
        parts.append(part)
        value = value - part
    return parts


def exponent_rows(points, factor, visiting):
    big, mid, low = pieces(points * factor, 3)
    half_sq = jnp.sum(points * points, axis=0, keepdims=True) * (-0.5 * LOG2E)
    sq_parts = pieces(half_sq, 3)
    row = lax.broadcasted_iota(jnp.int32, points.shape, 0)
    first = 0 if visiting else 3
    tail = jnp.where((row >= 3 - first) & (row < 6 - first), 1.0, 0.0)
    for k, part in enumerate(sq_parts):
        tail = jnp.where(row == first + k, part, tail)
    order = [big, big, big, mid, mid, low] if visiting else [big, mid, low, big, mid, big]
    return jnp.concatenate(order + [tail, jnp.zeros_like(tail)], axis=0)


def put_dirs(dirs_ref, at, value):
    both = jnp.concatenate(pieces(value, 2), axis=0).astype(BF16)
    dirs_ref[at] = jnp.concatenate([both, both], axis=1)


def shifted(value, stride, size, by):
    length = lax.axis_size("row")
    pairs = []
    for i in range(length):
        digit = (i // stride) % size
        pairs.append((i, i + ((digit - by) % size - digit) * stride))
    return lax.ppermute(value, "row", pairs)


def digits():
    chips = lax.axis_size("row") // 2
    near = 1
    while near * near * 4 <= chips:
        near *= 2
    return chips // near, near


def gathered(value):
    far, near = digits()
    own = value[None]
    line = [shifted(own, 2 * near, far, by) for by in range(1, far)]
    group = jnp.concatenate([own] + line, axis=0)
    beside = [shifted(group, 2, near, by) for by in range(1, near)]
    across = [shifted(g, 1, 2, 1) for g in [group] + beside]
    return [own], line, beside + across[:1], across[1:]


def along_line(value):
    far, near = digits()
    return [shifted(value, 2 * near, far, by) for by in range(1, far)]


def over_quad(value):
    _, near = digits()
    length = lax.axis_size("row")
    quad = [shifted(value, 1, 2, 1)]
    for by in range(1, near):
        quad.append(shifted(value, 2, near, by))
        pairs = []
        for i in range(length):
            digit = (i // 2) % near
            pairs.append((i, (i + ((digit - by) % near - digit) * 2) ^ 1))
        quad.append(lax.ppermute(value, "row", pairs))
    return quad


def tables():
    far, near = digits()
    place = lax.axis_index("row")
    core = place % 2
    side = (place // 2 % near) // (near // 2)
    picks = jnp.arange(far // 2, dtype=jnp.int32) * 2
    first, second, last_first, last_second = [], [], [], []
    for k in range(near - 1):
        base = k * far
        shift = k + 1
        if 2 * shift == near:
            first.append(base + picks + side)
            second.append(base + picks + 1 - side)
        else:
            whole = base + jnp.arange(far, dtype=jnp.int32)
            (first if 2 * shift < near else second).append(whole)
    base = (near - 1) * far
    first.append(base + picks + core)
    second.append(base + picks + 1 - core)
    for k in range(near - 1):
        last_first.append(k * far + picks + core)
        last_second.append(k * far + picks + 1 - core)
    return [jnp.concatenate(t) for t in (first, second, last_first, last_second)]


def add_block(yt_ref, at, own_ref, dirs_ref, acc_ref, keep_ref):
    width = own_ref.shape[1]
    for c in range(width // TILE):
        cols = slice(c * TILE, (c + 1) * TILE)
        expo = jnp.dot(yt_ref[at], own_ref[:, cols], preferred_element_type=F32)
        weight = jnp.exp2(expo)
        high = weight.astype(BF16)
        low = (weight - high.astype(F32)).astype(BF16)
        if keep_ref is not None:
            keep_ref[at, c, 0:width, :] = high
            keep_ref[at, c, width:, :] = low
        acc_ref[:, cols] += jnp.dot(
            dirs_ref[at, :, 0:width], high, preferred_element_type=F32
        ) + jnp.dot(dirs_ref[at, :, 0:width], low, preferred_element_type=F32)


def add_kept_block(keep_ref, at, dirs_ref, acc_ref):
    for c in range(keep_ref.shape[1]):
        acc_ref[:, c * TILE : (c + 1) * TILE] += jnp.dot(
            dirs_ref[at], keep_ref[at, c], preferred_element_type=F32
        )


def folded(acc_ref):
    nrhs = acc_ref.shape[0] // 2
    return acc_ref[0:nrhs, :] + acc_ref[nrhs:, :]


def each(stacks, function):
    base = 0
    for ref in stacks:

        def block(b, carry, ref=ref, base=base):
            function(base + b, ref[b])
            return carry

        if ref.shape[0] == 1:
            block(0, 0)
        else:
            lax.fori_loop(0, ref.shape[0], block, 0)
        base += ref.shape[0]


def over_points(nfeat, nstacks, first, amplitude, kept, *refs):
    scale_ref, *refs = refs
    own_ref = refs.pop(0) if not first else None
    sofar_ref = refs.pop(0) if not first else None
    noise_ref, mine_ref = (refs.pop(0), refs.pop(0)) if amplitude else (None, None)
    stacks = refs[:nstacks]
    refs = refs[nstacks:]
    if first:
        own_ref = refs.pop(0)
        own_ref[...] = exponent_rows(
            stacks[0][0, 0:nfeat, :] / scale_ref[...], 1.0, False
        ).astype(BF16)
    out_ref, yt_ref, dirs_ref, acc_ref = refs[:1] + refs[-3:]
    keep_ref = refs[1] if kept else None

    def prepare(b, value):
        rows = exponent_rows(value[0:nfeat, :] / scale_ref[...], LOG2E, True)
        yt_ref[b] = rows.T.astype(BF16)
        put_dirs(dirs_ref, b, value[nfeat:, :])

    each(stacks, prepare)
    acc_ref[...] = jnp.zeros_like(acc_ref)

    def step(b, carry):
        add_block(yt_ref, b, own_ref, dirs_ref, acc_ref, keep_ref)
        return carry

    lax.fori_loop(0, yt_ref.shape[0], step, 0)
    total = folded(acc_ref)
    if not first:
        total = total + sofar_ref[...]
    if amplitude:
        total = amplitude * total + noise_ref[...] * mine_ref[0, nfeat:, :]
    out_ref[...] = total


def over_images(nstacks, table, sofar, form, amplitude, kept, *refs):
    refs = list(refs)
    table_ref = refs.pop(0) if table else None
    sofar_ref = refs.pop(0) if sofar else None
    if form:
        once_ref, noise_ref, mine_ref = refs.pop(0), refs.pop(0), refs.pop(0)
    own_ref = None if kept else refs.pop(0)
    source_ref, *refs = refs
    stacks = refs[:nstacks]
    out_ref, *refs = refs[nstacks:]
    form_ref = refs.pop(0) if form else None
    dirs_ref, acc_ref = refs

    def prepare(b, value):
        put_dirs(dirs_ref, b, value)

    each(stacks, prepare)
    acc_ref[...] = jnp.zeros_like(acc_ref)

    def step(s, carry):
        b = table_ref[s] if table else s
        if kept:
            add_kept_block(source_ref, b, dirs_ref, acc_ref)
        else:
            add_block(source_ref, b, own_ref, dirs_ref, acc_ref, None)
        return carry

    lax.fori_loop(0, table_ref.shape[0] if table else source_ref.shape[0], step, 0)
    total = folded(acc_ref)
    if sofar:
        total = total + sofar_ref[...]
    if form:
        mine = mine_ref[0]
        twice = once_ref[...] + 2.0 * total
        inner = mine * (amplitude * twice + noise_ref[...] * mine)
        form_ref[...] = jnp.broadcast_to(
            jnp.sum(inner, axis=1, keepdims=True), form_ref.shape
        )
        total = total + once_ref[...]
    out_ref[...] = total


def scalars_kernel(nfeat, count, *refs):
    blocks = refs[:count]
    images = refs[count : 2 * count]
    out_ref = refs[2 * count]
    nothing = jnp.zeros((images[0].shape[1], images[0].shape[2]), F32)

    def walk(function, carry):
        for b_ref, m_ref in zip(blocks, images):

            def block(k, carry, b_ref=b_ref, m_ref=m_ref):
                return function(carry, b_ref[k, nfeat:, :], m_ref[k])

            carry = lax.fori_loop(0, b_ref.shape[0], block, carry)
        return carry

    def total(value):
        return jnp.sum(value, axis=1, keepdims=True)

    norm, curv, square = walk(
        lambda c, r, w: (c[0] + r * r, c[1] + r * w, c[2] + w * w), (nothing,) * 3
    )
    norm, curv, square = total(norm), total(curv), total(square)
    alpha = norm / curv

    def left(carry, r, w):
        rest = r - alpha * w
        return carry + rest * rest

    norm_next = total(walk(left, nothing))
    gain = 1.0 + norm_next / norm
    part = gain * (gain * curv - 2.0 * alpha * square)
    for k, value in enumerate((alpha, gain, norm_next, part)):
        out_ref[k] = jnp.broadcast_to(value, out_ref.shape[1:])


def last_kernel(
    nfeat, amplitude, scalars_ref, form_ref, total_ref, noise_ref, mine_ref, image_ref,
    sol_ref, res_ref,
):
    alpha, gain, norm_next, part = [scalars_ref[k][:, 0:1] for k in range(4)]
    alpha_next = norm_next / (part + alpha * alpha * form_ref[:, 0:1])
    rhs = mine_ref[0, nfeat:, :]
    image = image_ref[0]
    twice = amplitude * total_ref[...] + noise_ref[...] * image
    sol_ref[...] = alpha * rhs + alpha_next * (gain * rhs - alpha * image)
    res_ref[...] = (rhs - alpha * image) - alpha_next * (gain * image - alpha * twice)


def shards(features, lengthscale, noise, rhs):
    nfeat, width = features.shape
    nrhs = rhs.shape[0]
    amplitude = 1.0 / math.sqrt(width * lax.axis_size("row"))
    scale = lengthscale[:, None]
    noise = noise[None, :]
    field = jax.ShapeDtypeStruct((nrhs, width), F32)
    small = jax.ShapeDtypeStruct((nrhs, 128), F32)
    smem = pl.BlockSpec(memory_space=pltpu.SMEM)
    vmem = pl.BlockSpec(memory_space=pltpu.VMEM)

    def call(kernel, blocks, work, out_shape, operands, name, table=False, kept=0, fresh=0):
        entries = work * width * width
        scratch = [
            pltpu.VMEM((blocks, 2 * nrhs, 2 * width), BF16),
            pltpu.VMEM((2 * nrhs, width), F32),
        ]
        if fresh:
            scratch.insert(0, pltpu.VMEM((fresh, width, DEPTH), BF16))
        limit = 8 * MIB + blocks * 768 * width + 4 * kept * width * width
        return pl.pallas_call(
            kernel,
            out_shape=out_shape,
            in_specs=[smem if table and k == 0 else vmem for k in range(len(operands))],
            scratch_shapes=scratch,
            compiler_params=pltpu.CompilerParams(vmem_limit_bytes=min(limit, 60 * MIB)),
            cost_estimate=pl.CostEstimate(
                flops=2 * entries * 4 * TILE, bytes_accessed=1024 * width, transcendentals=entries
            ),
            name=name,
        )(*operands)

    def amount(stacks):
        return sum(s.shape[0] for s in stacks)

    groups = gathered(jnp.concatenate([features, rhs], axis=0))
    mine = groups[0][0]
    own_shape = jax.ShapeDtypeStruct((DEPTH, width), BF16)
    room = 40 * MIB - lax.axis_size("row") * 512 * width
    keep = [False] * len(groups)
    for k in KEPT_ORDER:
        size = 4 * amount(groups[k]) * width * width
        keep[k] = size <= room
        room -= size if keep[k] else 0
    own, total, prepared = None, None, []
    for k, stacks in enumerate(groups):
        blocks = amount(stacks)
        final = k == len(groups) - 1
        if keep[k]:
            source = jax.ShapeDtypeStruct((blocks, width // TILE, 2 * width, TILE), BF16)
        else:
            source = jax.ShapeDtypeStruct((blocks, width, DEPTH), BF16)
        out = (own_shape,) * (k == 0) + (field, source)
        *made, total, source = call(
            functools.partial(
                over_points, nfeat, len(stacks), k == 0, amplitude if final else None, keep[k]
            ),
            blocks, blocks, out,
            (scale,) + (() if k == 0 else (own, total)) + ((noise, mine) if final else ())
            + tuple(stacks),
            "blocks_%d" % k, kept=blocks * keep[k], fresh=blocks * keep[k],
        )
        own = made[0] if made else own
        prepared.append(source)
    images = gathered(total)
    image = images[0][0]

    def again(group, out, name, sofar=(), table=None, form=()):
        stacks = images[group]
        listed = () if table is None else (table,)
        work = amount(stacks) if table is None else table.shape[0]
        return call(
            functools.partial(
                over_images, len(stacks), table is not None, bool(sofar), bool(form), amplitude,
                keep[group],
            ),
            amount(stacks), work, out,
            listed + tuple(sofar) + tuple(form) + (() if keep[group] else (own,))
            + (prepared[group],) + tuple(stacks),
            name, table is not None, kept=amount(stacks) * keep[group],
        )

    first, second, last_first, last_second = tables()
    once = again(0, field, "own_again")
    once = again(1, field, "line_again", sofar=(once,))
    half = again(2, field, "beside_half", table=first)
    total, form = again(
        3, (field, small), "across_half", sofar=(half,), table=last_first,
        form=(once, noise, image),
    )
    parts = along_line(form)
    total = again(2, field, "beside_rest", sofar=(total,), table=second)
    *parts, total = lax.optimization_barrier((*parts, total))
    form = sum(parts, form)
    parts = over_quad(form)
    total = again(3, field, "across_rest", sofar=(total,), table=last_second)
    *parts, total = lax.optimization_barrier((*parts, total))
    form = sum(parts, form)
    flat = [s for g in groups for s in g]
    flat_images = [s for g in images for s in g]
    scalars = pl.pallas_call(
        functools.partial(scalars_kernel, nfeat, len(flat)),
        out_shape=jax.ShapeDtypeStruct((4, nrhs, 128), F32),
        name="scalars",
    )(*flat, *flat_images)
    return pl.pallas_call(
        functools.partial(last_kernel, nfeat, amplitude),
        out_shape=(field, field),
        name="last_update",
    )(scalars, form, total, noise, mine, image)


def solution(mesh):
    in_specs = (P(None, ("grp", "row")), P(), P(("grp", "row")), P(None, ("grp", "row")))
    out_specs = (P(None, ("grp", "row")), P(None, ("grp", "row")))
    return jax.shard_map(shards, mesh=mesh, in_specs=in_specs, out_specs=out_specs, check_vma=False)
```

```python
import functools
import math

import jax
import jax.numpy as jnp
from jax import lax
from jax.experimental import pallas as pl
from jax.experimental.pallas import tpu as pltpu
from jax.sharding import PartitionSpec as P

LOG2E = math.log2(math.e)
DEPTH = 64
TILE = 256
MIB = 1024 * 1024
KEPT_ORDER = (0, 1, 3, 2)
F32 = jnp.float32
BF16 = jnp.bfloat16


def pieces(value, count):
    parts = []
    for _ in range(count):
        part = value.astype(BF16).astype(F32)
        parts.append(part)
        value = value - part
    return parts


def exponent_rows(points, factor, visiting):
    big, mid, low = pieces(points * factor, 3)
    half_sq = jnp.sum(points * points, axis=0, keepdims=True) * (-0.5 * LOG2E)
    sq_parts = pieces(half_sq, 3)
    row = lax.broadcasted_iota(jnp.int32, points.shape, 0)
    first = 0 if visiting else 3
    tail = jnp.where((row >= 3 - first) & (row < 6 - first), 1.0, 0.0)
    for k, part in enumerate(sq_parts):
        tail = jnp.where(row == first + k, part, tail)
    order = [big, big, big, mid, mid, low] if visiting else [big, mid, low, big, mid, big]
    return jnp.concatenate(order + [tail, jnp.zeros_like(tail)], axis=0)


def put_dirs(dirs_ref, at, value):
    both = jnp.concatenate(pieces(value, 2), axis=0).astype(BF16)
    dirs_ref[at] = jnp.concatenate([both, both], axis=1)


def shifted(value, stride, size, by):
    length = lax.axis_size("row")
    pairs = []
    for i in range(length):
        digit = (i // stride) % size
        pairs.append((i, i + ((digit - by) % size - digit) * stride))
    return lax.ppermute(value, "row", pairs)


def digits():
    chips = lax.axis_size("row") // 2
    near = 1
    while near * near * 4 <= chips:
        near *= 2
    return chips // near, near


def gathered(value):
    far, near = digits()
    own = value[None]
    line = [shifted(own, 2 * near, far, by) for by in range(1, far)]
    group = jnp.concatenate([own] + line, axis=0)
    beside = [shifted(group, 2, near, by) for by in range(1, near)]
    across = [shifted(g, 1, 2, 1) for g in [group] + beside]
    return [own], line, beside + across[:1], across[1:]


def along_line(value):
    far, near = digits()
    return [shifted(value, 2 * near, far, by) for by in range(1, far)]


def over_quad(value):
    _, near = digits()
    length = lax.axis_size("row")
    quad = [shifted(value, 1, 2, 1)]
    for by in range(1, near):
        quad.append(shifted(value, 2, near, by))
        pairs = []
        for i in range(length):
            digit = (i // 2) % near
            pairs.append((i, (i + ((digit - by) % near - digit) * 2) ^ 1))
        quad.append(lax.ppermute(value, "row", pairs))
    return quad


def tables():
    far, near = digits()
    place = lax.axis_index("row")
    core = place % 2
    side = (place // 2 % near) // (near // 2)
    picks = jnp.arange(far // 2, dtype=jnp.int32) * 2
    first, second, last_first, last_second = [], [], [], []
    for k in range(near - 1):
        base = k * far
        shift = k + 1
        if 2 * shift == near:
            first.append(base + picks + side)
            second.append(base + picks + 1 - side)
        else:
            whole = base + jnp.arange(far, dtype=jnp.int32)
            (first if 2 * shift < near else second).append(whole)
    base = (near - 1) * far
    first.append(base + picks + core)
    second.append(base + picks + 1 - core)
    for k in range(near - 1):
        last_first.append(k * far + picks + core)
        last_second.append(k * far + picks + 1 - core)
    return [jnp.concatenate(t) for t in (first, second, last_first, last_second)]


def add_block(yt_ref, at, own_ref, dirs_ref, acc_ref, keep_ref):
    width = own_ref.shape[1]
    for c in range(width // TILE):
        cols = slice(c * TILE, (c + 1) * TILE)
        expo = jnp.dot(yt_ref[at], own_ref[:, cols], preferred_element_type=F32)
        weight = jnp.exp2(expo)
        high = weight.astype(BF16)
        low = (weight - high.astype(F32)).astype(BF16)
        if keep_ref is not None:
            keep_ref[at, c, 0:width, :] = high
            keep_ref[at, c, width:, :] = low
        acc_ref[:, cols] += jnp.dot(
            dirs_ref[at, :, 0:width], high, preferred_element_type=F32
        ) + jnp.dot(dirs_ref[at, :, 0:width], low, preferred_element_type=F32)


def add_kept_block(keep_ref, at, dirs_ref, acc_ref):
    for c in range(keep_ref.shape[1]):
        acc_ref[:, c * TILE : (c + 1) * TILE] += jnp.dot(
            dirs_ref[at], keep_ref[at, c], preferred_element_type=F32
        )


def folded(acc_ref):
    nrhs = acc_ref.shape[0] // 2
    return acc_ref[0:nrhs, :] + acc_ref[nrhs:, :]


def each(stacks, function):
    base = 0
    for ref in stacks:

        def block(b, carry, ref=ref, base=base):
            function(base + b, ref[b])
            return carry

        if ref.shape[0] == 1:
            block(0, 0)
        else:
            lax.fori_loop(0, ref.shape[0], block, 0)
        base += ref.shape[0]


def over_points(nfeat, nstacks, first, amplitude, kept, *refs):
    scale_ref, *refs = refs
    own_ref = refs.pop(0) if not first else None
    sofar_ref = refs.pop(0) if not first else None
    noise_ref, mine_ref = (refs.pop(0), refs.pop(0)) if amplitude else (None, None)
    stacks = refs[:nstacks]
    refs = refs[nstacks:]
    if first:
        own_ref = refs.pop(0)
        own_ref[...] = exponent_rows(
            stacks[0][0, 0:nfeat, :] / scale_ref[...], 1.0, False
        ).astype(BF16)
    out_ref, yt_ref, dirs_ref, acc_ref = refs[:1] + refs[-3:]
    keep_ref = refs[1] if kept else None

    def prepare(b, value):
        rows = exponent_rows(value[0:nfeat, :] / scale_ref[...], LOG2E, True)
        yt_ref[b] = rows.T.astype(BF16)
        put_dirs(dirs_ref, b, value[nfeat:, :])

    each(stacks, prepare)
    acc_ref[...] = jnp.zeros_like(acc_ref)

    def step(b, carry):
        add_block(yt_ref, b, own_ref, dirs_ref, acc_ref, keep_ref)
        return carry

    blocks = yt_ref.shape[0]
    lax.fori_loop(0, blocks, step, 0, unroll=2 if blocks % 2 == 0 else min(blocks, 3))
    total = folded(acc_ref)
    if not first:
        total = total + sofar_ref[...]
    if amplitude:
        total = amplitude * total + noise_ref[...] * mine_ref[0, nfeat:, :]
    out_ref[...] = total


def over_images(nstacks, table, sofar, form, amplitude, kept, *refs):
    refs = list(refs)
    table_ref = refs.pop(0) if table else None
    sofar_ref = refs.pop(0) if sofar else None
    if form:
        once_ref, noise_ref, mine_ref = refs.pop(0), refs.pop(0), refs.pop(0)
    own_ref = None if kept else refs.pop(0)
    source_ref, *refs = refs
    stacks = refs[:nstacks]
    out_ref, *refs = refs[nstacks:]
    form_ref = refs.pop(0) if form else None
    dirs_ref, acc_ref = refs

    def prepare(b, value):
        put_dirs(dirs_ref, b, value)

    each(stacks, prepare)
    acc_ref[...] = jnp.zeros_like(acc_ref)

    def step(s, carry):
        b = table_ref[s] if table else s
        if kept:
            add_kept_block(source_ref, b, dirs_ref, acc_ref)
        else:
            add_block(source_ref, b, own_ref, dirs_ref, acc_ref, None)
        return carry

    blocks = table_ref.shape[0] if table else source_ref.shape[0]
    lax.fori_loop(0, blocks, step, 0, unroll=2 if blocks % 2 == 0 else min(blocks, 3))
    total = folded(acc_ref)
    if sofar:
        total = total + sofar_ref[...]
    if form:
        mine = mine_ref[0]
        twice = once_ref[...] + 2.0 * total
        inner = mine * (amplitude * twice + noise_ref[...] * mine)
        form_ref[...] = jnp.broadcast_to(
            jnp.sum(inner, axis=1, keepdims=True), form_ref.shape
        )
        total = total + once_ref[...]
    out_ref[...] = total


def scalars_kernel(nfeat, count, *refs):
    blocks = refs[:count]
    images = refs[count : 2 * count]
    out_ref = refs[2 * count]
    nothing = jnp.zeros((images[0].shape[1], images[0].shape[2]), F32)

    def walk(function, carry):
        for b_ref, m_ref in zip(blocks, images):

            def block(k, carry, b_ref=b_ref, m_ref=m_ref):
                return function(carry, b_ref[k, nfeat:, :], m_ref[k])

            carry = lax.fori_loop(0, b_ref.shape[0], block, carry)
        return carry

    def total(value):
        return jnp.sum(value, axis=1, keepdims=True)

    norm, curv, square = walk(
        lambda c, r, w: (c[0] + r * r, c[1] + r * w, c[2] + w * w), (nothing,) * 3
    )
    norm, curv, square = total(norm), total(curv), total(square)
    alpha = norm / curv

    def left(carry, r, w):
        rest = r - alpha * w
        return carry + rest * rest

    norm_next = total(walk(left, nothing))
    gain = 1.0 + norm_next / norm
    part = gain * (gain * curv - 2.0 * alpha * square)
    for k, value in enumerate((alpha, gain, norm_next, part)):
        out_ref[k] = jnp.broadcast_to(value, out_ref.shape[1:])


def last_kernel(
    nfeat, amplitude, scalars_ref, form_ref, total_ref, noise_ref, mine_ref, image_ref,
    sol_ref, res_ref,
):
    alpha, gain, norm_next, part = [scalars_ref[k][:, 0:1] for k in range(4)]
    alpha_next = norm_next / (part + alpha * alpha * form_ref[:, 0:1])
    rhs = mine_ref[0, nfeat:, :]
    image = image_ref[0]
    twice = amplitude * total_ref[...] + noise_ref[...] * image
    sol_ref[...] = alpha * rhs + alpha_next * (gain * rhs - alpha * image)
    res_ref[...] = (rhs - alpha * image) - alpha_next * (gain * image - alpha * twice)


def shards(features, lengthscale, noise, rhs):
    nfeat, width = features.shape
    nrhs = rhs.shape[0]
    amplitude = 1.0 / math.sqrt(width * lax.axis_size("row"))
    scale = lengthscale[:, None]
    noise = noise[None, :]
    field = jax.ShapeDtypeStruct((nrhs, width), F32)
    small = jax.ShapeDtypeStruct((nrhs, 128), F32)
    smem = pl.BlockSpec(memory_space=pltpu.SMEM)
    vmem = pl.BlockSpec(memory_space=pltpu.VMEM)

    def call(kernel, blocks, work, out_shape, operands, name, table=False, fresh=0):
        entries = work * width * width
        scratch = [
            pltpu.VMEM((blocks, 2 * nrhs, 2 * width), BF16),
            pltpu.VMEM((2 * nrhs, width), F32),
        ]
        if fresh:
            scratch.insert(0, pltpu.VMEM((fresh, width, DEPTH), BF16))
        limit = 8 * MIB + blocks * 640 * width
        return pl.pallas_call(
            kernel,
            out_shape=out_shape,
            in_specs=[smem if table and k == 0 else vmem for k in range(len(operands))],
            scratch_shapes=scratch,
            compiler_params=pltpu.CompilerParams(vmem_limit_bytes=min(limit, 60 * MIB)),
            cost_estimate=pl.CostEstimate(
                flops=2 * entries * 4 * TILE, bytes_accessed=1024 * width, transcendentals=entries
            ),
            name=name,
        )(*operands)

    def amount(stacks):
        return sum(s.shape[0] for s in stacks)

    groups = gathered(jnp.concatenate([features, rhs], axis=0))
    mine = groups[0][0]
    own_shape = jax.ShapeDtypeStruct((DEPTH, width), BF16)
    room = 40 * MIB - lax.axis_size("row") * 512 * width
    keep = [False] * len(groups)
    for k in KEPT_ORDER:
        size = 4 * amount(groups[k]) * width * width
        keep[k] = size <= room
        room -= size if keep[k] else 0
    own, total, prepared = None, None, []
    for k, stacks in enumerate(groups):
        blocks = amount(stacks)
        final = k == len(groups) - 1
        if keep[k]:
            source = pltpu.VMEM((blocks, width // TILE, 2 * width, TILE), BF16)
        else:
            source = jax.ShapeDtypeStruct((blocks, width, DEPTH), BF16)
        out = (own_shape,) * (k == 0) + (field, source)
        *made, total, source = call(
            functools.partial(
                over_points, nfeat, len(stacks), k == 0, amplitude if final else None, keep[k]
            ),
            blocks, blocks, out,
            (scale,) + (() if k == 0 else (own, total)) + ((noise, mine) if final else ())
            + tuple(stacks),
            "blocks_%d" % k, fresh=blocks * keep[k],
        )
        own = made[0] if made else own
        prepared.append(source)
    images = gathered(total)
    image = images[0][0]

    def again(group, out, name, sofar=(), table=None, form=()):
        stacks = images[group]
        listed = () if table is None else (table,)
        work = amount(stacks) if table is None else table.shape[0]
        source = prepared[group]
        if keep[group]:
            source = pltpu.with_memory_space_constraint(source, pltpu.VMEM)
        return call(
            functools.partial(
                over_images, len(stacks), table is not None, bool(sofar), bool(form), amplitude,
                keep[group],
            ),
            amount(stacks), work, out,
            listed + tuple(sofar) + tuple(form) + (() if keep[group] else (own,))
            + (source,) + tuple(stacks),
            name, table is not None,
        )

    first, second, last_first, last_second = tables()
    once = again(0, field, "own_again")
    once = again(1, field, "line_again", sofar=(once,))
    half = again(2, field, "beside_half", table=first)
    total, form = again(
        3, (field, small), "across_half", sofar=(half,), table=last_first,
        form=(once, noise, image),
    )
    parts = along_line(form)
    total = again(2, field, "beside_rest", sofar=(total,), table=second)
    *parts, total = lax.optimization_barrier((*parts, total))
    form = sum(parts, form)
    parts = over_quad(form)
    total = again(3, field, "across_rest", sofar=(total,), table=last_second)
    *parts, total = lax.optimization_barrier((*parts, total))
    form = sum(parts, form)
    flat = [s for g in groups for s in g]
    flat_images = [s for g in images for s in g]
    scalars = pl.pallas_call(
        functools.partial(scalars_kernel, nfeat, len(flat)),
        out_shape=jax.ShapeDtypeStruct((4, nrhs, 128), F32),
        name="scalars",
    )(*flat, *flat_images)
    return pl.pallas_call(
        functools.partial(last_kernel, nfeat, amplitude),
        out_shape=(field, field),
        name="last_update",
    )(scalars, form, total, noise, mine, image)


def solution(mesh):
    in_specs = (P(None, ("grp", "row")), P(), P(("grp", "row")), P(None, ("grp", "row")))
    out_specs = (P(None, ("grp", "row")), P(None, ("grp", "row")))
    return jax.shard_map(shards, mesh=mesh, in_specs=in_specs, out_specs=out_specs, check_vma=False)
```

```python
import functools
import math

import jax
import jax.numpy as jnp
from jax import lax
from jax.experimental import pallas as pl
from jax.experimental.pallas import tpu as pltpu
from jax.sharding import PartitionSpec as P

LOG2E = math.log2(math.e)
DEPTH = 64
TILE = 256
MIB = 1024 * 1024
KEPT_ORDER = (0, 2, 4, 1, 3)
F32 = jnp.float32
BF16 = jnp.bfloat16


def pieces(value, count):
    parts = []
    for _ in range(count):
        part = value.astype(BF16).astype(F32)
        parts.append(part)
        value = value - part
    return parts


def exponent_rows(points, factor, visiting):
    big, mid, low = pieces(points * factor, 3)
    half_sq = jnp.sum(points * points, axis=0, keepdims=True) * (-0.5 * LOG2E)
    sq_parts = pieces(half_sq, 3)
    row = lax.broadcasted_iota(jnp.int32, points.shape, 0)
    first = 0 if visiting else 3
    tail = jnp.where((row >= 3 - first) & (row < 6 - first), 1.0, 0.0)
    for k, part in enumerate(sq_parts):
        tail = jnp.where(row == first + k, part, tail)
    order = [big, big, big, mid, mid, low] if visiting else [big, mid, low, big, mid, big]
    return jnp.concatenate(order + [tail, jnp.zeros_like(tail)], axis=0)


def put_dirs(dirs_ref, at, value):
    both = jnp.concatenate(pieces(value, 2), axis=0).astype(BF16)
    dirs_ref[at] = jnp.concatenate([both, both], axis=1)


def shifted(value, stride, size, by):
    length = lax.axis_size("row")
    pairs = []
    for i in range(length):
        digit = (i // stride) % size
        pairs.append((i, i + ((digit - by) % size - digit) * stride))
    return lax.ppermute(value, "row", pairs)


def digits():
    chips = lax.axis_size("row") // 2
    near = 1
    while near * near * 4 <= chips:
        near *= 2
    return chips // near, near


def gathered(value):
    far, near = digits()
    own = value[None]
    line = [shifted(own, 2 * near, far, by) for by in range(1, far)]
    group = jnp.concatenate([own] + line, axis=0)
    beside = [shifted(group, 2, near, by) for by in range(1, near)]
    across = [shifted(g, 1, 2, 1) for g in [group] + beside]
    return [own], line, beside, across[:1], across[1:]


def along_line(value):
    far, near = digits()
    return [shifted(value, 2 * near, far, by) for by in range(1, far)]


def over_quad(value):
    _, near = digits()
    length = lax.axis_size("row")
    quad = [shifted(value, 1, 2, 1)]
    for by in range(1, near):
        quad.append(shifted(value, 2, near, by))
        pairs = []
        for i in range(length):
            digit = (i // 2) % near
            pairs.append((i, (i + ((digit - by) % near - digit) * 2) ^ 1))
        quad.append(lax.ppermute(value, "row", pairs))
    return quad


def tables():
    far, near = digits()
    place = lax.axis_index("row")
    core = place % 2
    side = (place // 2 % near) // (near // 2)
    picks = jnp.arange(far // 2, dtype=jnp.int32) * 2
    first, second, last_first, last_second = [], [], [], []
    for k in range(near - 1):
        base = k * far
        shift = k + 1
        if 2 * shift == near:
            first.append(base + picks + side)
            second.append(base + picks + 1 - side)
        else:
            whole = base + jnp.arange(far, dtype=jnp.int32)
            (first if 2 * shift < near else second).append(whole)
        last_first.append(base + picks + core)
        last_second.append(base + picks + 1 - core)
    return (
        [jnp.concatenate(first), picks + core, jnp.concatenate(last_first)],
        [jnp.concatenate(second), picks + 1 - core, jnp.concatenate(last_second)],
    )


def add_block(yt_ref, at, own_ref, dirs_ref, acc_ref, keep_ref):
    width = own_ref.shape[1]
    for c in range(width // TILE):
        cols = slice(c * TILE, (c + 1) * TILE)
        expo = jnp.dot(yt_ref[at], own_ref[:, cols], preferred_element_type=F32)
        weight = jnp.exp2(expo)
        high = weight.astype(BF16)
        low = (weight - high.astype(F32)).astype(BF16)
        if keep_ref is not None:
            keep_ref[at, c, 0:width, :] = high
            keep_ref[at, c, width:, :] = low
        acc_ref[:, cols] += jnp.dot(
            dirs_ref[at, :, 0:width], high, preferred_element_type=F32
        ) + jnp.dot(dirs_ref[at, :, 0:width], low, preferred_element_type=F32)


def add_kept_block(keep_ref, at, dirs_ref, acc_ref):
    for c in range(keep_ref.shape[1]):
        acc_ref[:, c * TILE : (c + 1) * TILE] += jnp.dot(
            dirs_ref[at], keep_ref[at, c], preferred_element_type=F32
        )


def folded(acc_ref):
    nrhs = acc_ref.shape[0] // 2
    return acc_ref[0:nrhs, :] + acc_ref[nrhs:, :]


def unrolled(steps):
    return next(n for n in (4, 3, 2, 1) if steps % n == 0)


def each(stacks, function):
    base = 0
    for ref in stacks:

        def block(b, carry, ref=ref, base=base):
            function(base + b, ref[b])
            return carry

        if ref.shape[0] == 1:
            block(0, 0)
        else:
            lax.fori_loop(0, ref.shape[0], block, 0)
        base += ref.shape[0]


def over_points(nfeat, nstacks, first, amplitude, kept, *refs):
    scale_ref, *refs = refs
    own_ref = refs.pop(0) if not first else None
    sofar_ref = refs.pop(0) if not first else None
    noise_ref, mine_ref = (refs.pop(0), refs.pop(0)) if amplitude else (None, None)
    stacks = refs[:nstacks]
    refs = refs[nstacks:]
    if first:
        own_ref = refs.pop(0)
        own_ref[...] = exponent_rows(
            stacks[0][0, 0:nfeat, :] / scale_ref[...], 1.0, False
        ).astype(BF16)
    out_ref, yt_ref, dirs_ref, acc_ref = refs[:1] + refs[-3:]
    keep_ref = refs[1] if kept else None

    def prepare(b, value):
        rows = exponent_rows(value[0:nfeat, :] / scale_ref[...], LOG2E, True)
        yt_ref[b] = rows.T.astype(BF16)
        put_dirs(dirs_ref, b, value[nfeat:, :])

    each(stacks, prepare)
    acc_ref[...] = jnp.zeros_like(acc_ref)

    def step(b, carry):
        add_block(yt_ref, b, own_ref, dirs_ref, acc_ref, keep_ref)
        return carry

    blocks = yt_ref.shape[0]
    lax.fori_loop(0, blocks, step, 0, unroll=unrolled(blocks))
    total = folded(acc_ref)
    if not first:
        total = total + sofar_ref[...]
    if amplitude:
        total = amplitude * total + noise_ref[...] * mine_ref[0, nfeat:, :]
    out_ref[...] = total


def over_images(nstacks, table, sofar, form, amplitude, kept, *refs):
    refs = list(refs)
    table_ref = refs.pop(0) if table else None
    sofar_ref = refs.pop(0) if sofar else None
    if form:
        once_ref, noise_ref, mine_ref = refs.pop(0), refs.pop(0), refs.pop(0)
    own_ref = None if kept else refs.pop(0)
    source_ref, *refs = refs
    stacks = refs[:nstacks]
    out_ref, *refs = refs[nstacks:]
    form_ref = refs.pop(0) if form else None
    dirs_ref, acc_ref = refs

    def prepare(b, value):
        put_dirs(dirs_ref, b, value)

    alone = nstacks == 1
    if not alone:
        each(stacks, prepare)
    acc_ref[...] = jnp.zeros_like(acc_ref)

    def step(s, carry):
        b = table_ref[s] if table else s
        if alone:
            prepare(b, stacks[0][b])
        if kept:
            add_kept_block(source_ref, b, dirs_ref, acc_ref)
        else:
            add_block(source_ref, b, own_ref, dirs_ref, acc_ref, None)
        return carry

    blocks = table_ref.shape[0] if table else source_ref.shape[0]
    lax.fori_loop(0, blocks, step, 0, unroll=unrolled(blocks))
    total = folded(acc_ref)
    if sofar:
        total = total + sofar_ref[...]
    if form:
        mine = mine_ref[0]
        twice = once_ref[...] + 2.0 * total
        inner = mine * (amplitude * twice + noise_ref[...] * mine)
        form_ref[...] = jnp.broadcast_to(
            jnp.sum(inner, axis=1, keepdims=True), form_ref.shape
        )
        total = total + once_ref[...]
    out_ref[...] = total


def scalars_kernel(nfeat, count, *refs):
    blocks = refs[:count]
    images = refs[count : 2 * count]
    out_ref = refs[2 * count]
    nothing = jnp.zeros((images[0].shape[1], images[0].shape[2]), F32)

    def walk(function, carry):
        for b_ref, m_ref in zip(blocks, images):

            def block(k, carry, b_ref=b_ref, m_ref=m_ref):
                return function(carry, b_ref[k, nfeat:, :], m_ref[k])

            steps = b_ref.shape[0]
            carry = lax.fori_loop(0, steps, block, carry, unroll=unrolled(steps))
        return carry

    def total(value):
        return jnp.sum(value, axis=1, keepdims=True)

    norm, curv, square = walk(
        lambda c, r, w: (c[0] + r * r, c[1] + r * w, c[2] + w * w), (nothing,) * 3
    )
    norm, curv, square = total(norm), total(curv), total(square)
    alpha = norm / curv

    def left(carry, r, w):
        rest = r - alpha * w
        return carry + rest * rest

    norm_next = total(walk(left, nothing))
    gain = 1.0 + norm_next / norm
    part = gain * (gain * curv - 2.0 * alpha * square)
    for k, value in enumerate((alpha, gain, norm_next, part)):
        out_ref[k] = jnp.broadcast_to(value, out_ref.shape[1:])


def last_kernel(
    nfeat, amplitude, scalars_ref, form_ref, total_ref, noise_ref, mine_ref, image_ref,
    sol_ref, res_ref,
):
    alpha, gain, norm_next, part = [scalars_ref[k][:, 0:1] for k in range(4)]
    alpha_next = norm_next / (part + alpha * alpha * form_ref[:, 0:1])
    rhs = mine_ref[0, nfeat:, :]
    image = image_ref[0]
    twice = amplitude * total_ref[...] + noise_ref[...] * image
    sol_ref[...] = alpha * rhs + alpha_next * (gain * rhs - alpha * image)
    res_ref[...] = (rhs - alpha * image) - alpha_next * (gain * image - alpha * twice)


def shards(features, lengthscale, noise, rhs):
    nfeat, width = features.shape
    nrhs = rhs.shape[0]
    amplitude = 1.0 / math.sqrt(width * lax.axis_size("row"))
    scale = lengthscale[:, None]
    noise = noise[None, :]
    field = jax.ShapeDtypeStruct((nrhs, width), F32)
    small = jax.ShapeDtypeStruct((nrhs, 128), F32)
    smem = pl.BlockSpec(memory_space=pltpu.SMEM)
    vmem = pl.BlockSpec(memory_space=pltpu.VMEM)

    def call(kernel, blocks, work, out_shape, operands, name, table=False, fresh=0):
        entries = work * width * width
        scratch = [
            pltpu.VMEM((blocks, 2 * nrhs, 2 * width), BF16),
            pltpu.VMEM((2 * nrhs, width), F32),
        ]
        if fresh:
            scratch.insert(0, pltpu.VMEM((fresh, width, DEPTH), BF16))
        limit = 4 * MIB + blocks * 512 * width
        return pl.pallas_call(
            kernel,
            out_shape=out_shape,
            in_specs=[smem if table and k == 0 else vmem for k in range(len(operands))],
            scratch_shapes=scratch,
            compiler_params=pltpu.CompilerParams(vmem_limit_bytes=min(limit, 60 * MIB)),
            cost_estimate=pl.CostEstimate(
                flops=2 * entries * 4 * TILE, bytes_accessed=1024 * width, transcendentals=entries
            ),
            name=name,
        )(*operands)

    def amount(stacks):
        return sum(s.shape[0] for s in stacks)

    groups = gathered(jnp.concatenate([features, rhs], axis=0))
    mine = groups[0][0]
    own_shape = jax.ShapeDtypeStruct((DEPTH, width), BF16)
    room = 52 * MIB - lax.axis_size("row") * 512 * width
    keep = [False] * len(groups)
    for k in KEPT_ORDER:
        size = 4 * amount(groups[k]) * width * width
        keep[k] = size <= room
        room -= size if keep[k] else 0
    own, total, prepared = None, None, []
    for k, stacks in enumerate(groups):
        blocks = amount(stacks)
        final = k == len(groups) - 1
        if keep[k]:
            source = pltpu.VMEM((blocks, width // TILE, 2 * width, TILE), BF16)
        else:
            source = jax.ShapeDtypeStruct((blocks, width, DEPTH), BF16)
        out = (own_shape,) * (k == 0) + (field, source)
        *made, total, source = call(
            functools.partial(
                over_points, nfeat, len(stacks), k == 0, amplitude if final else None, keep[k]
            ),
            blocks, blocks, out,
            (scale,) + (() if k == 0 else (own, total)) + ((noise, mine) if final else ())
            + tuple(stacks),
            "blocks_%d" % k, fresh=blocks * keep[k],
        )
        own = made[0] if made else own
        prepared.append(source)
    images = gathered(total)
    image = images[0][0]

    def again(group, out, name, sofar=(), table=None, form=()):
        stacks = images[group]
        listed = () if table is None else (table,)
        work = amount(stacks) if table is None else table.shape[0]
        source = prepared[group]
        if keep[group]:
            source = pltpu.with_memory_space_constraint(source, pltpu.VMEM)
        return call(
            functools.partial(
                over_images, len(stacks), table is not None, bool(sofar), bool(form), amplitude,
                keep[group],
            ),
            amount(stacks), work, out,
            listed + tuple(sofar) + tuple(form) + (() if keep[group] else (own,))
            + (source,) + tuple(stacks),
            name, table is not None,
        )

    halves, rests = tables()
    once = again(0, field, "own_again")
    once = again(1, field, "line_again", sofar=(once,))
    half = again(2, field, "beside_half", table=halves[0])
    half = again(3, field, "across_half", sofar=(half,), table=halves[1])
    total, form = again(
        4, (field, small), "far_half", sofar=(half,), table=halves[2], form=(once, noise, image)
    )
    parts = along_line(form)
    total = again(2, field, "beside_rest", sofar=(total,), table=rests[0])
    total = again(3, field, "across_rest", sofar=(total,), table=rests[1])
    *parts, total = lax.optimization_barrier((*parts, total))
    form = sum(parts, form)
    parts = over_quad(form)
    total = again(4, field, "far_rest", sofar=(total,), table=rests[2])
    *parts, total = lax.optimization_barrier((*parts, total))
    form = sum(parts, form)
    flat = [s for g in groups for s in g]
    flat_images = [s for g in images for s in g]
    scalars = pl.pallas_call(
        functools.partial(scalars_kernel, nfeat, len(flat)),
        out_shape=jax.ShapeDtypeStruct((4, nrhs, 128), F32),
        compiler_params=pltpu.CompilerParams(
            vmem_limit_bytes=4 * MIB + 96 * lax.axis_size("row") * width
        ),
        name="scalars",
    )(*flat, *flat_images)
    return pl.pallas_call(
        functools.partial(last_kernel, nfeat, amplitude),
        out_shape=(field, field),
        compiler_params=pltpu.CompilerParams(vmem_limit_bytes=4 * MIB),
        name="last_update",
    )(scalars, form, total, noise, mine, image)


def solution(mesh):
    in_specs = (P(None, ("grp", "row")), P(), P(("grp", "row")), P(None, ("grp", "row")))
    out_specs = (P(None, ("grp", "row")), P(None, ("grp", "row")))
    return jax.shard_map(shards, mesh=mesh, in_specs=in_specs, out_specs=out_specs, check_vma=False)
```

```python
import functools
import math

import jax
import jax.numpy as jnp
from jax import lax
from jax.experimental import pallas as pl
from jax.experimental.pallas import tpu as pltpu
from jax.sharding import PartitionSpec as P

LOG2E = math.log2(math.e)
DEPTH = 64
TILE = 256
MIB = 1024 * 1024
KEPT_ORDER = (0, 1, 4, 3, 2)
KEPT_ROOM = 52 * MIB
F32 = jnp.float32
BF16 = jnp.bfloat16


def pieces(value, count):
    parts = []
    for _ in range(count):
        part = value.astype(BF16).astype(F32)
        parts.append(part)
        value = value - part
    return parts


def exponent_rows(points, factor, visiting):
    big, mid, low = pieces(points * factor, 3)
    half_sq = jnp.sum(points * points, axis=0, keepdims=True) * (-0.5 * LOG2E)
    sq_parts = pieces(half_sq, 3)
    row = lax.broadcasted_iota(jnp.int32, points.shape, 0)
    first = 0 if visiting else 3
    tail = jnp.where((row >= 3 - first) & (row < 6 - first), 1.0, 0.0)
    for k, part in enumerate(sq_parts):
        tail = jnp.where(row == first + k, part, tail)
    order = [big, big, big, mid, mid, low] if visiting else [big, mid, low, big, mid, big]
    return jnp.concatenate(order + [tail, jnp.zeros_like(tail)], axis=0)


def put_dirs(dirs_ref, at, value):
    both = jnp.concatenate(pieces(value, 2), axis=0).astype(BF16)
    dirs_ref[at] = jnp.concatenate([both, both], axis=1)


def swapped(value, far_by, near_by, core_by):
    length = lax.axis_size("row")
    _, near = digits()
    by = (far_by * near + near_by) * 2 + core_by
    return lax.ppermute(value, "row", [(i, i ^ by) for i in range(length)])


def digits():
    chips = lax.axis_size("row") // 2
    near = 1
    while near * near * 4 <= chips:
        near *= 2
    return chips // near, near


def gathered(value):
    far, near = digits()
    own = value[None]
    line = [swapped(own, by, 0, 0) for by in range(1, far)]
    group = jnp.concatenate([own] + line, axis=0)
    across = swapped(group, 0, 0, 1)
    beside = [swapped(group, 0, by, 0) for by in range(1, near)]
    return [own], line, [across], beside, [swapped(g, 0, 0, 1) for g in beside]


def along_line(value):
    far, _ = digits()
    return [swapped(value, by, 0, 0) for by in range(1, far)]


def over_quad(value):
    _, near = digits()
    return [swapped(value, 0, by // 2, by % 2) for by in range(1, 2 * near)]


def tables():
    far, near = digits()
    place = lax.axis_index("row")
    core = place % 2
    picks = jnp.arange(far // 2, dtype=jnp.int32) * 2
    sides = [(place // 2 // (by & -by)) % 2 for by in range(1, near)]

    def listed(flip):
        def one(k, side):
            return k * far + picks + (side + flip) % 2

        return [
            one(0, core),
            jnp.concatenate([one(k, side) for k, side in enumerate(sides)]),
            jnp.concatenate([one(k, core) for k in range(near - 1)]),
        ]

    return listed(0), listed(1)


def add_block(yt_ref, at, own_ref, dirs_ref, slot, acc_ref, keep_ref=None, kept_at=None):
    width = own_ref.shape[1]
    for c in range(width // TILE):
        cols = slice(c * TILE, (c + 1) * TILE)
        expo = jnp.dot(yt_ref[at], own_ref[:, cols], preferred_element_type=F32)
        weight = jnp.exp2(expo)
        high = weight.astype(BF16)
        low = (weight - high.astype(F32)).astype(BF16)
        if keep_ref is not None:
            keep_ref[kept_at, c, 0:width, :] = high
            keep_ref[kept_at, c, width:, :] = low
        acc_ref[:, cols] += jnp.dot(
            dirs_ref[slot, :, 0:width], high, preferred_element_type=F32
        ) + jnp.dot(dirs_ref[slot, :, 0:width], low, preferred_element_type=F32)


def add_kept_block(keep_ref, at, dirs_ref, slot, acc_ref):
    for c in range(keep_ref.shape[1]):
        acc_ref[:, c * TILE : (c + 1) * TILE] += jnp.dot(
            dirs_ref[slot], keep_ref[at, c], preferred_element_type=F32
        )


def folded(acc_ref):
    nrhs = acc_ref.shape[0] // 2
    return acc_ref[0:nrhs, :] + acc_ref[nrhs:, :]


def unrolled(steps):
    return next(n for n in (4, 3, 2, 1) if steps % n == 0)


def repeated(steps, function):
    if steps <= 4:
        for k in range(steps):
            function(k)
    else:

        def step(k, carry):
            function(k)
            return carry

        lax.fori_loop(0, steps, step, 0, unroll=unrolled(steps))


def each(stacks, function):
    base = 0
    for ref in stacks:
        repeated(ref.shape[0], lambda b, ref=ref, base=base: function(base + b, ref[b]))
        base += ref.shape[0]


def over_points(nfeat, nstacks, first, amplitude, kept, *refs):
    scale_ref, *refs = refs
    own_ref = refs.pop(0) if not first else None
    sofar_ref = refs.pop(0) if not first else None
    noise_ref, mine_ref = (refs.pop(0), refs.pop(0)) if amplitude else (None, None)
    stacks = refs[:nstacks]
    refs = refs[nstacks:]
    blocks = sum(ref.shape[0] for ref in stacks)
    if first:
        own_ref = refs.pop(0)
        own_ref[...] = exponent_rows(
            stacks[0][0, 0:nfeat, :] / scale_ref[...], 1.0, False
        ).astype(BF16)
    out_ref = refs.pop(0)
    keep_ref = refs.pop(0) if kept else None
    yt_ref = refs.pop(0) if kept < blocks else None
    dirs_ref, acc_ref, *fresh = refs
    acc_ref[...] = jnp.zeros_like(acc_ref)

    def step(b, value):
        rows = exponent_rows(value[0:nfeat, :] / scale_ref[...], LOG2E, True)
        put_dirs(dirs_ref, b, value[nfeat:, :])
        if kept and b < kept:
            fresh[0][b] = rows.T.astype(BF16)
            add_block(fresh[0], b, own_ref, dirs_ref, b, acc_ref, keep_ref, b)
        else:
            yt_ref[b - kept] = rows.T.astype(BF16)
            add_block(yt_ref, b - kept, own_ref, dirs_ref, b, acc_ref)

    each(stacks, step)
    total = folded(acc_ref)
    if not first:
        total = total + sofar_ref[...]
    if amplitude:
        total = amplitude * total + noise_ref[...] * mine_ref[0, nfeat:, :]
    out_ref[...] = total


def over_images(nstacks, table, sofar, form, amplitude, kept, blocks, *refs):
    refs = list(refs)
    table_ref = refs.pop(0) if table else None
    sofar_ref = refs.pop(0) if sofar else None
    if form:
        once_ref, noise_ref, mine_ref = refs.pop(0), refs.pop(0), refs.pop(0)
    keep_ref = refs.pop(0) if kept else None
    own_ref, yt_ref = (refs.pop(0), refs.pop(0)) if kept < blocks else (None, None)
    stacks = refs[:nstacks]
    out_ref, *refs = refs[nstacks:]
    form_ref = refs.pop(0) if form else None
    dirs_ref, acc_ref = refs
    acc_ref[...] = jnp.zeros_like(acc_ref)

    def add(at, slot, is_kept):
        if is_kept:
            add_kept_block(keep_ref, at, dirs_ref, slot, acc_ref)
        else:
            add_block(yt_ref, at - kept, own_ref, dirs_ref, slot, acc_ref)

    if table:
        if nstacks > 1:
            each(stacks, lambda b, value: put_dirs(dirs_ref, b, value))

        def step(s):
            b = table_ref[s]
            if nstacks == 1:
                put_dirs(dirs_ref, s, stacks[0][b])
            add(b, s if nstacks == 1 else b, bool(kept) and 2 * s + 1 < kept)

        repeated(table_ref.shape[0], step)
    else:

        def direct(b, value):
            put_dirs(dirs_ref, b, value)
            add(b, b, bool(kept) and b < kept)

        each(stacks, direct)
    total = folded(acc_ref)
    if sofar:
        total = total + sofar_ref[...]
    if form:
        mine = mine_ref[0]
        twice = once_ref[...] + 2.0 * total
        inner = mine * (amplitude * twice + noise_ref[...] * mine)
        form_ref[...] = jnp.broadcast_to(
            jnp.sum(inner, axis=1, keepdims=True), form_ref.shape
        )
        total = total + once_ref[...]
    out_ref[...] = total


def scalars_kernel(nfeat, count, *refs):
    blocks = refs[:count]
    images = refs[count : 2 * count]
    out_ref = refs[2 * count]
    nothing = jnp.zeros((images[0].shape[1], images[0].shape[2]), F32)

    def walk(function, carry):
        for b_ref, m_ref in zip(blocks, images):

            def block(k, carry, b_ref=b_ref, m_ref=m_ref):
                return function(carry, b_ref[k, nfeat:, :], m_ref[k])

            steps = b_ref.shape[0]
            carry = lax.fori_loop(0, steps, block, carry, unroll=unrolled(steps))
        return carry

    def total(value):
        return jnp.sum(value, axis=1, keepdims=True)

    norm, curv, square = walk(
        lambda c, r, w: (c[0] + r * r, c[1] + r * w, c[2] + w * w), (nothing,) * 3
    )
    norm, curv, square = total(norm), total(curv), total(square)
    alpha = norm / curv

    def left(carry, r, w):
        rest = r - alpha * w
        return carry + rest * rest

    norm_next = total(walk(left, nothing))
    gain = 1.0 + norm_next / norm
    part = gain * (gain * curv - 2.0 * alpha * square)
    for k, value in enumerate((alpha, gain, norm_next, part)):
        out_ref[k] = jnp.broadcast_to(value, out_ref.shape[1:])


def last_kernel(
    nfeat, amplitude, scalars_ref, form_ref, total_ref, noise_ref, mine_ref, image_ref,
    sol_ref, res_ref,
):
    alpha, gain, norm_next, part = [scalars_ref[k][:, 0:1] for k in range(4)]
    alpha_next = norm_next / (part + alpha * alpha * form_ref[:, 0:1])
    rhs = mine_ref[0, nfeat:, :]
    image = image_ref[0]
    twice = amplitude * total_ref[...] + noise_ref[...] * image
    sol_ref[...] = alpha * rhs + alpha_next * (gain * rhs - alpha * image)
    res_ref[...] = (rhs - alpha * image) - alpha_next * (gain * image - alpha * twice)


def shards(features, lengthscale, noise, rhs):
    nfeat, width = features.shape
    nrhs = rhs.shape[0]
    amplitude = 1.0 / math.sqrt(width * lax.axis_size("row"))
    scale = lengthscale[:, None]
    noise = noise[None, :]
    field = jax.ShapeDtypeStruct((nrhs, width), F32)
    small = jax.ShapeDtypeStruct((nrhs, 128), F32)
    smem = pl.BlockSpec(memory_space=pltpu.SMEM)
    vmem = pl.BlockSpec(memory_space=pltpu.VMEM)

    def call(kernel, blocks, work, out_shape, operands, name, table=False, fresh=0):
        entries = work * width * width
        scratch = [
            pltpu.VMEM((blocks, 2 * nrhs, 2 * width), BF16),
            pltpu.VMEM((2 * nrhs, width), F32),
        ]
        if fresh:
            scratch.append(pltpu.VMEM((fresh, width, DEPTH), BF16))
        limit = 4 * MIB + blocks * 512 * width
        return pl.pallas_call(
            kernel,
            out_shape=out_shape,
            in_specs=[smem if table and k == 0 else vmem for k in range(len(operands))],
            scratch_shapes=scratch,
            compiler_params=pltpu.CompilerParams(vmem_limit_bytes=min(limit, 60 * MIB)),
            cost_estimate=pl.CostEstimate(
                flops=2 * entries * 4 * TILE, bytes_accessed=1024 * width, transcendentals=entries
            ),
            name=name,
        )(*operands)

    def amount(stacks):
        return sum(s.shape[0] for s in stacks)

    groups = gathered(jnp.concatenate([features, rhs], axis=0))
    mine = groups[0][0]
    own_shape = jax.ShapeDtypeStruct((DEPTH, width), BF16)
    room = KEPT_ROOM - lax.axis_size("row") * 512 * width
    keep = [0] * len(groups)
    for k in KEPT_ORDER:
        fit = max(room, 0) // (4 * width * width)
        blocks = amount(groups[k])
        keep[k] = blocks if blocks <= fit else fit // 2 * 2 if blocks <= 4 else 0
        room -= 4 * keep[k] * width * width
    own, total, prepared = None, None, []
    for k, stacks in enumerate(groups):
        blocks = amount(stacks)
        final = k == len(groups) - 1
        made = (own_shape,) * (k == 0) + (field,)
        if keep[k]:
            made += (pltpu.VMEM((keep[k], width // TILE, 2 * width, TILE), BF16),)
        if keep[k] < blocks:
            made += (jax.ShapeDtypeStruct((blocks - keep[k], width, DEPTH), BF16),)
        made = call(
            functools.partial(
                over_points, nfeat, len(stacks), k == 0, amplitude if final else None, keep[k]
            ),
            blocks, blocks, made,
            (scale,) + (() if k == 0 else (own, total)) + ((noise, mine) if final else ())
            + tuple(stacks),
            "blocks_%d" % k, fresh=keep[k],
        )
        if k == 0:
            own, *made = made
        total, *sources = made
        prepared.append(sources)
    images = gathered(total)
    image = images[0][0]

    def again(group, out, name, sofar=(), table=None, form=()):
        stacks = images[group]
        blocks = amount(stacks)
        listed = () if table is None else (table,)
        work = blocks if table is None else table.shape[0]
        sources = list(prepared[group])
        if keep[group]:
            sources[0] = pltpu.with_memory_space_constraint(sources[0], pltpu.VMEM)
        if keep[group] < blocks:
            sources.insert(len(sources) - 1, own)
        return call(
            functools.partial(
                over_images, len(stacks), table is not None, bool(sofar), bool(form), amplitude,
                keep[group], blocks,
            ),
            blocks, work, out,
            listed + tuple(sofar) + tuple(form) + tuple(sources) + tuple(stacks),
            name, table is not None,
        )

    halves, rests = tables()
    once = again(0, field, "own_again")
    once = again(1, field, "line_again", sofar=(once,))
    half = again(2, field, "across_half", table=halves[0])
    half = again(3, field, "beside_half", sofar=(half,), table=halves[1])
    total, form = again(
        4, (field, small), "far_half", sofar=(half,), table=halves[2], form=(once, noise, image)
    )
    parts = along_line(form)
    total = again(2, field, "across_rest", sofar=(total,), table=rests[0])
    total = again(3, field, "beside_rest", sofar=(total,), table=rests[1])
    *parts, total = lax.optimization_barrier((*parts, total))
    form = sum(parts, form)
    parts = over_quad(form)
    total = again(4, field, "far_rest", sofar=(total,), table=rests[2])
    *parts, total = lax.optimization_barrier((*parts, total))
    form = sum(parts, form)
    flat = [s for g in groups for s in g]
    flat_images = [s for g in images for s in g]
    scalars = pl.pallas_call(
        functools.partial(scalars_kernel, nfeat, len(flat)),
        out_shape=jax.ShapeDtypeStruct((4, nrhs, 128), F32),
        compiler_params=pltpu.CompilerParams(
            vmem_limit_bytes=4 * MIB + 96 * lax.axis_size("row") * width
        ),
        name="scalars",
    )(*flat, *flat_images)
    return pl.pallas_call(
        functools.partial(last_kernel, nfeat, amplitude),
        out_shape=(field, field),
        compiler_params=pltpu.CompilerParams(vmem_limit_bytes=4 * MIB),
        name="last_update",
    )(scalars, form, total, noise, mine, image)


def solution(mesh):
    in_specs = (P(None, ("grp", "row")), P(), P(("grp", "row")), P(None, ("grp", "row")))
    out_specs = (P(None, ("grp", "row")), P(None, ("grp", "row")))
    return jax.shard_map(shards, mesh=mesh, in_specs=in_specs, out_specs=out_specs, check_vma=False)
```

```python
import functools
import math

import jax
import jax.numpy as jnp
from jax import lax
from jax.experimental import pallas as pl
from jax.experimental.pallas import tpu as pltpu
from jax.sharding import PartitionSpec as P

LOG2E = math.log2(math.e)
DEPTH = 64
TILE = 256
MIB = 1024 * 1024
KEPT_ORDER = (0, 1, 4, 3, 2)
KEPT_ROOM = 52 * MIB
F32 = jnp.float32
BF16 = jnp.bfloat16


def pieces(value, count):
    parts = []
    for _ in range(count):
        part = value.astype(BF16).astype(F32)
        parts.append(part)
        value = value - part
    return parts


def exponent_rows(points, factor, visiting):
    big, mid, low = pieces(points * factor, 3)
    half_sq = jnp.sum(points * points, axis=0, keepdims=True) * (-0.5 * LOG2E)
    sq_parts = pieces(half_sq, 3)
    row = lax.broadcasted_iota(jnp.int32, points.shape, 0)
    first = 0 if visiting else 3
    tail = jnp.where((row >= 3 - first) & (row < 6 - first), 1.0, 0.0)
    for k, part in enumerate(sq_parts):
        tail = jnp.where(row == first + k, part, tail)
    order = [big, big, big, mid, mid, low] if visiting else [big, mid, low, big, mid, big]
    return jnp.concatenate(order + [tail, jnp.zeros_like(tail)], axis=0)


def put_dirs(dirs_ref, at, value):
    both = jnp.concatenate(pieces(value, 2), axis=0).astype(BF16)
    dirs_ref[at] = jnp.concatenate([both, both], axis=1)


def swapped(value, far_by, near_by, core_by):
    length = lax.axis_size("row")
    _, near = digits()
    by = (far_by * near + near_by) * 2 + core_by
    return lax.ppermute(value, "row", [(i, i ^ by) for i in range(length)])


def turned(value, by):
    length = lax.axis_size("row")
    far, _ = digits()
    step = length // far
    return lax.ppermute(value, "row", [(i, (i - by * step) % length) for i in range(length)])


def digits():
    chips = lax.axis_size("row") // 2
    near = 1
    while near * near * 4 <= chips:
        near *= 2
    return chips // near, near


def gathered(value):
    far, near = digits()
    own = value[None]
    line = [turned(own, by) for by in range(1, far)]
    group = jnp.concatenate([own] + line, axis=0)
    across = swapped(group, 0, 0, 1)
    beside = [swapped(group, 0, by, 0) for by in range(1, near)]
    return [[own], line, [across], beside]


def held_back(groups, value):
    *beside, value = lax.optimization_barrier((*groups[3], value))
    return groups[:3] + [beside, [swapped(g, 0, 0, 1) for g in beside]], value


def along_line(value):
    far, _ = digits()
    return [turned(value, by) for by in range(1, far)]


def over_quad(value):
    _, near = digits()
    return [swapped(value, 0, by // 2, by % 2) for by in range(1, 2 * near)]


def tables():
    far, near = digits()
    place = lax.axis_index("row")
    core = place % 2
    picks = jnp.arange(far // 2, dtype=jnp.int32) * 2
    sides = [(place // 2 // (by & -by)) % 2 for by in range(1, near)]

    def listed(flip):
        def one(k, side):
            return k * far + picks + (side + flip) % 2

        return [
            one(0, core),
            jnp.concatenate([one(k, side) for k, side in enumerate(sides)]),
            jnp.concatenate([one(k, core) for k in range(near - 1)]),
        ]

    return listed(0), listed(1)


def add_block(yt_ref, at, own_ref, dirs_ref, slot, acc_ref, keep_ref=None, kept_at=None):
    width = own_ref.shape[1]
    for c in range(width // TILE):
        cols = slice(c * TILE, (c + 1) * TILE)
        expo = jnp.dot(yt_ref[at], own_ref[:, cols], preferred_element_type=F32)
        weight = jnp.exp2(expo)
        high = weight.astype(BF16)
        low = (weight - high.astype(F32)).astype(BF16)
        if keep_ref is not None:
            keep_ref[kept_at, c, 0:width, :] = high
            keep_ref[kept_at, c, width:, :] = low
        acc_ref[:, cols] += jnp.dot(
            dirs_ref[slot, :, 0:width], high, preferred_element_type=F32
        ) + jnp.dot(dirs_ref[slot, :, 0:width], low, preferred_element_type=F32)


def add_kept_block(keep_ref, at, dirs_ref, slot, acc_ref):
    for c in range(keep_ref.shape[1]):
        acc_ref[:, c * TILE : (c + 1) * TILE] += jnp.dot(
            dirs_ref[slot], keep_ref[at, c], preferred_element_type=F32
        )


def folded(acc_ref):
    nrhs = acc_ref.shape[0] // 2
    return acc_ref[0:nrhs, :] + acc_ref[nrhs:, :]


def unrolled(steps):
    return next(n for n in (4, 3, 2, 1) if steps % n == 0)


def repeated(steps, function):
    if steps <= 4:
        for k in range(steps):
            function(k)
    else:

        def step(k, carry):
            function(k)
            return carry

        lax.fori_loop(0, steps, step, 0, unroll=unrolled(steps))


def each(stacks, function):
    base = 0
    for ref in stacks:
        repeated(ref.shape[0], lambda b, ref=ref, base=base: function(base + b, ref[b]))
        base += ref.shape[0]


def over_points(nfeat, nstacks, first, amplitude, kept, *refs):
    scale_ref, *refs = refs
    own_ref = refs.pop(0) if not first else None
    sofar_ref = refs.pop(0) if not first else None
    noise_ref, mine_ref = (refs.pop(0), refs.pop(0)) if amplitude else (None, None)
    stacks = refs[:nstacks]
    refs = refs[nstacks:]
    blocks = sum(ref.shape[0] for ref in stacks)
    if first:
        own_ref = refs.pop(0)
        own_ref[...] = exponent_rows(
            stacks[0][0, 0:nfeat, :] / scale_ref[...], 1.0, False
        ).astype(BF16)
    out_ref = refs.pop(0)
    keep_ref = refs.pop(0) if kept else None
    yt_ref = refs.pop(0) if kept < blocks else None
    dirs_ref, acc_ref, *fresh = refs
    acc_ref[...] = jnp.zeros_like(acc_ref)

    def step(b, value):
        rows = exponent_rows(value[0:nfeat, :] / scale_ref[...], LOG2E, True)
        put_dirs(dirs_ref, b, value[nfeat:, :])
        if kept and b < kept:
            fresh[0][b] = rows.T.astype(BF16)
            add_block(fresh[0], b, own_ref, dirs_ref, b, acc_ref, keep_ref, b)
        else:
            yt_ref[b - kept] = rows.T.astype(BF16)
            add_block(yt_ref, b - kept, own_ref, dirs_ref, b, acc_ref)

    each(stacks, step)
    total = folded(acc_ref)
    if not first:
        total = total + sofar_ref[...]
    if amplitude:
        total = amplitude * total + noise_ref[...] * mine_ref[0, nfeat:, :]
    out_ref[...] = total


def over_images(nstacks, table, sofar, form, amplitude, kept, blocks, *refs):
    refs = list(refs)
    table_ref = refs.pop(0) if table else None
    sofar_ref = refs.pop(0) if sofar else None
    if form:
        once_ref, noise_ref, mine_ref = refs.pop(0), refs.pop(0), refs.pop(0)
    keep_ref = refs.pop(0) if kept else None
    own_ref, yt_ref = (refs.pop(0), refs.pop(0)) if kept < blocks else (None, None)
    stacks = refs[:nstacks]
    out_ref, *refs = refs[nstacks:]
    form_ref = refs.pop(0) if form else None
    dirs_ref, acc_ref = refs
    acc_ref[...] = jnp.zeros_like(acc_ref)

    def add(at, slot, is_kept):
        if is_kept:
            add_kept_block(keep_ref, at, dirs_ref, slot, acc_ref)
        else:
            add_block(yt_ref, at - kept, own_ref, dirs_ref, slot, acc_ref)

    if table:
        if nstacks > 1:
            each(stacks, lambda b, value: put_dirs(dirs_ref, b, value))

        def step(s):
            b = table_ref[s]
            if nstacks == 1:
                put_dirs(dirs_ref, s, stacks[0][b])
            add(b, s if nstacks == 1 else b, bool(kept) and 2 * s + 1 < kept)

        repeated(table_ref.shape[0], step)
    else:

        def direct(b, value):
            put_dirs(dirs_ref, b, value)
            add(b, b, bool(kept) and b < kept)

        each(stacks, direct)
    total = folded(acc_ref)
    if sofar:
        total = total + sofar_ref[...]
    if form:
        mine = mine_ref[0]
        twice = once_ref[...] + 2.0 * total
        inner = mine * (amplitude * twice + noise_ref[...] * mine)
        form_ref[...] = jnp.broadcast_to(
            jnp.sum(inner, axis=1, keepdims=True), form_ref.shape
        )
        total = total + once_ref[...]
    out_ref[...] = total


def scalars_kernel(nfeat, count, *refs):
    blocks = refs[:count]
    images = refs[count : 2 * count]
    out_ref = refs[2 * count]
    nothing = jnp.zeros((images[0].shape[1], images[0].shape[2]), F32)

    def walk(function, carry):
        for b_ref, m_ref in zip(blocks, images):

            def block(k, carry, b_ref=b_ref, m_ref=m_ref):
                return function(carry, b_ref[k, nfeat:, :], m_ref[k])

            steps = b_ref.shape[0]
            carry = lax.fori_loop(0, steps, block, carry, unroll=unrolled(steps))
        return carry

    def total(value):
        return jnp.sum(value, axis=1, keepdims=True)

    norm, curv, square = walk(
        lambda c, r, w: (c[0] + r * r, c[1] + r * w, c[2] + w * w), (nothing,) * 3
    )
    norm, curv, square = total(norm), total(curv), total(square)
    alpha = norm / curv

    def left(carry, r, w):
        rest = r - alpha * w
        return carry + rest * rest

    norm_next = total(walk(left, nothing))
    gain = 1.0 + norm_next / norm
    part = gain * (gain * curv - 2.0 * alpha * square)
    for k, value in enumerate((alpha, gain, norm_next, part)):
        out_ref[k] = jnp.broadcast_to(value, out_ref.shape[1:])


def last_kernel(
    nfeat, amplitude, scalars_ref, form_ref, total_ref, noise_ref, mine_ref, image_ref,
    sol_ref, res_ref,
):
    alpha, gain, norm_next, part = [scalars_ref[k][:, 0:1] for k in range(4)]
    alpha_next = norm_next / (part + alpha * alpha * form_ref[:, 0:1])
    rhs = mine_ref[0, nfeat:, :]
    image = image_ref[0]
    twice = amplitude * total_ref[...] + noise_ref[...] * image
    sol_ref[...] = alpha * rhs + alpha_next * (gain * rhs - alpha * image)
    res_ref[...] = (rhs - alpha * image) - alpha_next * (gain * image - alpha * twice)


def shards(features, lengthscale, noise, rhs):
    nfeat, width = features.shape
    nrhs = rhs.shape[0]
    amplitude = 1.0 / math.sqrt(width * lax.axis_size("row"))
    scale = lengthscale[:, None]
    noise = noise[None, :]
    field = jax.ShapeDtypeStruct((nrhs, width), F32)
    small = jax.ShapeDtypeStruct((nrhs, 128), F32)
    smem = pl.BlockSpec(memory_space=pltpu.SMEM)
    vmem = pl.BlockSpec(memory_space=pltpu.VMEM)

    def call(kernel, blocks, work, out_shape, operands, name, table=False, fresh=0):
        entries = work * width * width
        scratch = [
            pltpu.VMEM((blocks, 2 * nrhs, 2 * width), BF16),
            pltpu.VMEM((2 * nrhs, width), F32),
        ]
        if fresh:
            scratch.append(pltpu.VMEM((fresh, width, DEPTH), BF16))
        limit = 4 * MIB + blocks * 512 * width
        return pl.pallas_call(
            kernel,
            out_shape=out_shape,
            in_specs=[smem if table and k == 0 else vmem for k in range(len(operands))],
            scratch_shapes=scratch,
            compiler_params=pltpu.CompilerParams(vmem_limit_bytes=min(limit, 60 * MIB)),
            cost_estimate=pl.CostEstimate(
                flops=2 * entries * 4 * TILE, bytes_accessed=1024 * width, transcendentals=entries
            ),
            name=name,
        )(*operands)

    def amount(stacks):
        return sum(s.shape[0] for s in stacks)

    groups = gathered(jnp.concatenate([features, rhs], axis=0))
    mine = groups[0][0]
    own_shape = jax.ShapeDtypeStruct((DEPTH, width), BF16)
    room = KEPT_ROOM - lax.axis_size("row") * 512 * width
    sizes = [amount(g) for g in groups]
    sizes.append(sizes[3])
    keep = [0] * len(sizes)
    for k in KEPT_ORDER:
        fit = max(room, 0) // (4 * width * width)
        blocks = sizes[k]
        keep[k] = blocks if blocks <= fit else fit // 2 * 2 if blocks <= 4 else 0
        room -= 4 * keep[k] * width * width
    own, total, prepared = None, None, []
    for k, blocks in enumerate(sizes):
        if k == 3:
            groups, total = held_back(groups, total)
        stacks = groups[k]
        final = k == len(sizes) - 1
        made = (own_shape,) * (k == 0) + (field,)
        if keep[k]:
            made += (pltpu.VMEM((keep[k], width // TILE, 2 * width, TILE), BF16),)
        if keep[k] < blocks:
            made += (jax.ShapeDtypeStruct((blocks - keep[k], width, DEPTH), BF16),)
        made = call(
            functools.partial(
                over_points, nfeat, len(stacks), k == 0, amplitude if final else None, keep[k]
            ),
            blocks, blocks, made,
            (scale,) + (() if k == 0 else (own, total)) + ((noise, mine) if final else ())
            + tuple(stacks),
            "blocks_%d" % k, fresh=keep[k],
        )
        if k == 0:
            own, *made = made
        total, *sources = made
        prepared.append(sources)
    images = gathered(total)
    image = images[0][0]

    def again(group, out, name, sofar=(), table=None, form=()):
        stacks = images[group]
        blocks = amount(stacks)
        listed = () if table is None else (table,)
        work = blocks if table is None else table.shape[0]
        sources = list(prepared[group])
        if keep[group]:
            sources[0] = pltpu.with_memory_space_constraint(sources[0], pltpu.VMEM)
        if keep[group] < blocks:
            sources.insert(len(sources) - 1, own)
        return call(
            functools.partial(
                over_images, len(stacks), table is not None, bool(sofar), bool(form), amplitude,
                keep[group], blocks,
            ),
            blocks, work, out,
            listed + tuple(sofar) + tuple(form) + tuple(sources) + tuple(stacks),
            name, table is not None,
        )

    halves, rests = tables()
    once = again(0, field, "own_again")
    once = again(1, field, "line_again", sofar=(once,))
    half = again(2, field, "across_half", table=halves[0])
    images, half = held_back(images, half)
    half = again(3, field, "beside_half", sofar=(half,), table=halves[1])
    total, form = again(
        4, (field, small), "far_half", sofar=(half,), table=halves[2], form=(once, noise, image)
    )
    parts = along_line(form)
    total = again(2, field, "across_rest", sofar=(total,), table=rests[0])
    total = again(3, field, "beside_rest", sofar=(total,), table=rests[1])
    *parts, total = lax.optimization_barrier((*parts, total))
    form = sum(parts, form)
    parts = over_quad(form)
    total = again(4, field, "far_rest", sofar=(total,), table=rests[2])
    *parts, total = lax.optimization_barrier((*parts, total))
    form = sum(parts, form)
    flat = [s for g in groups for s in g]
    flat_images = [s for g in images for s in g]
    scalars = pl.pallas_call(
        functools.partial(scalars_kernel, nfeat, len(flat)),
        out_shape=jax.ShapeDtypeStruct((4, nrhs, 128), F32),
        compiler_params=pltpu.CompilerParams(
            vmem_limit_bytes=4 * MIB + 96 * lax.axis_size("row") * width
        ),
        name="scalars",
    )(*flat, *flat_images)
    return pl.pallas_call(
        functools.partial(last_kernel, nfeat, amplitude),
        out_shape=(field, field),
        compiler_params=pltpu.CompilerParams(vmem_limit_bytes=4 * MIB),
        name="last_update",
    )(scalars, form, total, noise, mine, image)


def solution(mesh):
    in_specs = (P(None, ("grp", "row")), P(), P(("grp", "row")), P(None, ("grp", "row")))
    out_specs = (P(None, ("grp", "row")), P(None, ("grp", "row")))
    return jax.shard_map(shards, mesh=mesh, in_specs=in_specs, out_specs=out_specs, check_vma=False)
```

```python
import functools
import math

import jax
import jax.numpy as jnp
from jax import lax
from jax.experimental import pallas as pl
from jax.experimental.pallas import tpu as pltpu
from jax.sharding import PartitionSpec as P

LOG2E = math.log2(math.e)
DEPTH = 64
TILE = 256
MIB = 1024 * 1024
KEPT_ORDER = (0, 1, 4, 3, 2)
KEPT_ROOM = 52 * MIB
F32 = jnp.float32
BF16 = jnp.bfloat16


def pieces(value, count):
    parts = []
    for _ in range(count):
        part = value.astype(BF16).astype(F32)
        parts.append(part)
        value = value - part
    return parts


def exponent_rows(points, factor, visiting):
    big, mid, low = pieces(points * factor, 3)
    half_sq = jnp.sum(points * points, axis=0, keepdims=True) * (-0.5 * LOG2E)
    sq_parts = pieces(half_sq, 3)
    row = lax.broadcasted_iota(jnp.int32, points.shape, 0)
    first = 0 if visiting else 3
    tail = jnp.where((row >= 3 - first) & (row < 6 - first), 1.0, 0.0)
    for k, part in enumerate(sq_parts):
        tail = jnp.where(row == first + k, part, tail)
    order = [big, big, big, mid, mid, low] if visiting else [big, mid, low, big, mid, big]
    return jnp.concatenate(order + [tail, jnp.zeros_like(tail)], axis=0)


def put_dirs(dirs_ref, at, value):
    both = jnp.concatenate(pieces(value, 2), axis=0).astype(BF16)
    dirs_ref[at] = jnp.concatenate([both, both], axis=1)


def swapped(value, far_by, near_by, core_by):
    length = lax.axis_size("row")
    _, near = digits()
    by = (far_by * near + near_by) * 2 + core_by
    return lax.ppermute(value, "row", [(i, i ^ by) for i in range(length)])


def turned(value, by):
    length = lax.axis_size("row")
    far, _ = digits()
    step = length // far
    return lax.ppermute(value, "row", [(i, (i - by * step) % length) for i in range(length)])


def digits():
    chips = lax.axis_size("row") // 2
    near = 1
    while near * near * 4 <= chips:
        near *= 2
    return chips // near, near


def gathered(value, at_once):
    far, near = digits()
    step = 2 * near
    if at_once:
        lines = [[step * z + k for z in range(far)] for k in range(step)]
        group = lax.all_gather(value, "row", axis_index_groups=lines)
        group = jnp.concatenate([group, group[:-1]], axis=0)
        group = lax.dynamic_slice_in_dim(group, lax.axis_index("row") // step, far, 0)
    else:
        own = value[None]
        group = jnp.concatenate([own] + [turned(own, by) for by in range(1, far)], axis=0)
    across = swapped(group, 0, 0, 1)
    beside = [swapped(group, 0, by, 0) for by in range(1, near)]
    return [[value[None]], [group], [across], beside]


def held_back(groups, value):
    *beside, value = lax.optimization_barrier((*groups[3], value))
    return groups[:3] + [beside, [swapped(g, 0, 0, 1) for g in beside]], value


def along_line(value):
    far, _ = digits()
    return [turned(value, by) for by in range(1, far)]


def over_quad(value):
    _, near = digits()
    return [swapped(value, 0, by // 2, by % 2) for by in range(1, 2 * near)]


def tables():
    far, near = digits()
    place = lax.axis_index("row")
    core = place % 2
    picks = jnp.arange(far // 2, dtype=jnp.int32) * 2
    sides = [(place // 2 // (by & -by)) % 2 for by in range(1, near)]

    def listed(flip):
        def one(k, side):
            return k * far + picks + (side + flip) % 2

        return [
            one(0, core),
            jnp.concatenate([one(k, side) for k, side in enumerate(sides)]),
            jnp.concatenate([one(k, core) for k in range(near - 1)]),
        ]

    others = 1 + jnp.arange(far - 1, dtype=jnp.int32)
    return others, listed(0), listed(1)


def add_block(yt_ref, at, own_ref, dirs_ref, slot, acc_ref, keep_ref=None, kept_at=None):
    width = own_ref.shape[1]
    for c in range(width // TILE):
        cols = slice(c * TILE, (c + 1) * TILE)
        expo = jnp.dot(yt_ref[at], own_ref[:, cols], preferred_element_type=F32)
        weight = jnp.exp2(expo)
        high = weight.astype(BF16)
        low = (weight - high.astype(F32)).astype(BF16)
        if keep_ref is not None:
            keep_ref[kept_at, c, 0:width, :] = high
            keep_ref[kept_at, c, width:, :] = low
        acc_ref[:, cols] += jnp.dot(
            dirs_ref[slot, :, 0:width], high, preferred_element_type=F32
        ) + jnp.dot(dirs_ref[slot, :, 0:width], low, preferred_element_type=F32)


def add_kept_block(keep_ref, at, dirs_ref, slot, acc_ref):
    for c in range(keep_ref.shape[1]):
        acc_ref[:, c * TILE : (c + 1) * TILE] += jnp.dot(
            dirs_ref[slot], keep_ref[at, c], preferred_element_type=F32
        )


def folded(acc_ref):
    nrhs = acc_ref.shape[0] // 2
    return acc_ref[0:nrhs, :] + acc_ref[nrhs:, :]


def unrolled(steps):
    return next(n for n in (4, 3, 2, 1) if steps % n == 0)


def repeated(steps, function):
    if steps <= 4:
        for k in range(steps):
            function(k)
    else:

        def step(k, carry):
            function(k)
            return carry

        lax.fori_loop(0, steps, step, 0, unroll=unrolled(steps))


def each(stacks, function):
    base = 0
    for ref in stacks:
        repeated(ref.shape[0], lambda b, ref=ref, base=base: function(base + b, ref[b]))
        base += ref.shape[0]


def over_points(nfeat, nstacks, first, amplitude, kept, table, *refs):
    refs = list(refs)
    table_ref = refs.pop(0) if table else None
    scale_ref = refs.pop(0)
    own_ref = refs.pop(0) if not first else None
    sofar_ref = refs.pop(0) if not first else None
    noise_ref, mine_ref = (refs.pop(0), refs.pop(0)) if amplitude else (None, None)
    stacks = refs[:nstacks]
    refs = refs[nstacks:]
    blocks = table_ref.shape[0] if table else sum(ref.shape[0] for ref in stacks)
    if first:
        own_ref = refs.pop(0)
        own_ref[...] = exponent_rows(
            stacks[0][0, 0:nfeat, :] / scale_ref[...], 1.0, False
        ).astype(BF16)
    out_ref = refs.pop(0)
    keep_ref = refs.pop(0) if kept else None
    yt_ref = refs.pop(0) if kept < blocks else None
    dirs_ref, acc_ref, *fresh = refs
    acc_ref[...] = jnp.zeros_like(acc_ref)

    def step(b, value):
        rows = exponent_rows(value[0:nfeat, :] / scale_ref[...], LOG2E, True)
        put_dirs(dirs_ref, b, value[nfeat:, :])
        if kept and b < kept:
            fresh[0][b] = rows.T.astype(BF16)
            add_block(fresh[0], b, own_ref, dirs_ref, b, acc_ref, keep_ref, b)
        else:
            yt_ref[b - kept] = rows.T.astype(BF16)
            add_block(yt_ref, b - kept, own_ref, dirs_ref, b, acc_ref)

    if table:
        repeated(blocks, lambda s: step(s, stacks[0][table_ref[s]]))
    else:
        each(stacks, step)
    total = folded(acc_ref)
    if not first:
        total = total + sofar_ref[...]
    if amplitude:
        total = amplitude * total + noise_ref[...] * mine_ref[0, nfeat:, :]
    out_ref[...] = total


def over_images(nstacks, table, line, sofar, form, amplitude, kept, blocks, *refs):
    refs = list(refs)
    table_ref = refs.pop(0) if table else None
    sofar_ref = refs.pop(0) if sofar else None
    if form:
        once_ref, noise_ref, mine_ref = refs.pop(0), refs.pop(0), refs.pop(0)
    keep_ref = refs.pop(0) if kept else None
    own_ref, yt_ref = (refs.pop(0), refs.pop(0)) if kept < blocks else (None, None)
    stacks = refs[:nstacks]
    out_ref, *refs = refs[nstacks:]
    form_ref = refs.pop(0) if form else None
    dirs_ref, acc_ref = refs
    acc_ref[...] = jnp.zeros_like(acc_ref)

    def add(at, slot, is_kept):
        if is_kept:
            add_kept_block(keep_ref, at, dirs_ref, slot, acc_ref)
        else:
            add_block(yt_ref, at - kept, own_ref, dirs_ref, slot, acc_ref)

    if line:

        def other(s):
            put_dirs(dirs_ref, s, stacks[0][table_ref[s]])
            add(s, s, bool(kept) and s < kept)

        repeated(blocks, other)
    elif table:
        if nstacks > 1:
            each(stacks, lambda b, value: put_dirs(dirs_ref, b, value))

        def step(s):
            b = table_ref[s]
            if nstacks == 1:
                put_dirs(dirs_ref, s, stacks[0][b])
            add(b, s if nstacks == 1 else b, bool(kept) and 2 * s + 1 < kept)

        repeated(table_ref.shape[0], step)
    else:

        def direct(b, value):
            put_dirs(dirs_ref, b, value)
            add(b, b, bool(kept) and b < kept)

        each(stacks, direct)
    total = folded(acc_ref)
    if sofar:
        total = total + sofar_ref[...]
    if form:
        mine = mine_ref[0]
        twice = once_ref[...] + 2.0 * total
        inner = mine * (amplitude * twice + noise_ref[...] * mine)
        form_ref[...] = jnp.broadcast_to(
            jnp.sum(inner, axis=1, keepdims=True), form_ref.shape
        )
        total = total + once_ref[...]
    out_ref[...] = total


def scalars_kernel(nfeat, count, *refs):
    blocks = refs[:count]
    images = refs[count : 2 * count]
    out_ref = refs[2 * count]
    nothing = jnp.zeros((images[0].shape[1], images[0].shape[2]), F32)

    def walk(function, carry):
        for b_ref, m_ref in zip(blocks, images):

            def block(k, carry, b_ref=b_ref, m_ref=m_ref):
                return function(carry, b_ref[k, nfeat:, :], m_ref[k])

            steps = b_ref.shape[0]
            carry = lax.fori_loop(0, steps, block, carry, unroll=unrolled(steps))
        return carry

    def total(value):
        return jnp.sum(value, axis=1, keepdims=True)

    norm, curv, square = walk(
        lambda c, r, w: (c[0] + r * r, c[1] + r * w, c[2] + w * w), (nothing,) * 3
    )
    norm, curv, square = total(norm), total(curv), total(square)
    alpha = norm / curv

    def left(carry, r, w):
        rest = r - alpha * w
        return carry + rest * rest

    norm_next = total(walk(left, nothing))
    gain = 1.0 + norm_next / norm
    part = gain * (gain * curv - 2.0 * alpha * square)
    for k, value in enumerate((alpha, gain, norm_next, part)):
        out_ref[k] = jnp.broadcast_to(value, out_ref.shape[1:])


def last_kernel(
    nfeat, amplitude, scalars_ref, form_ref, total_ref, noise_ref, mine_ref, image_ref,
    sol_ref, res_ref,
):
    alpha, gain, norm_next, part = [scalars_ref[k][:, 0:1] for k in range(4)]
    alpha_next = norm_next / (part + alpha * alpha * form_ref[:, 0:1])
    rhs = mine_ref[0, nfeat:, :]
    image = image_ref[0]
    twice = amplitude * total_ref[...] + noise_ref[...] * image
    sol_ref[...] = alpha * rhs + alpha_next * (gain * rhs - alpha * image)
    res_ref[...] = (rhs - alpha * image) - alpha_next * (gain * image - alpha * twice)


def shards(features, lengthscale, noise, rhs):
    nfeat, width = features.shape
    nrhs = rhs.shape[0]
    amplitude = 1.0 / math.sqrt(width * lax.axis_size("row"))
    scale = lengthscale[:, None]
    noise = noise[None, :]
    field = jax.ShapeDtypeStruct((nrhs, width), F32)
    small = jax.ShapeDtypeStruct((nrhs, 128), F32)
    smem = pl.BlockSpec(memory_space=pltpu.SMEM)
    vmem = pl.BlockSpec(memory_space=pltpu.VMEM)

    def call(kernel, blocks, work, out_shape, operands, name, table=False, fresh=0):
        entries = work * width * width
        scratch = [
            pltpu.VMEM((blocks, 2 * nrhs, 2 * width), BF16),
            pltpu.VMEM((2 * nrhs, width), F32),
        ]
        if fresh:
            scratch.append(pltpu.VMEM((fresh, width, DEPTH), BF16))
        limit = 4 * MIB + blocks * 512 * width
        return pl.pallas_call(
            kernel,
            out_shape=out_shape,
            in_specs=[smem if table and k == 0 else vmem for k in range(len(operands))],
            scratch_shapes=scratch,
            compiler_params=pltpu.CompilerParams(vmem_limit_bytes=min(limit, 60 * MIB)),
            cost_estimate=pl.CostEstimate(
                flops=2 * entries * 4 * TILE, bytes_accessed=1024 * width, transcendentals=entries
            ),
            name=name,
        )(*operands)

    def amount(stacks):
        return sum(s.shape[0] for s in stacks)

    groups = gathered(jnp.concatenate([features, rhs], axis=0), False)
    mine = groups[0][0]
    own_shape = jax.ShapeDtypeStruct((DEPTH, width), BF16)
    room = KEPT_ROOM - lax.axis_size("row") * 512 * width
    others, halves, rests = tables()
    sizes = [amount(g) for g in groups]
    sizes[1] -= 1
    sizes.append(sizes[3])
    keep = [0] * len(sizes)
    for k in KEPT_ORDER:
        fit = max(room, 0) // (4 * width * width)
        blocks = sizes[k]
        keep[k] = blocks if blocks <= fit else fit // 2 * 2 if blocks <= 4 else 0
        room -= 4 * keep[k] * width * width
    own, total, prepared = None, None, []
    for k, blocks in enumerate(sizes):
        if k == 3:
            groups, total = held_back(groups, total)
        stacks = groups[k]
        final = k == len(sizes) - 1
        made = (own_shape,) * (k == 0) + (field,)
        if keep[k]:
            made += (pltpu.VMEM((keep[k], width // TILE, 2 * width, TILE), BF16),)
        if keep[k] < blocks:
            made += (jax.ShapeDtypeStruct((blocks - keep[k], width, DEPTH), BF16),)
        made = call(
            functools.partial(
                over_points, nfeat, len(stacks), k == 0, amplitude if final else None, keep[k],
                k == 1,
            ),
            blocks, blocks, made,
            ((others,) if k == 1 else ()) + (scale,) + (() if k == 0 else (own, total)) + ((noise, mine) if final else ())
            + tuple(stacks),
            "blocks_%d" % k, k == 1, fresh=keep[k],
        )
        if k == 0:
            own, *made = made
        total, *sources = made
        prepared.append(sources)
    images = gathered(total, True)
    image = images[0][0]

    def again(group, out, name, sofar=(), table=None, form=()):
        stacks = images[group]
        blocks = sizes[group]
        listed = () if table is None else (table,)
        work = blocks if table is None else table.shape[0]
        sources = list(prepared[group])
        if keep[group]:
            sources[0] = pltpu.with_memory_space_constraint(sources[0], pltpu.VMEM)
        if keep[group] < blocks:
            sources.insert(len(sources) - 1, own)
        return call(
            functools.partial(
                over_images, len(stacks), table is not None, group == 1, bool(sofar), bool(form),
                amplitude, keep[group], blocks,
            ),
            blocks, work, out,
            listed + tuple(sofar) + tuple(form) + tuple(sources) + tuple(stacks),
            name, table is not None,
        )

    once = again(0, field, "own_again")
    once = again(1, field, "line_again", sofar=(once,), table=others)
    half = again(2, field, "across_half", table=halves[0])
    images, half = held_back(images, half)
    half = again(3, field, "beside_half", sofar=(half,), table=halves[1])
    total, form = again(
        4, (field, small), "far_half", sofar=(half,), table=halves[2], form=(once, noise, image)
    )
    parts = along_line(form)
    total = again(2, field, "across_rest", sofar=(total,), table=rests[0])
    total = again(3, field, "beside_rest", sofar=(total,), table=rests[1])
    *parts, total = lax.optimization_barrier((*parts, total))
    form = sum(parts, form)
    parts = over_quad(form)
    total = again(4, field, "far_rest", sofar=(total,), table=rests[2])
    *parts, total = lax.optimization_barrier((*parts, total))
    form = sum(parts, form)
    flat = [s for g in groups[1:] for s in g]
    flat_images = [s for g in images[1:] for s in g]
    scalars = pl.pallas_call(
        functools.partial(scalars_kernel, nfeat, len(flat)),
        out_shape=jax.ShapeDtypeStruct((4, nrhs, 128), F32),
        compiler_params=pltpu.CompilerParams(
            vmem_limit_bytes=4 * MIB + 96 * lax.axis_size("row") * width
        ),
        name="scalars",
    )(*flat, *flat_images)
    return pl.pallas_call(
        functools.partial(last_kernel, nfeat, amplitude),
        out_shape=(field, field),
        compiler_params=pltpu.CompilerParams(vmem_limit_bytes=4 * MIB),
        name="last_update",
    )(scalars, form, total, noise, mine, image)


def solution(mesh):
    in_specs = (P(None, ("grp", "row")), P(), P(("grp", "row")), P(None, ("grp", "row")))
    out_specs = (P(None, ("grp", "row")), P(None, ("grp", "row")))
    return jax.shard_map(shards, mesh=mesh, in_specs=in_specs, out_specs=out_specs, check_vma=False)
```

```python
import functools
import math

import jax
import jax.numpy as jnp
from jax import lax
from jax.experimental import pallas as pl
from jax.experimental.pallas import tpu as pltpu
from jax.sharding import PartitionSpec as P

LOG2E = math.log2(math.e)
DEPTH = 64
TILE = 256
MIB = 1024 * 1024
KEPT_ORDER = (1, 4, 3)
KEPT_ROOM = 44 * MIB
F32 = jnp.float32
BF16 = jnp.bfloat16


def pieces(value, count):
    parts = []
    for _ in range(count):
        part = value.astype(BF16).astype(F32)
        parts.append(part)
        value = value - part
    return parts


def exponent_rows(points, factor, visiting):
    big, mid, low = pieces(points * factor, 3)
    half_sq = jnp.sum(points * points, axis=0, keepdims=True) * (-0.5 * LOG2E)
    sq_parts = pieces(half_sq, 3)
    row = lax.broadcasted_iota(jnp.int32, points.shape, 0)
    first = 0 if visiting else 3
    tail = jnp.where((row >= 3 - first) & (row < 6 - first), 1.0, 0.0)
    for k, part in enumerate(sq_parts):
        tail = jnp.where(row == first + k, part, tail)
    order = [big, big, big, mid, mid, low] if visiting else [big, mid, low, big, mid, big]
    return jnp.concatenate(order + [tail, jnp.zeros_like(tail)], axis=0)


def put_dirs(dirs_ref, at, value):
    both = jnp.concatenate(pieces(value, 2), axis=0).astype(BF16)
    dirs_ref[at] = jnp.concatenate([both, both], axis=1)


def swapped(value, far_by, near_by, core_by):
    length = lax.axis_size("row")
    _, near = digits()
    by = (far_by * near + near_by) * 2 + core_by
    return lax.ppermute(value, "row", [(i, i ^ by) for i in range(length)])


def turned(value, by):
    length = lax.axis_size("row")
    far, _ = digits()
    step = length // far
    return lax.ppermute(value, "row", [(i, (i - by * step) % length) for i in range(length)])


def digits():
    chips = lax.axis_size("row") // 2
    near = 1
    while near * near * 4 <= chips:
        near *= 2
    return chips // near, near


def gathered(value):
    far, near = digits()
    own = value[None]
    line = [turned(own, by) for by in range(1, far)]
    group = jnp.concatenate([own] + line, axis=0)
    across = swapped(group, 0, 0, 1)
    beside = [swapped(group, 0, by, 0) for by in range(1, near)]
    return [[own], line, [across], beside]


def held_back(groups, value):
    *beside, value = lax.optimization_barrier((*groups[3], value))
    return groups[:3] + [beside, [swapped(g, 0, 0, 1) for g in beside]], value


def along_line(value):
    far, _ = digits()
    return [turned(value, by) for by in range(1, far)]


def over_quad(value):
    _, near = digits()
    return [swapped(value, 0, by // 2, by % 2) for by in range(1, 2 * near)]


def tables():
    far, near = digits()
    place = lax.axis_index("row")
    core = place % 2
    picks = jnp.arange(far // 2, dtype=jnp.int32) * 2
    sides = [(place // 2 // (by & -by)) % 2 for by in range(1, near)]

    def listed(flip):
        def one(k, side):
            return k * far + picks + (side + flip) % 2

        return [
            one(0, core),
            jnp.concatenate([one(k, side) for k, side in enumerate(sides)]),
            jnp.concatenate([one(k, core) for k in range(near - 1)]),
        ]

    return listed(0), listed(1)


def add_block(yt_ref, at, own_ref, dirs_ref, slot, acc_ref, keep_ref=None, kept_at=None):
    width = own_ref.shape[1]
    for c in range(width // TILE):
        cols = slice(c * TILE, (c + 1) * TILE)
        expo = jnp.dot(yt_ref[at], own_ref[:, cols], preferred_element_type=F32)
        weight = jnp.exp2(expo)
        high = weight.astype(BF16)
        low = (weight - high.astype(F32)).astype(BF16)
        if keep_ref is not None:
            keep_ref[kept_at, c, 0:width, :] = high
            keep_ref[kept_at, c, width:, :] = low
        acc_ref[:, cols] += jnp.dot(
            dirs_ref[slot, :, 0:width], high, preferred_element_type=F32
        ) + jnp.dot(dirs_ref[slot, :, 0:width], low, preferred_element_type=F32)


def add_kept_block(keep_ref, at, dirs_ref, slot, acc_ref):
    for c in range(keep_ref.shape[1]):
        acc_ref[:, c * TILE : (c + 1) * TILE] += jnp.dot(
            dirs_ref[slot], keep_ref[at, c], preferred_element_type=F32
        )


def folded(acc_ref):
    nrhs = acc_ref.shape[0] // 2
    return acc_ref[0:nrhs, :] + acc_ref[nrhs:, :]


def unrolled(steps):
    return next(n for n in (4, 3, 2, 1) if steps % n == 0)


def repeated(steps, function):
    if steps <= 4:
        for k in range(steps):
            function(k)
    else:

        def step(k, carry):
            function(k)
            return carry

        lax.fori_loop(0, steps, step, 0, unroll=unrolled(steps))


def each(stacks, function):
    base = 0
    for ref in stacks:
        repeated(ref.shape[0], lambda b, ref=ref, base=base: function(base + b, ref[b]))
        base += ref.shape[0]


def over_points(nfeat, nstacks, first, amplitude, kept, *refs):
    refs = list(refs)
    own_ref = refs.pop(0) if not first else None
    sofar_ref = refs.pop(0) if not first else None
    noise_ref, mine_ref = (refs.pop(0), refs.pop(0)) if amplitude else (None, None)
    stacks = refs[:nstacks]
    refs = refs[nstacks:]
    blocks = sum(ref.shape[0] for ref in stacks)
    if first:
        own_ref = refs.pop(0)
        own_ref[...] = exponent_rows(
            stacks[0][0, 0:nfeat, :], 1.0, False
        ).astype(BF16)
    out_ref = refs.pop(0)
    keep_ref = refs.pop(0) if kept else None
    yt_ref = refs.pop(0) if kept < blocks else None
    dirs_ref, acc_ref, *fresh = refs
    acc_ref[...] = jnp.zeros_like(acc_ref)

    def step(b, value):
        rows = exponent_rows(value[0:nfeat, :], LOG2E, True)
        put_dirs(dirs_ref, b, value[nfeat:, :])
        if kept and b < kept:
            fresh[0][b] = rows.T.astype(BF16)
            add_block(fresh[0], b, own_ref, dirs_ref, b, acc_ref, keep_ref, b)
        else:
            yt_ref[b - kept] = rows.T.astype(BF16)
            add_block(yt_ref, b - kept, own_ref, dirs_ref, b, acc_ref)

    each(stacks, step)
    total = folded(acc_ref)
    if not first:
        total = total + sofar_ref[...]
    if amplitude:
        total = amplitude * total + noise_ref[...] * mine_ref[0, nfeat:, :]
    out_ref[...] = total


def over_images(nstacks, table, sofar, form, amplitude, kept, blocks, *refs):
    refs = list(refs)
    table_ref = refs.pop(0) if table else None
    sofar_ref = refs.pop(0) if sofar else None
    if form:
        once_ref, noise_ref, mine_ref = refs.pop(0), refs.pop(0), refs.pop(0)
    keep_ref = refs.pop(0) if kept else None
    own_ref, yt_ref = (refs.pop(0), refs.pop(0)) if kept < blocks else (None, None)
    stacks = refs[:nstacks]
    out_ref, *refs = refs[nstacks:]
    form_ref = refs.pop(0) if form else None
    dirs_ref, acc_ref = refs
    acc_ref[...] = jnp.zeros_like(acc_ref)

    def add(at, slot, is_kept):
        if is_kept:
            add_kept_block(keep_ref, at, dirs_ref, slot, acc_ref)
        else:
            add_block(yt_ref, at - kept, own_ref, dirs_ref, slot, acc_ref)

    if table:
        if nstacks > 1:
            each(stacks, lambda b, value: put_dirs(dirs_ref, b, value))

        def step(s):
            b = table_ref[s]
            if nstacks == 1:
                put_dirs(dirs_ref, s, stacks[0][b])
            add(b, s if nstacks == 1 else b, bool(kept) and 2 * s + 1 < kept)

        repeated(table_ref.shape[0], step)
    else:

        def direct(b, value):
            put_dirs(dirs_ref, b, value)
            add(b, b, bool(kept) and b < kept)

        each(stacks, direct)
    total = folded(acc_ref)
    if sofar:
        total = total + sofar_ref[...]
    if form:
        mine = mine_ref[0]
        twice = once_ref[...] + 2.0 * total
        inner = mine * (amplitude * twice + noise_ref[...] * mine)
        form_ref[...] = jnp.broadcast_to(
            jnp.sum(inner, axis=1, keepdims=True), form_ref.shape
        )
        total = total + once_ref[...]
    out_ref[...] = total


def scalars_kernel(nfeat, count, *refs):
    blocks = refs[:count]
    images = refs[count : 2 * count]
    out_ref = refs[2 * count]
    nothing = jnp.zeros((images[0].shape[1], images[0].shape[2]), F32)

    def walk(function, carry):
        for b_ref, m_ref in zip(blocks, images):

            def block(k, carry, b_ref=b_ref, m_ref=m_ref):
                return function(carry, b_ref[k, nfeat:, :], m_ref[k])

            steps = b_ref.shape[0]
            carry = lax.fori_loop(0, steps, block, carry, unroll=unrolled(steps))
        return carry

    def total(value):
        return jnp.sum(value, axis=1, keepdims=True)

    norm, curv, square = walk(
        lambda c, r, w: (c[0] + r * r, c[1] + r * w, c[2] + w * w), (nothing,) * 3
    )
    norm, curv, square = total(norm), total(curv), total(square)
    alpha = norm / curv

    def left(carry, r, w):
        rest = r - alpha * w
        return carry + rest * rest

    norm_next = total(walk(left, nothing))
    gain = 1.0 + norm_next / norm
    part = gain * (gain * curv - 2.0 * alpha * square)
    for k, value in enumerate((alpha, gain, norm_next, part)):
        out_ref[k] = jnp.broadcast_to(value, out_ref.shape[1:])


def last_kernel(
    nfeat, amplitude, scalars_ref, form_ref, total_ref, noise_ref, mine_ref, image_ref,
    sol_ref, res_ref,
):
    alpha, gain, norm_next, part = [scalars_ref[k][:, 0:1] for k in range(4)]
    alpha_next = norm_next / (part + alpha * alpha * form_ref[:, 0:1])
    rhs = mine_ref[0, nfeat:, :]
    image = image_ref[0]
    twice = amplitude * total_ref[...] + noise_ref[...] * image
    sol_ref[...] = alpha * rhs + alpha_next * (gain * rhs - alpha * image)
    res_ref[...] = (rhs - alpha * image) - alpha_next * (gain * image - alpha * twice)


def shards(features, lengthscale, noise, rhs):
    nfeat, width = features.shape
    nrhs = rhs.shape[0]
    amplitude = 1.0 / math.sqrt(width * lax.axis_size("row"))
    scaled = features / lengthscale[:, None]
    noise = noise[None, :]
    field = jax.ShapeDtypeStruct((nrhs, width), F32)
    small = jax.ShapeDtypeStruct((nrhs, 128), F32)
    smem = pl.BlockSpec(memory_space=pltpu.SMEM)
    vmem = pl.BlockSpec(memory_space=pltpu.VMEM)

    def call(kernel, blocks, work, out_shape, operands, name, table=False, fresh=0):
        entries = work * width * width
        scratch = [
            pltpu.VMEM((blocks, 2 * nrhs, 2 * width), BF16),
            pltpu.VMEM((2 * nrhs, width), F32),
        ]
        if fresh:
            scratch.append(pltpu.VMEM((fresh, width, DEPTH), BF16))
        limit = 4 * MIB + blocks * 512 * width
        return pl.pallas_call(
            kernel,
            out_shape=out_shape,
            in_specs=[smem if table and k == 0 else vmem for k in range(len(operands))],
            scratch_shapes=scratch,
            compiler_params=pltpu.CompilerParams(vmem_limit_bytes=min(limit, 60 * MIB)),
            cost_estimate=pl.CostEstimate(
                flops=2 * entries * 4 * TILE, bytes_accessed=1024 * width, transcendentals=entries
            ),
            name=name,
        )(*operands)

    def amount(stacks):
        return sum(s.shape[0] for s in stacks)

    groups = gathered(jnp.concatenate([scaled, rhs], axis=0))
    mine = groups[0][0]
    own_shape = jax.ShapeDtypeStruct((DEPTH, width), BF16)
    room = KEPT_ROOM - lax.axis_size("row") * 512 * width
    sizes = [amount(g) for g in groups]
    sizes.append(sizes[3])
    keep = [0] * len(sizes)
    for k in KEPT_ORDER:
        fit = max(room, 0) // (4 * width * width)
        blocks = sizes[k]
        keep[k] = blocks if blocks <= fit else fit // 2 * 2 if blocks <= 4 else 0
        room -= 4 * keep[k] * width * width
    own, total, prepared = None, None, []
    for k, blocks in enumerate(sizes):
        if k == 3:
            groups, total = held_back(groups, total)
        stacks = groups[k]
        final = k == len(sizes) - 1
        made = (own_shape,) * (k == 0) + (field,)
        if keep[k]:
            made += (pltpu.VMEM((keep[k], width // TILE, 2 * width, TILE), BF16),)
        if keep[k] < blocks:
            made += (jax.ShapeDtypeStruct((blocks - keep[k], width, DEPTH), BF16),)
        made = call(
            functools.partial(
                over_points, nfeat, len(stacks), k == 0, amplitude if final else None, keep[k]
            ),
            blocks, blocks, made,
            (() if k == 0 else (own, total)) + ((noise, mine) if final else ())
            + tuple(stacks),
            "blocks_%d" % k, fresh=keep[k],
        )
        if k == 0:
            own, *made = made
        total, *sources = made
        prepared.append(sources)
    images = gathered(total)
    image = images[0][0]

    def again(group, out, name, sofar=(), table=None, form=()):
        stacks = images[group]
        blocks = amount(stacks)
        listed = () if table is None else (table,)
        work = blocks if table is None else table.shape[0]
        sources = list(prepared[group])
        if keep[group]:
            sources[0] = pltpu.with_memory_space_constraint(sources[0], pltpu.VMEM)
        if keep[group] < blocks:
            sources.insert(len(sources) - 1, own)
        return call(
            functools.partial(
                over_images, len(stacks), table is not None, bool(sofar), bool(form), amplitude,
                keep[group], blocks,
            ),
            blocks, work, out,
            listed + tuple(sofar) + tuple(form) + tuple(sources) + tuple(stacks),
            name, table is not None,
        )

    halves, rests = tables()
    once = again(0, field, "own_again")
    once = again(1, field, "line_again", sofar=(once,))
    half = again(2, field, "across_half", table=halves[0])
    images, half = held_back(images, half)
    half = again(3, field, "beside_half", sofar=(half,), table=halves[1])
    total, form = again(
        4, (field, small), "far_half", sofar=(half,), table=halves[2], form=(once, noise, image)
    )
    parts = along_line(form)
    total = again(2, field, "across_rest", sofar=(total,), table=rests[0])
    total = again(3, field, "beside_rest", sofar=(total,), table=rests[1])
    *parts, total = lax.optimization_barrier((*parts, total))
    form = sum(parts, form)
    parts = over_quad(form)
    total = again(4, field, "far_rest", sofar=(total,), table=rests[2])
    *parts, total = lax.optimization_barrier((*parts, total))
    form = sum(parts, form)
    flat = [s for g in groups for s in g]
    flat_images = [s for g in images for s in g]
    scalars = pl.pallas_call(
        functools.partial(scalars_kernel, nfeat, len(flat)),
        out_shape=jax.ShapeDtypeStruct((4, nrhs, 128), F32),
        compiler_params=pltpu.CompilerParams(
            vmem_limit_bytes=4 * MIB + 96 * lax.axis_size("row") * width
        ),
        name="scalars",
    )(*flat, *flat_images)
    return pl.pallas_call(
        functools.partial(last_kernel, nfeat, amplitude),
        out_shape=(field, field),
        compiler_params=pltpu.CompilerParams(vmem_limit_bytes=4 * MIB),
        name="last_update",
    )(scalars, form, total, noise, mine, image)


def solution(mesh):
    in_specs = (P(None, ("grp", "row")), P(), P(("grp", "row")), P(None, ("grp", "row")))
    out_specs = (P(None, ("grp", "row")), P(None, ("grp", "row")))
    return jax.shard_map(shards, mesh=mesh, in_specs=in_specs, out_specs=out_specs, check_vma=False)
```

```python
import functools
import math

import jax
import jax.numpy as jnp
from jax import lax
from jax.experimental import pallas as pl
from jax.experimental.pallas import tpu as pltpu
from jax.sharding import PartitionSpec as P

LOG2E = math.log2(math.e)
DEPTH = 64
TILE = 256
MIB = 1024 * 1024
KEPT_ORDER = (1, 4, 3)
KEPT_ROOM = 44 * MIB
F32 = jnp.float32
BF16 = jnp.bfloat16


def pieces(value, count):
    parts = []
    for _ in range(count):
        part = value.astype(BF16).astype(F32)
        parts.append(part)
        value = value - part
    return parts


def exponent_rows(points, factor, visiting):
    big, mid, low = pieces(points * factor, 3)
    half_sq = jnp.sum(points * points, axis=0, keepdims=True) * (-0.5 * LOG2E)
    sq_parts = pieces(half_sq, 3)
    row = lax.broadcasted_iota(jnp.int32, points.shape, 0)
    first = 0 if visiting else 3
    tail = jnp.where((row >= 3 - first) & (row < 6 - first), 1.0, 0.0)
    for k, part in enumerate(sq_parts):
        tail = jnp.where(row == first + k, part, tail)
    order = [big, big, big, mid, mid, low] if visiting else [big, mid, low, big, mid, big]
    return jnp.concatenate(order + [tail, jnp.zeros_like(tail)], axis=0)


def put_dirs(dirs_ref, at, value):
    both = jnp.concatenate(pieces(value, 2), axis=0).astype(BF16)
    dirs_ref[at] = jnp.concatenate([both, both], axis=1)


def swapped(value, far_by, near_by, core_by):
    length = lax.axis_size("row")
    _, near = digits()
    by = (far_by * near + near_by) * 2 + core_by
    return lax.ppermute(value, "row", [(i, i ^ by) for i in range(length)])


def turned(value, by):
    length = lax.axis_size("row")
    far, _ = digits()
    step = length // far
    return lax.ppermute(value, "row", [(i, (i - by * step) % length) for i in range(length)])


def digits():
    chips = lax.axis_size("row") // 2
    near = 1
    while near * near * 4 <= chips:
        near *= 2
    return chips // near, near


def gathered(value):
    far, near = digits()
    own = value[None]
    line = [turned(own, by) for by in range(1, far)]
    group = jnp.concatenate([own] + line, axis=0)
    across = swapped(group, 0, 0, 1)
    beside = [swapped(group, 0, by, 0) for by in range(1, near)]
    return [[own], line, [across], beside]


def held_back(groups, value):
    *beside, value = lax.optimization_barrier((*groups[3], value))
    return groups[:3] + [beside, [swapped(g, 0, 0, 1) for g in beside]], value


def along_line(value):
    far, _ = digits()
    return [turned(value, by) for by in range(1, far)]


def over_quad(value):
    _, near = digits()
    return [swapped(value, 0, by // 2, by % 2) for by in range(1, 2 * near)]


def tables():
    far, near = digits()
    place = lax.axis_index("row")
    core = place % 2
    picks = jnp.arange(far // 2, dtype=jnp.int32) * 2
    sides = [(place // 2 // (by & -by)) % 2 for by in range(1, near)]

    def listed(flip):
        def one(k, side):
            return k * far + picks + (side + flip) % 2

        return [
            one(0, core),
            jnp.concatenate([one(k, side) for k, side in enumerate(sides)]),
            jnp.concatenate([one(k, core) for k in range(near - 1)]),
        ]

    return listed(0), listed(1)


def add_block(yt_ref, at, own_ref, dirs_ref, slot, acc_ref, keep_ref=None, kept_at=None):
    width = own_ref.shape[1]
    for c in range(width // TILE):
        cols = slice(c * TILE, (c + 1) * TILE)
        expo = jnp.dot(yt_ref[at], own_ref[:, cols], preferred_element_type=F32)
        weight = jnp.exp2(expo)
        high = weight.astype(BF16)
        low = (weight - high.astype(F32)).astype(BF16)
        if keep_ref is not None:
            keep_ref[kept_at, c, 0:width, :] = high
            keep_ref[kept_at, c, width:, :] = low
        acc_ref[:, cols] += jnp.dot(
            dirs_ref[slot, :, 0:width], high, preferred_element_type=F32
        ) + jnp.dot(dirs_ref[slot, :, 0:width], low, preferred_element_type=F32)


def add_kept_block(keep_ref, at, dirs_ref, slot, acc_ref):
    for c in range(keep_ref.shape[1]):
        acc_ref[:, c * TILE : (c + 1) * TILE] += jnp.dot(
            dirs_ref[slot], keep_ref[at, c], preferred_element_type=F32
        )


def folded(acc_ref):
    nrhs = acc_ref.shape[0] // 2
    return acc_ref[0:nrhs, :] + acc_ref[nrhs:, :]


def unrolled(steps):
    return next(n for n in (4, 3, 2, 1) if steps % n == 0)


def repeated(steps, function):
    if steps <= 4:
        for k in range(steps):
            function(k)
    else:

        def step(k, carry):
            function(k)
            return carry

        lax.fori_loop(0, steps, step, 0, unroll=unrolled(steps))


def each(stacks, function):
    base = 0
    for ref in stacks:
        repeated(ref.shape[0], lambda b, ref=ref, base=base: function(base + b, ref[b]))
        base += ref.shape[0]


def join_kernel(scale_ref, features_ref, rhs_ref, out_ref):
    nfeat = features_ref.shape[0]
    row = lax.broadcasted_iota(jnp.int32, (nfeat, 128), 0)
    scale = jnp.zeros((nfeat, 128), F32)
    for k in range(nfeat):
        scale = jnp.where(row == k, scale_ref[k], scale)
    out_ref[0:nfeat, :] = features_ref[...] / scale[:, 0:1]
    out_ref[nfeat:, :] = rhs_ref[...]


def over_points(nfeat, nstacks, first, amplitude, kept, *refs):
    refs = list(refs)
    own_ref = refs.pop(0) if not first else None
    sofar_ref = refs.pop(0) if not first else None
    noise_ref, mine_ref = (refs.pop(0), refs.pop(0)) if amplitude else (None, None)
    stacks = refs[:nstacks]
    refs = refs[nstacks:]
    blocks = sum(ref.shape[0] for ref in stacks)
    if first:
        own_ref = refs.pop(0)
        own_ref[...] = exponent_rows(
            stacks[0][0, 0:nfeat, :], 1.0, False
        ).astype(BF16)
    out_ref = refs.pop(0)
    keep_ref = refs.pop(0) if kept else None
    yt_ref = refs.pop(0) if kept < blocks else None
    dirs_ref, acc_ref, *fresh = refs
    acc_ref[...] = jnp.zeros_like(acc_ref)

    def step(b, value):
        rows = exponent_rows(value[0:nfeat, :], LOG2E, True)
        put_dirs(dirs_ref, b, value[nfeat:, :])
        if kept and b < kept:
            fresh[0][b] = rows.T.astype(BF16)
            add_block(fresh[0], b, own_ref, dirs_ref, b, acc_ref, keep_ref, b)
        else:
            yt_ref[b - kept] = rows.T.astype(BF16)
            add_block(yt_ref, b - kept, own_ref, dirs_ref, b, acc_ref)

    each(stacks, step)
    total = folded(acc_ref)
    if not first:
        total = total + sofar_ref[...]
    if amplitude:
        total = amplitude * total + noise_ref[...] * mine_ref[0, nfeat:, :]
    out_ref[...] = total


def over_images(nstacks, table, sofar, form, amplitude, kept, blocks, *refs):
    refs = list(refs)
    table_ref = refs.pop(0) if table else None
    sofar_ref = refs.pop(0) if sofar else None
    if form:
        once_ref, noise_ref, mine_ref = refs.pop(0), refs.pop(0), refs.pop(0)
    keep_ref = refs.pop(0) if kept else None
    own_ref, yt_ref = (refs.pop(0), refs.pop(0)) if kept < blocks else (None, None)
    stacks = refs[:nstacks]
    out_ref, *refs = refs[nstacks:]
    form_ref = refs.pop(0) if form else None
    dirs_ref, acc_ref = refs
    acc_ref[...] = jnp.zeros_like(acc_ref)

    def add(at, slot, is_kept):
        if is_kept:
            add_kept_block(keep_ref, at, dirs_ref, slot, acc_ref)
        else:
            add_block(yt_ref, at - kept, own_ref, dirs_ref, slot, acc_ref)

    if table:
        if nstacks > 1:
            each(stacks, lambda b, value: put_dirs(dirs_ref, b, value))

        def step(s):
            b = table_ref[s]
            if nstacks == 1:
                put_dirs(dirs_ref, s, stacks[0][b])
            add(b, s if nstacks == 1 else b, bool(kept) and 2 * s + 1 < kept)

        repeated(table_ref.shape[0], step)
    else:

        def direct(b, value):
            put_dirs(dirs_ref, b, value)
            add(b, b, bool(kept) and b < kept)

        each(stacks, direct)
    total = folded(acc_ref)
    if sofar:
        total = total + sofar_ref[...]
    if form:
        mine = mine_ref[0]
        twice = once_ref[...] + 2.0 * total
        inner = mine * (amplitude * twice + noise_ref[...] * mine)
        form_ref[...] = jnp.broadcast_to(
            jnp.sum(inner, axis=1, keepdims=True), form_ref.shape
        )
        total = total + once_ref[...]
    out_ref[...] = total


def scalars_kernel(nfeat, count, *refs):
    blocks = refs[:count]
    images = refs[count : 2 * count]
    out_ref = refs[2 * count]
    nothing = jnp.zeros((images[0].shape[1], images[0].shape[2]), F32)

    def walk(function, carry):
        for b_ref, m_ref in zip(blocks, images):

            def block(k, carry, b_ref=b_ref, m_ref=m_ref):
                return function(carry, b_ref[k, nfeat:, :], m_ref[k])

            steps = b_ref.shape[0]
            carry = lax.fori_loop(0, steps, block, carry, unroll=unrolled(steps))
        return carry

    def total(value):
        return jnp.sum(value, axis=1, keepdims=True)

    norm, curv, square = walk(
        lambda c, r, w: (c[0] + r * r, c[1] + r * w, c[2] + w * w), (nothing,) * 3
    )
    norm, curv, square = total(norm), total(curv), total(square)
    alpha = norm / curv

    def left(carry, r, w):
        rest = r - alpha * w
        return carry + rest * rest

    norm_next = total(walk(left, nothing))
    gain = 1.0 + norm_next / norm
    part = gain * (gain * curv - 2.0 * alpha * square)
    for k, value in enumerate((alpha, gain, norm_next, part)):
        out_ref[k] = jnp.broadcast_to(value, out_ref.shape[1:])


def last_kernel(
    nfeat, amplitude, scalars_ref, form_ref, total_ref, noise_ref, mine_ref, image_ref,
    sol_ref, res_ref,
):
    alpha, gain, norm_next, part = [scalars_ref[k][:, 0:1] for k in range(4)]
    alpha_next = norm_next / (part + alpha * alpha * form_ref[:, 0:1])
    rhs = mine_ref[0, nfeat:, :]
    image = image_ref[0]
    twice = amplitude * total_ref[...] + noise_ref[...] * image
    sol_ref[...] = alpha * rhs + alpha_next * (gain * rhs - alpha * image)
    res_ref[...] = (rhs - alpha * image) - alpha_next * (gain * image - alpha * twice)


def shards(features, lengthscale, noise, rhs):
    nfeat, width = features.shape
    nrhs = rhs.shape[0]
    amplitude = 1.0 / math.sqrt(width * lax.axis_size("row"))
    noise = noise[None, :]
    field = jax.ShapeDtypeStruct((nrhs, width), F32)
    small = jax.ShapeDtypeStruct((nrhs, 128), F32)
    smem = pl.BlockSpec(memory_space=pltpu.SMEM)
    vmem = pl.BlockSpec(memory_space=pltpu.VMEM)

    def call(kernel, blocks, work, out_shape, operands, name, table=False, fresh=0):
        entries = work * width * width
        scratch = [
            pltpu.VMEM((blocks, 2 * nrhs, 2 * width), BF16),
            pltpu.VMEM((2 * nrhs, width), F32),
        ]
        if fresh:
            scratch.append(pltpu.VMEM((fresh, width, DEPTH), BF16))
        limit = 4 * MIB + blocks * 512 * width
        return pl.pallas_call(
            kernel,
            out_shape=out_shape,
            in_specs=[smem if table and k == 0 else vmem for k in range(len(operands))],
            scratch_shapes=scratch,
            compiler_params=pltpu.CompilerParams(vmem_limit_bytes=min(limit, 60 * MIB)),
            cost_estimate=pl.CostEstimate(
                flops=2 * entries * 4 * TILE, bytes_accessed=1024 * width, transcendentals=entries
            ),
            name=name,
        )(*operands)

    def amount(stacks):
        return sum(s.shape[0] for s in stacks)

    joined = pl.pallas_call(
        join_kernel,
        out_shape=jax.ShapeDtypeStruct((nfeat + nrhs, width), F32),
        in_specs=[smem, vmem, vmem],
        compiler_params=pltpu.CompilerParams(vmem_limit_bytes=4 * MIB),
        name="join",
    )(lengthscale, features, rhs)
    groups = gathered(joined)
    mine = groups[0][0]
    own_shape = jax.ShapeDtypeStruct((DEPTH, width), BF16)
    room = KEPT_ROOM - lax.axis_size("row") * 512 * width
    sizes = [amount(g) for g in groups]
    sizes.append(sizes[3])
    keep = [0] * len(sizes)
    for k in KEPT_ORDER:
        fit = max(room, 0) // (4 * width * width)
        blocks = sizes[k]
        keep[k] = blocks if blocks <= fit else fit // 2 * 2 if blocks <= 4 else 0
        room -= 4 * keep[k] * width * width
    own, total, prepared = None, None, []
    for k, blocks in enumerate(sizes):
        if k == 3:
            groups, total = held_back(groups, total)
        stacks = groups[k]
        final = k == len(sizes) - 1
        made = (own_shape,) * (k == 0) + (field,)
        if keep[k]:
            made += (pltpu.VMEM((keep[k], width // TILE, 2 * width, TILE), BF16),)
        if keep[k] < blocks:
            made += (jax.ShapeDtypeStruct((blocks - keep[k], width, DEPTH), BF16),)
        made = call(
            functools.partial(
                over_points, nfeat, len(stacks), k == 0, amplitude if final else None, keep[k]
            ),
            blocks, blocks, made,
            (() if k == 0 else (own, total)) + ((noise, mine) if final else ())
            + tuple(stacks),
            "blocks_%d" % k, fresh=keep[k],
        )
        if k == 0:
            own, *made = made
        total, *sources = made
        prepared.append(sources)
    images = gathered(total)
    image = images[0][0]

    def again(group, out, name, sofar=(), table=None, form=()):
        stacks = images[group]
        blocks = amount(stacks)
        listed = () if table is None else (table,)
        work = blocks if table is None else table.shape[0]
        sources = list(prepared[group])
        if keep[group]:
            sources[0] = pltpu.with_memory_space_constraint(sources[0], pltpu.VMEM)
        if keep[group] < blocks:
            sources.insert(len(sources) - 1, own)
        return call(
            functools.partial(
                over_images, len(stacks), table is not None, bool(sofar), bool(form), amplitude,
                keep[group], blocks,
            ),
            blocks, work, out,
            listed + tuple(sofar) + tuple(form) + tuple(sources) + tuple(stacks),
            name, table is not None,
        )

    halves, rests = tables()
    once = again(0, field, "own_again")
    once = again(1, field, "line_again", sofar=(once,))
    half = again(2, field, "across_half", table=halves[0])
    images, half = held_back(images, half)
    half = again(3, field, "beside_half", sofar=(half,), table=halves[1])
    total, form = again(
        4, (field, small), "far_half", sofar=(half,), table=halves[2], form=(once, noise, image)
    )
    parts = along_line(form)
    total = again(2, field, "across_rest", sofar=(total,), table=rests[0])
    total = again(3, field, "beside_rest", sofar=(total,), table=rests[1])
    *parts, total = lax.optimization_barrier((*parts, total))
    form = sum(parts, form)
    parts = over_quad(form)
    total = again(4, field, "far_rest", sofar=(total,), table=rests[2])
    *parts, total = lax.optimization_barrier((*parts, total))
    form = sum(parts, form)
    flat = [s for g in groups for s in g]
    flat_images = [s for g in images for s in g]
    scalars = pl.pallas_call(
        functools.partial(scalars_kernel, nfeat, len(flat)),
        out_shape=jax.ShapeDtypeStruct((4, nrhs, 128), F32),
        compiler_params=pltpu.CompilerParams(
            vmem_limit_bytes=4 * MIB + 96 * lax.axis_size("row") * width
        ),
        name="scalars",
    )(*flat, *flat_images)
    return pl.pallas_call(
        functools.partial(last_kernel, nfeat, amplitude),
        out_shape=(field, field),
        compiler_params=pltpu.CompilerParams(vmem_limit_bytes=4 * MIB),
        name="last_update",
    )(scalars, form, total, noise, mine, image)


def solution(mesh):
    in_specs = (P(None, ("grp", "row")), P(), P(("grp", "row")), P(None, ("grp", "row")))
    out_specs = (P(None, ("grp", "row")), P(None, ("grp", "row")))
    return jax.shard_map(shards, mesh=mesh, in_specs=in_specs, out_specs=out_specs, check_vma=False)
```

```python
import functools
import math

import jax
import jax.numpy as jnp
from jax import lax
from jax.experimental import pallas as pl
from jax.experimental.pallas import tpu as pltpu
from jax.sharding import PartitionSpec as P

LOG2E = math.log2(math.e)
DEPTH = 64
TILE = 256
MIB = 1024 * 1024
KEPT_ORDER = (2, 5, 4)
KEPT_ROOM = 44 * MIB
F32 = jnp.float32
BF16 = jnp.bfloat16


def pieces(value, count):
    parts = []
    for _ in range(count):
        part = value.astype(BF16).astype(F32)
        parts.append(part)
        value = value - part
    return parts


def exponent_rows(points, factor, visiting):
    big, mid, low = pieces(points * factor, 3)
    half_sq = jnp.sum(points * points, axis=0, keepdims=True) * (-0.5 * LOG2E)
    sq_parts = pieces(half_sq, 3)
    row = lax.broadcasted_iota(jnp.int32, points.shape, 0)
    first = 0 if visiting else 3
    tail = jnp.where((row >= 3 - first) & (row < 6 - first), 1.0, 0.0)
    for k, part in enumerate(sq_parts):
        tail = jnp.where(row == first + k, part, tail)
    order = [big, big, big, mid, mid, low] if visiting else [big, mid, low, big, mid, big]
    return jnp.concatenate(order + [tail, jnp.zeros_like(tail)], axis=0)


def put_dirs(dirs_ref, at, value):
    both = jnp.concatenate(pieces(value, 2), axis=0).astype(BF16)
    dirs_ref[at] = jnp.concatenate([both, both], axis=1)


def swapped(value, far_by, near_by, core_by):
    length = lax.axis_size("row")
    _, near = digits()
    by = (far_by * near + near_by) * 2 + core_by
    return lax.ppermute(value, "row", [(i, i ^ by) for i in range(length)])


def turned(value, by):
    length = lax.axis_size("row")
    far, _ = digits()
    step = length // far
    return lax.ppermute(value, "row", [(i, (i - by * step) % length) for i in range(length)])


def digits():
    chips = lax.axis_size("row") // 2
    near = 1
    while near * near * 4 <= chips:
        near *= 2
    return chips // near, near


def neighbours(value):
    far, _ = digits()
    own = value[None]
    return [[own], [swapped(own, 0, 0, 1)], [turned(own, by) for by in range(1, far)]]


def with_groups(groups, value):
    _, near = digits()
    *line, value = lax.optimization_barrier((*groups[2], value))
    stack = jnp.concatenate(line, axis=0)
    group = jnp.concatenate(groups[0] + line, axis=0)
    across = swapped(stack, 0, 0, 1)
    beside = [swapped(group, 0, by, 0) for by in range(1, near)]
    return groups[:2] + [line, [across], beside], value


def held_back(groups, value):
    *beside, value = lax.optimization_barrier((*groups[4], value))
    return groups[:4] + [beside, [swapped(g, 0, 0, 1) for g in beside]], value


def along_line(value):
    far, _ = digits()
    return [turned(value, by) for by in range(1, far)]


def over_quad(value):
    _, near = digits()
    return [swapped(value, 0, by // 2, by % 2) for by in range(1, 2 * near)]


def tables():
    far, near = digits()
    place = lax.axis_index("row")
    core = place % 2
    picks = jnp.arange(far // 2, dtype=jnp.int32) * 2
    sides = [(place // 2 // (by & -by)) % 2 for by in range(1, near)]

    def listed(flip):
        def one(k, side):
            return k * far + picks + (side + flip) % 2

        return [
            jnp.concatenate([one(k, side) for k, side in enumerate(sides)]),
            jnp.concatenate([one(k, core) for k in range(near - 1)]),
        ]

    return listed(0), listed(1)


def add_block(yt_ref, at, own_ref, dirs_ref, slot, acc_ref, keep_ref=None, kept_at=None):
    width = own_ref.shape[1]
    for c in range(width // TILE):
        cols = slice(c * TILE, (c + 1) * TILE)
        expo = jnp.dot(yt_ref[at], own_ref[:, cols], preferred_element_type=F32)
        weight = jnp.exp2(expo)
        high = weight.astype(BF16)
        low = (weight - high.astype(F32)).astype(BF16)
        if keep_ref is not None:
            keep_ref[kept_at, c, 0:width, :] = high
            keep_ref[kept_at, c, width:, :] = low
        acc_ref[:, cols] += jnp.dot(
            dirs_ref[slot, :, 0:width], high, preferred_element_type=F32
        ) + jnp.dot(dirs_ref[slot, :, 0:width], low, preferred_element_type=F32)


def add_kept_block(keep_ref, at, dirs_ref, slot, acc_ref):
    for c in range(keep_ref.shape[1]):
        acc_ref[:, c * TILE : (c + 1) * TILE] += jnp.dot(
            dirs_ref[slot], keep_ref[at, c], preferred_element_type=F32
        )


def folded(acc_ref):
    nrhs = acc_ref.shape[0] // 2
    return acc_ref[0:nrhs, :] + acc_ref[nrhs:, :]


def unrolled(steps):
    return next(n for n in (4, 3, 2, 1) if steps % n == 0)


def repeated(steps, function):
    if steps <= 4:
        for k in range(steps):
            function(k)
    else:

        def step(k, carry):
            function(k)
            return carry

        lax.fori_loop(0, steps, step, 0, unroll=unrolled(steps))


def each(stacks, function):
    base = 0
    for ref in stacks:
        repeated(ref.shape[0], lambda b, ref=ref, base=base: function(base + b, ref[b]))
        base += ref.shape[0]


def over_points(nfeat, nstacks, first, amplitude, kept, *refs):
    scale_ref, *refs = refs
    own_ref = refs.pop(0) if not first else None
    sofar_ref = refs.pop(0) if not first else None
    noise_ref, mine_ref = (refs.pop(0), refs.pop(0)) if amplitude else (None, None)
    stacks = refs[:nstacks]
    refs = refs[nstacks:]
    blocks = sum(ref.shape[0] for ref in stacks)
    if first:
        own_ref = refs.pop(0)
        own_ref[...] = exponent_rows(
            stacks[0][0, 0:nfeat, :] / scale_ref[...], 1.0, False
        ).astype(BF16)
    out_ref = refs.pop(0)
    keep_ref = refs.pop(0) if kept else None
    yt_ref = refs.pop(0) if kept < blocks else None
    dirs_ref, acc_ref, *fresh = refs
    acc_ref[...] = jnp.zeros_like(acc_ref)

    def step(b, value):
        rows = exponent_rows(value[0:nfeat, :] / scale_ref[...], LOG2E, True)
        put_dirs(dirs_ref, b, value[nfeat:, :])
        if kept and b < kept:
            fresh[0][b] = rows.T.astype(BF16)
            add_block(fresh[0], b, own_ref, dirs_ref, b, acc_ref, keep_ref, b)
        else:
            yt_ref[b - kept] = rows.T.astype(BF16)
            add_block(yt_ref, b - kept, own_ref, dirs_ref, b, acc_ref)

    each(stacks, step)
    total = folded(acc_ref)
    if not first:
        total = total + sofar_ref[...]
    if amplitude:
        total = amplitude * total + noise_ref[...] * mine_ref[0, nfeat:, :]
    out_ref[...] = total


def over_images(nstacks, table, sofar, form, amplitude, kept, blocks, *refs):
    refs = list(refs)
    table_ref = refs.pop(0) if table else None
    sofar_ref = refs.pop(0) if sofar else None
    if form:
        once_ref, noise_ref, mine_ref = refs.pop(0), refs.pop(0), refs.pop(0)
    keep_ref = refs.pop(0) if kept else None
    own_ref, yt_ref = (refs.pop(0), refs.pop(0)) if kept < blocks else (None, None)
    stacks = refs[:nstacks]
    out_ref, *refs = refs[nstacks:]
    form_ref = refs.pop(0) if form else None
    dirs_ref, acc_ref = refs
    acc_ref[...] = jnp.zeros_like(acc_ref)

    def add(at, slot, is_kept):
        if is_kept:
            add_kept_block(keep_ref, at, dirs_ref, slot, acc_ref)
        else:
            add_block(yt_ref, at - kept, own_ref, dirs_ref, slot, acc_ref)

    if table:
        if nstacks > 1:
            each(stacks, lambda b, value: put_dirs(dirs_ref, b, value))

        def step(s):
            b = table_ref[s]
            if nstacks == 1:
                put_dirs(dirs_ref, s, stacks[0][b])
            add(b, s if nstacks == 1 else b, bool(kept) and 2 * s + 1 < kept)

        repeated(table_ref.shape[0], step)
    else:

        def direct(b, value):
            put_dirs(dirs_ref, b, value)
            add(b, b, bool(kept) and b < kept)

        each(stacks, direct)
    total = folded(acc_ref)
    if sofar:
        total = total + sofar_ref[...]
    if form:
        mine = mine_ref[0]
        twice = once_ref[...] + 2.0 * total
        inner = mine * (amplitude * twice + noise_ref[...] * mine)
        form_ref[...] = jnp.broadcast_to(
            jnp.sum(inner, axis=1, keepdims=True), form_ref.shape
        )
        total = total + once_ref[...]
    out_ref[...] = total


def scalars_kernel(nfeat, count, *refs):
    blocks = refs[:count]
    images = refs[count : 2 * count]
    out_ref = refs[2 * count]
    nothing = jnp.zeros((images[0].shape[1], images[0].shape[2]), F32)

    def walk(function, carry):
        for b_ref, m_ref in zip(blocks, images):

            def block(k, carry, b_ref=b_ref, m_ref=m_ref):
                return function(carry, b_ref[k, nfeat:, :], m_ref[k])

            steps = b_ref.shape[0]
            carry = lax.fori_loop(0, steps, block, carry, unroll=unrolled(steps))
        return carry

    def total(value):
        return jnp.sum(value, axis=1, keepdims=True)

    norm, curv, square = walk(
        lambda c, r, w: (c[0] + r * r, c[1] + r * w, c[2] + w * w), (nothing,) * 3
    )
    norm, curv, square = total(norm), total(curv), total(square)
    alpha = norm / curv

    def left(carry, r, w):
        rest = r - alpha * w
        return carry + rest * rest

    norm_next = total(walk(left, nothing))
    gain = 1.0 + norm_next / norm
    part = gain * (gain * curv - 2.0 * alpha * square)
    for k, value in enumerate((alpha, gain, norm_next, part)):
        out_ref[k] = jnp.broadcast_to(value, out_ref.shape[1:])


def last_kernel(
    nfeat, amplitude, scalars_ref, form_ref, total_ref, noise_ref, mine_ref, image_ref,
    sol_ref, res_ref,
):
    alpha, gain, norm_next, part = [scalars_ref[k][:, 0:1] for k in range(4)]
    alpha_next = norm_next / (part + alpha * alpha * form_ref[:, 0:1])
    rhs = mine_ref[0, nfeat:, :]
    image = image_ref[0]
    twice = amplitude * total_ref[...] + noise_ref[...] * image
    sol_ref[...] = alpha * rhs + alpha_next * (gain * rhs - alpha * image)
    res_ref[...] = (rhs - alpha * image) - alpha_next * (gain * image - alpha * twice)


def shards(features, lengthscale, noise, rhs):
    nfeat, width = features.shape
    nrhs = rhs.shape[0]
    amplitude = 1.0 / math.sqrt(width * lax.axis_size("row"))
    scale = lengthscale[:, None]
    noise = noise[None, :]
    field = jax.ShapeDtypeStruct((nrhs, width), F32)
    small = jax.ShapeDtypeStruct((nrhs, 128), F32)
    smem = pl.BlockSpec(memory_space=pltpu.SMEM)
    vmem = pl.BlockSpec(memory_space=pltpu.VMEM)

    def call(kernel, blocks, work, out_shape, operands, name, table=False, fresh=0):
        entries = work * width * width
        scratch = [
            pltpu.VMEM((blocks, 2 * nrhs, 2 * width), BF16),
            pltpu.VMEM((2 * nrhs, width), F32),
        ]
        if fresh:
            scratch.append(pltpu.VMEM((fresh, width, DEPTH), BF16))
        limit = 4 * MIB + blocks * 512 * width
        return pl.pallas_call(
            kernel,
            out_shape=out_shape,
            in_specs=[smem if table and k == 0 else vmem for k in range(len(operands))],
            scratch_shapes=scratch,
            compiler_params=pltpu.CompilerParams(vmem_limit_bytes=min(limit, 60 * MIB)),
            cost_estimate=pl.CostEstimate(
                flops=2 * entries * 4 * TILE, bytes_accessed=1024 * width, transcendentals=entries
            ),
            name=name,
        )(*operands)

    def amount(stacks):
        return sum(s.shape[0] for s in stacks)

    groups = neighbours(jnp.concatenate([features, rhs], axis=0))
    mine = groups[0][0]
    own_shape = jax.ShapeDtypeStruct((DEPTH, width), BF16)
    room = KEPT_ROOM - lax.axis_size("row") * 512 * width
    far, near = digits()
    sizes = [1, 1, far - 1, far - 1, far * (near - 1), far * (near - 1)]
    keep = [0] * len(sizes)
    for k in KEPT_ORDER:
        fit = max(room, 0) // (4 * width * width)
        blocks = sizes[k]
        keep[k] = blocks if blocks <= fit else fit // 2 * 2 if blocks <= 4 else 0
        room -= 4 * keep[k] * width * width
    own, total, prepared = None, None, []
    for k, blocks in enumerate(sizes):
        if k == 2:
            groups, total = with_groups(groups, total)
        if k == 4:
            groups, total = held_back(groups, total)
        stacks = groups[k]
        final = k == len(sizes) - 1
        made = (own_shape,) * (k == 0) + (field,)
        if keep[k]:
            made += (pltpu.VMEM((keep[k], width // TILE, 2 * width, TILE), BF16),)
        if keep[k] < blocks:
            made += (jax.ShapeDtypeStruct((blocks - keep[k], width, DEPTH), BF16),)
        made = call(
            functools.partial(
                over_points, nfeat, len(stacks), k == 0, amplitude if final else None, keep[k]
            ),
            blocks, blocks, made,
            (scale,) + (() if k == 0 else (own, total)) + ((noise, mine) if final else ())
            + tuple(stacks),
            "blocks_%d" % k, fresh=keep[k],
        )
        if k == 0:
            own, *made = made
        total, *sources = made
        prepared.append(sources)
    images = neighbours(total)
    image = images[0][0]

    def again(group, out, name, sofar=(), table=None, form=()):
        stacks = images[group]
        blocks = sizes[group]
        listed = () if table is None else (table,)
        work = blocks if table is None else table.shape[0]
        sources = list(prepared[group])
        if keep[group]:
            sources[0] = pltpu.with_memory_space_constraint(sources[0], pltpu.VMEM)
        if keep[group] < blocks:
            sources.insert(len(sources) - 1, own)
        return call(
            functools.partial(
                over_images, len(stacks), table is not None, bool(sofar), bool(form), amplitude,
                keep[group], blocks,
            ),
            blocks, work, out,
            listed + tuple(sofar) + tuple(form) + tuple(sources) + tuple(stacks),
            name, table is not None,
        )

    halves, rests = tables()
    shifts = jnp.arange(far - 1, dtype=jnp.int32)
    middle = far // 2 - 1
    once = again(0, field, "own_again")
    once = again(1, field, "pair_again", sofar=(once,))
    images, once = with_groups(images, once)
    once = again(2, field, "line_again", sofar=(once,))
    once = again(3, field, "across_once", sofar=(once,), table=shifts[middle : middle + 1])
    half = again(3, field, "across_half", table=shifts[:middle])
    images, half = held_back(images, half)
    half = again(4, field, "beside_half", sofar=(half,), table=halves[0])
    total, form = again(
        5, (field, small), "far_half", sofar=(half,), table=halves[1], form=(once, noise, image)
    )
    parts = along_line(form)
    total = again(3, field, "across_rest", sofar=(total,), table=shifts[middle + 1 :])
    total = again(4, field, "beside_rest", sofar=(total,), table=rests[0])
    *parts, total = lax.optimization_barrier((*parts, total))
    form = sum(parts, form)
    parts = over_quad(form)
    total = again(5, field, "far_rest", sofar=(total,), table=rests[1])
    *parts, total = lax.optimization_barrier((*parts, total))
    form = sum(parts, form)
    flat = [s for g in groups for s in g]
    flat_images = [s for g in images for s in g]
    scalars = pl.pallas_call(
        functools.partial(scalars_kernel, nfeat, len(flat)),
        out_shape=jax.ShapeDtypeStruct((4, nrhs, 128), F32),
        compiler_params=pltpu.CompilerParams(
            vmem_limit_bytes=4 * MIB + 96 * lax.axis_size("row") * width
        ),
        name="scalars",
    )(*flat, *flat_images)
    return pl.pallas_call(
        functools.partial(last_kernel, nfeat, amplitude),
        out_shape=(field, field),
        compiler_params=pltpu.CompilerParams(vmem_limit_bytes=4 * MIB),
        name="last_update",
    )(scalars, form, total, noise, mine, image)


def solution(mesh):
    in_specs = (P(None, ("grp", "row")), P(), P(("grp", "row")), P(None, ("grp", "row")))
    out_specs = (P(None, ("grp", "row")), P(None, ("grp", "row")))
    return jax.shard_map(shards, mesh=mesh, in_specs=in_specs, out_specs=out_specs, check_vma=False)
```

```python
import functools
import math

import jax
import jax.numpy as jnp
from jax import lax
from jax.experimental import pallas as pl
from jax.experimental.pallas import tpu as pltpu
from jax.sharding import PartitionSpec as P

LOG2E = math.log2(math.e)
DEPTH = 64
TILE = 256
MIB = 1024 * 1024
KEPT_ORDER = (2, 5, 4)
KEPT_ROOM = 44 * MIB
F32 = jnp.float32
BF16 = jnp.bfloat16


def pieces(value, count):
    parts = []
    for _ in range(count):
        part = value.astype(BF16).astype(F32)
        parts.append(part)
        value = value - part
    return parts


def exponent_rows(points, factor, visiting):
    big, mid, low = pieces(points * factor, 3)
    half_sq = jnp.sum(points * points, axis=0, keepdims=True) * (-0.5 * LOG2E)
    sq_parts = pieces(half_sq, 3)
    row = lax.broadcasted_iota(jnp.int32, points.shape, 0)
    first = 0 if visiting else 3
    tail = jnp.where((row >= 3 - first) & (row < 6 - first), 1.0, 0.0)
    for k, part in enumerate(sq_parts):
        tail = jnp.where(row == first + k, part, tail)
    order = [big, big, big, mid, mid, low] if visiting else [big, mid, low, big, mid, big]
    return jnp.concatenate(order + [tail, jnp.zeros_like(tail)], axis=0)


def put_dirs(dirs_ref, at, value):
    both = jnp.concatenate(pieces(value, 2), axis=0).astype(BF16)
    dirs_ref[at] = jnp.concatenate([both, both], axis=1)


def swapped(value, far_by, near_by, core_by):
    length = lax.axis_size("row")
    _, near = digits()
    by = (far_by * near + near_by) * 2 + core_by
    return lax.ppermute(value, "row", [(i, i ^ by) for i in range(length)])


def turned(value, by):
    length = lax.axis_size("row")
    far, _ = digits()
    step = length // far
    return lax.ppermute(value, "row", [(i, (i - by * step) % length) for i in range(length)])


def digits():
    chips = lax.axis_size("row") // 2
    near = 1
    while near * near * 4 <= chips:
        near *= 2
    return chips // near, near


def neighbours(value):
    far, _ = digits()
    own = value[None]
    return [[own], [swapped(own, 0, 0, 1)], [turned(own, by) for by in range(1, far)]]


def with_groups(groups, value):
    _, near = digits()
    *line, value = lax.optimization_barrier((*groups[2], value))
    stack = jnp.concatenate(line, axis=0)
    group = jnp.concatenate(groups[0] + line, axis=0)
    across = swapped(stack, 0, 0, 1)
    beside = [swapped(group, 0, by, 0) for by in range(1, near)]
    return groups[:2] + [line, [across], beside], value


def gathered(value, done):
    far, near = digits()
    own = value[None]
    line = [turned(own, by) for by in range(1, far)]
    *line, done = lax.optimization_barrier((*line, done))
    group = jnp.concatenate([own] + line, axis=0)
    across = swapped(group, 0, 0, 1)
    beside = [swapped(group, 0, by, 0) for by in range(1, near)]
    return [[own], line, [across], beside], done


def held_back(groups, *values):
    near = len(groups[-1])
    tied = lax.optimization_barrier((*groups[-1], *values))
    beside = list(tied[:near])
    return (groups[:-1] + [beside, [swapped(g, 0, 0, 1) for g in beside]], *tied[near:])


def along_line(value):
    far, _ = digits()
    return [turned(value, by) for by in range(1, far)]


def over_quad(value):
    _, near = digits()
    return [swapped(value, 0, by // 2, by % 2) for by in range(1, 2 * near)]


def tables():
    far, near = digits()
    place = lax.axis_index("row")
    core = place % 2
    picks = jnp.arange(far // 2, dtype=jnp.int32) * 2
    sides = [(place // 2 // (by & -by)) % 2 for by in range(1, near)]

    def listed(flip):
        def one(k, side):
            return k * far + picks + (side + flip) % 2

        return [
            one(0, core),
            jnp.concatenate([one(k, side) for k, side in enumerate(sides)]),
            jnp.concatenate([one(k, core) for k in range(near - 1)]),
        ]

    return listed(0), listed(1)


def add_block(yt_ref, at, own_ref, dirs_ref, slot, acc_ref, keep_ref=None, kept_at=None):
    width = own_ref.shape[1]
    for c in range(width // TILE):
        cols = slice(c * TILE, (c + 1) * TILE)
        expo = jnp.dot(yt_ref[at], own_ref[:, cols], preferred_element_type=F32)
        weight = jnp.exp2(expo)
        high = weight.astype(BF16)
        low = (weight - high.astype(F32)).astype(BF16)
        if keep_ref is not None:
            keep_ref[kept_at, c, 0:width, :] = high
            keep_ref[kept_at, c, width:, :] = low
        acc_ref[:, cols] += jnp.dot(
            dirs_ref[slot, :, 0:width], high, preferred_element_type=F32
        ) + jnp.dot(dirs_ref[slot, :, 0:width], low, preferred_element_type=F32)


def add_kept_block(keep_ref, at, dirs_ref, slot, acc_ref):
    for c in range(keep_ref.shape[1]):
        acc_ref[:, c * TILE : (c + 1) * TILE] += jnp.dot(
            dirs_ref[slot], keep_ref[at, c], preferred_element_type=F32
        )


def folded(acc_ref):
    nrhs = acc_ref.shape[0] // 2
    return acc_ref[0:nrhs, :] + acc_ref[nrhs:, :]


def unrolled(steps):
    return next(n for n in (4, 3, 2, 1) if steps % n == 0)


def repeated(steps, function):
    if steps <= 4:
        for k in range(steps):
            function(k)
    else:

        def step(k, carry):
            function(k)
            return carry

        lax.fori_loop(0, steps, step, 0, unroll=unrolled(steps))


def each(stacks, function):
    base = 0
    for ref in stacks:
        repeated(ref.shape[0], lambda b, ref=ref, base=base: function(base + b, ref[b]))
        base += ref.shape[0]


def over_points(nfeat, nstacks, first, amplitude, kept, *refs):
    scale_ref, *refs = refs
    own_ref = refs.pop(0) if not first else None
    sofar_ref = refs.pop(0) if not first else None
    noise_ref, mine_ref = (refs.pop(0), refs.pop(0)) if amplitude else (None, None)
    stacks = refs[:nstacks]
    refs = refs[nstacks:]
    blocks = sum(ref.shape[0] for ref in stacks)
    if first:
        own_ref = refs.pop(0)
        own_ref[...] = exponent_rows(
            stacks[0][0, 0:nfeat, :] / scale_ref[...], 1.0, False
        ).astype(BF16)
    out_ref = refs.pop(0)
    keep_ref = refs.pop(0) if kept else None
    yt_ref = refs.pop(0) if kept < blocks else None
    dirs_ref, acc_ref, *fresh = refs
    acc_ref[...] = jnp.zeros_like(acc_ref)

    def step(b, value):
        rows = exponent_rows(value[0:nfeat, :] / scale_ref[...], LOG2E, True)
        put_dirs(dirs_ref, b, value[nfeat:, :])
        if kept and b < kept:
            fresh[0][b] = rows.T.astype(BF16)
            add_block(fresh[0], b, own_ref, dirs_ref, b, acc_ref, keep_ref, b)
        else:
            yt_ref[b - kept] = rows.T.astype(BF16)
            add_block(yt_ref, b - kept, own_ref, dirs_ref, b, acc_ref)

    each(stacks, step)
    total = folded(acc_ref)
    if not first:
        total = total + sofar_ref[...]
    if amplitude:
        total = amplitude * total + noise_ref[...] * mine_ref[0, nfeat:, :]
    out_ref[...] = total


def over_images(nstacks, table, sofar, form, amplitude, kept, blocks, *refs):
    refs = list(refs)
    table_ref = refs.pop(0) if table else None
    sofar_ref = refs.pop(0) if sofar else None
    if form:
        once_ref, noise_ref, mine_ref = refs.pop(0), refs.pop(0), refs.pop(0)
    keep_ref = refs.pop(0) if kept else None
    own_ref, yt_ref = (refs.pop(0), refs.pop(0)) if kept < blocks else (None, None)
    stacks = refs[:nstacks]
    out_ref, *refs = refs[nstacks:]
    form_ref = refs.pop(0) if form else None
    dirs_ref, acc_ref = refs
    acc_ref[...] = jnp.zeros_like(acc_ref)

    def add(at, slot, is_kept):
        if is_kept:
            add_kept_block(keep_ref, at, dirs_ref, slot, acc_ref)
        else:
            add_block(yt_ref, at - kept, own_ref, dirs_ref, slot, acc_ref)

    if table:
        if nstacks > 1:
            each(stacks, lambda b, value: put_dirs(dirs_ref, b, value))

        def step(s):
            b = table_ref[s]
            if nstacks == 1:
                put_dirs(dirs_ref, s, stacks[0][b])
            add(b, s if nstacks == 1 else b, bool(kept) and 2 * s + 1 < kept)

        repeated(table_ref.shape[0], step)
    else:

        def direct(b, value):
            put_dirs(dirs_ref, b, value)
            add(b, b, bool(kept) and b < kept)

        each(stacks, direct)
    total = folded(acc_ref)
    if sofar:
        total = total + sofar_ref[...]
    if form:
        mine = mine_ref[0]
        twice = once_ref[...] + 2.0 * total
        inner = mine * (amplitude * twice + noise_ref[...] * mine)
        form_ref[...] = jnp.broadcast_to(
            jnp.sum(inner, axis=1, keepdims=True), form_ref.shape
        )
        total = total + once_ref[...]
    out_ref[...] = total


def scalars_kernel(nfeat, count, *refs):
    blocks = refs[:count]
    images = refs[count : 2 * count]
    out_ref = refs[2 * count]
    nothing = jnp.zeros((images[0].shape[1], images[0].shape[2]), F32)

    def walk(function, carry):
        for b_ref, m_ref in zip(blocks, images):

            def block(k, carry, b_ref=b_ref, m_ref=m_ref):
                return function(carry, b_ref[k, nfeat:, :], m_ref[k])

            steps = b_ref.shape[0]
            carry = lax.fori_loop(0, steps, block, carry, unroll=unrolled(steps))
        return carry

    def total(value):
        return jnp.sum(value, axis=1, keepdims=True)

    norm, curv, square = walk(
        lambda c, r, w: (c[0] + r * r, c[1] + r * w, c[2] + w * w), (nothing,) * 3
    )
    norm, curv, square = total(norm), total(curv), total(square)
    alpha = norm / curv

    def left(carry, r, w):
        rest = r - alpha * w
        return carry + rest * rest

    norm_next = total(walk(left, nothing))
    gain = 1.0 + norm_next / norm
    part = gain * (gain * curv - 2.0 * alpha * square)
    for k, value in enumerate((alpha, gain, norm_next, part)):
        out_ref[k] = jnp.broadcast_to(value, out_ref.shape[1:])


def last_kernel(
    nfeat, amplitude, scalars_ref, form_ref, total_ref, noise_ref, mine_ref, image_ref,
    sol_ref, res_ref,
):
    alpha, gain, norm_next, part = [scalars_ref[k][:, 0:1] for k in range(4)]
    alpha_next = norm_next / (part + alpha * alpha * form_ref[:, 0:1])
    rhs = mine_ref[0, nfeat:, :]
    image = image_ref[0]
    twice = amplitude * total_ref[...] + noise_ref[...] * image
    sol_ref[...] = alpha * rhs + alpha_next * (gain * rhs - alpha * image)
    res_ref[...] = (rhs - alpha * image) - alpha_next * (gain * image - alpha * twice)


def shards(features, lengthscale, noise, rhs):
    nfeat, width = features.shape
    nrhs = rhs.shape[0]
    amplitude = 1.0 / math.sqrt(width * lax.axis_size("row"))
    scale = lengthscale[:, None]
    noise = noise[None, :]
    field = jax.ShapeDtypeStruct((nrhs, width), F32)
    small = jax.ShapeDtypeStruct((nrhs, 128), F32)
    smem = pl.BlockSpec(memory_space=pltpu.SMEM)
    vmem = pl.BlockSpec(memory_space=pltpu.VMEM)

    def call(kernel, blocks, work, out_shape, operands, name, table=False, fresh=0):
        entries = work * width * width
        scratch = [
            pltpu.VMEM((blocks, 2 * nrhs, 2 * width), BF16),
            pltpu.VMEM((2 * nrhs, width), F32),
        ]
        if fresh:
            scratch.append(pltpu.VMEM((fresh, width, DEPTH), BF16))
        limit = 4 * MIB + blocks * 512 * width
        return pl.pallas_call(
            kernel,
            out_shape=out_shape,
            in_specs=[smem if table and k == 0 else vmem for k in range(len(operands))],
            scratch_shapes=scratch,
            compiler_params=pltpu.CompilerParams(vmem_limit_bytes=min(limit, 60 * MIB)),
            cost_estimate=pl.CostEstimate(
                flops=2 * entries * TILE, bytes_accessed=1024 * width, transcendentals=0
            ),
            name=name,
        )(*operands)

    def amount(stacks):
        return sum(s.shape[0] for s in stacks)

    groups = neighbours(jnp.concatenate([features, rhs], axis=0))
    mine = groups[0][0]
    own_shape = jax.ShapeDtypeStruct((DEPTH, width), BF16)
    room = KEPT_ROOM - lax.axis_size("row") * 512 * width
    far, near = digits()
    sizes = [1, 1, far - 1, far - 1, far * (near - 1), far * (near - 1)]
    keep = [0] * len(sizes)
    for k in KEPT_ORDER:
        fit = max(room, 0) // (4 * width * width)
        blocks = sizes[k]
        keep[k] = blocks if blocks <= fit else fit // 2 * 2 if blocks <= 4 else 0
        room -= 4 * keep[k] * width * width
    own, total, prepared = None, None, []
    for k, blocks in enumerate(sizes):
        if k == 2:
            groups, total = with_groups(groups, total)
        if k == 4:
            groups, total = held_back(groups, total)
        stacks = groups[k]
        final = k == len(sizes) - 1
        made = (own_shape,) * (k == 0) + (field,)
        if keep[k]:
            made += (pltpu.VMEM((keep[k], width // TILE, 2 * width, TILE), BF16),)
        if keep[k] < blocks:
            made += (jax.ShapeDtypeStruct((blocks - keep[k], width, DEPTH), BF16),)
        made = call(
            functools.partial(
                over_points, nfeat, len(stacks), k == 0, amplitude if final else None, keep[k]
            ),
            blocks, blocks, made,
            (scale,) + (() if k == 0 else (own, total)) + ((noise, mine) if final else ())
            + tuple(stacks),
            "blocks_%d" % k, fresh=keep[k],
        )
        if k == 0:
            own, *made = made
        total, *sources = made
        prepared.append(sources)
    images = [[total[None]]]
    across_points = jnp.concatenate([prepared[1][0], prepared[3][0]], axis=0)
    prepared = [prepared[0], prepared[2], [across_points]] + prepared[4:]
    keep = [keep[0], keep[2], 0] + keep[4:]
    sizes = [sizes[0], sizes[2], far] + sizes[4:]
    image = images[0][0]

    def again(group, out, name, sofar=(), table=None, form=()):
        stacks = images[group]
        blocks = sizes[group]
        listed = () if table is None else (table,)
        work = blocks if table is None else table.shape[0]
        sources = list(prepared[group])
        if keep[group]:
            sources[0] = pltpu.with_memory_space_constraint(sources[0], pltpu.VMEM)
        if keep[group] < blocks:
            sources.insert(len(sources) - 1, own)
        return call(
            functools.partial(
                over_images, len(stacks), table is not None, bool(sofar), bool(form), amplitude,
                keep[group], blocks,
            ),
            blocks, work, out,
            listed + tuple(sofar) + tuple(form) + tuple(sources) + tuple(stacks),
            name, table is not None,
        )

    halves, rests = tables()
    once = again(0, field, "own_again")
    images, once = gathered(total, once)
    once = again(1, field, "line_again", sofar=(once,))
    half = again(2, field, "across_half", table=halves[0])
    images, half, once = held_back(images, half, once)
    half = again(3, field, "beside_half", sofar=(half,), table=halves[1])
    total, form = again(
        4, (field, small), "far_half", sofar=(half,), table=halves[2], form=(once, noise, image)
    )
    parts = along_line(form)
    total = again(2, field, "across_rest", sofar=(total,), table=rests[0])
    total = again(3, field, "beside_rest", sofar=(total,), table=rests[1])
    *parts, total = lax.optimization_barrier((*parts, total))
    form = sum(parts, form)
    parts = over_quad(form)
    total = again(4, field, "far_rest", sofar=(total,), table=rests[2])
    *parts, total = lax.optimization_barrier((*parts, total))
    form = sum(parts, form)
    flat = [s for g in groups for s in g]
    own_images, line_images, (core_image,), beside_images, far_images = images
    flat_images = own_images + [core_image[:1]] + line_images + [core_image[1:]]
    flat_images += beside_images + far_images
    scalars = pl.pallas_call(
        functools.partial(scalars_kernel, nfeat, len(flat)),
        out_shape=jax.ShapeDtypeStruct((4, nrhs, 128), F32),
        compiler_params=pltpu.CompilerParams(
            vmem_limit_bytes=4 * MIB + 96 * lax.axis_size("row") * width
        ),
        name="scalars",
    )(*flat, *flat_images)
    return pl.pallas_call(
        functools.partial(last_kernel, nfeat, amplitude),
        out_shape=(field, field),
        compiler_params=pltpu.CompilerParams(vmem_limit_bytes=4 * MIB),
        name="last_update",
    )(scalars, form, total, noise, mine, image)


def solution(mesh):
    in_specs = (P(None, ("grp", "row")), P(), P(("grp", "row")), P(None, ("grp", "row")))
    out_specs = (P(None, ("grp", "row")), P(None, ("grp", "row")))
    return jax.shard_map(shards, mesh=mesh, in_specs=in_specs, out_specs=out_specs, check_vma=False)
```

```python
import functools
import math

import jax
import jax.numpy as jnp
from jax import lax
from jax.experimental import pallas as pl
from jax.experimental.pallas import tpu as pltpu
from jax.sharding import PartitionSpec as P

LOG2E = math.log2(math.e)
DEPTH = 64
TILE = 256
MIB = 1024 * 1024
KEPT_ORDER = (2, 4, 3)
KEPT_ROOM = 48 * MIB
F32 = jnp.float32
BF16 = jnp.bfloat16


def pieces(value, count):
    parts = []
    for _ in range(count):
        part = value.astype(BF16).astype(F32)
        parts.append(part)
        value = value - part
    return parts


def exponent_rows(points, factor, visiting):
    big, mid, low = pieces(points * factor, 3)
    half_sq = jnp.sum(points * points, axis=0, keepdims=True) * (-0.5 * LOG2E)
    sq_parts = pieces(half_sq, 3)
    row = lax.broadcasted_iota(jnp.int32, points.shape, 0)
    first = 0 if visiting else 3
    tail = jnp.where((row >= 3 - first) & (row < 6 - first), 1.0, 0.0)
    for k, part in enumerate(sq_parts):
        tail = jnp.where(row == first + k, part, tail)
    order = [big, big, big, mid, mid, low] if visiting else [big, mid, low, big, mid, big]
    return jnp.concatenate(order + [tail, jnp.zeros_like(tail)], axis=0)


def put_dirs(dirs_ref, at, value):
    both = jnp.concatenate(pieces(value, 2), axis=0).astype(BF16)
    dirs_ref[at] = jnp.concatenate([both, both], axis=1)


def swapped(value, far_by, near_by, core_by):
    length = lax.axis_size("row")
    _, near = digits()
    by = (far_by * near + near_by) * 2 + core_by
    return lax.ppermute(value, "row", [(i, i ^ by) for i in range(length)])


def turned(value, by):
    length = lax.axis_size("row")
    far, _ = digits()
    step = length // far
    return lax.ppermute(value, "row", [(i, (i - by * step) % length) for i in range(length)])


def digits():
    chips = lax.axis_size("row") // 2
    near = 1
    while near * near * 4 <= chips:
        near *= 2
    return chips // near, near


def gathered(value):
    far, near = digits()
    own = value[None]
    line = [turned(own, by) for by in range(1, far)]
    group = jnp.concatenate([own] + line, axis=0)
    across = swapped(group, 0, 0, 1)
    beside = [swapped(group, 0, by, 0) for by in range(1, near)]
    return [[own], line, [across], beside]


def held_back(groups, value):
    *beside, value = lax.optimization_barrier((*groups[3], value))
    return groups[:3] + [beside, [swapped(g, 0, 0, 1) for g in beside]], value


def along_line(value):
    far, _ = digits()
    return [turned(value, by) for by in range(1, far)]


def over_quad(value):
    _, near = digits()
    return [swapped(value, 0, by // 2, by % 2) for by in range(1, 2 * near)]


def tables():
    far, near = digits()
    place = lax.axis_index("row")
    core = place % 2
    picks = jnp.arange(far // 2, dtype=jnp.int32) * 2
    sides = [(place // 2 // (by & -by)) % 2 for by in range(1, near)]

    def listed(flip):
        def one(k, side):
            return k * far + picks + (side + flip) % 2

        return [
            one(0, core),
            jnp.concatenate([one(k, side) for k, side in enumerate(sides)]),
            jnp.concatenate([one(k, core) for k in range(near - 1)]),
        ]

    return listed(0), listed(1)


def add_block(yt_ref, at, own_ref, dirs_ref, slot, acc_ref, keep_ref=None, kept_at=None):
    width = own_ref.shape[1]
    for c in range(width // TILE):
        cols = slice(c * TILE, (c + 1) * TILE)
        expo = jnp.dot(yt_ref[at], own_ref[:, cols], preferred_element_type=F32)
        weight = jnp.exp2(expo)
        high = weight.astype(BF16)
        low = (weight - high.astype(F32)).astype(BF16)
        if keep_ref is not None:
            keep_ref[kept_at, c, 0:width, :] = high
            keep_ref[kept_at, c, width:, :] = low
        acc_ref[:, cols] += jnp.dot(
            dirs_ref[slot, :, 0:width], high, preferred_element_type=F32
        ) + jnp.dot(dirs_ref[slot, :, 0:width], low, preferred_element_type=F32)


def add_kept_block(keep_ref, at, dirs_ref, slot, acc_ref):
    for c in range(keep_ref.shape[1]):
        acc_ref[:, c * TILE : (c + 1) * TILE] += jnp.dot(
            dirs_ref[slot], keep_ref[at, c], preferred_element_type=F32
        )


def folded(acc_ref):
    nrhs = acc_ref.shape[0] // 2
    return acc_ref[0:nrhs, :] + acc_ref[nrhs:, :]


def unrolled(steps):
    return next(n for n in (4, 3, 2, 1) if steps % n == 0)


def repeated(steps, function):
    if steps <= 4:
        for k in range(steps):
            function(k)
    else:

        def step(k, carry):
            function(k)
            return carry

        lax.fori_loop(0, steps, step, 0, unroll=unrolled(steps))


def each(stacks, function):
    base = 0
    for ref in stacks:
        repeated(ref.shape[0], lambda b, ref=ref, base=base: function(base + b, ref[b]))
        base += ref.shape[0]


def over_points(nfeat, nstacks, first, amplitude, kept, *refs):
    scale_ref, *refs = refs
    own_ref = refs.pop(0) if not first else None
    sofar_ref = refs.pop(0) if not first else None
    noise_ref, mine_ref = (refs.pop(0), refs.pop(0)) if amplitude else (None, None)
    stacks = refs[:nstacks]
    refs = refs[nstacks:]
    blocks = sum(ref.shape[0] for ref in stacks)
    if first:
        own_ref = refs.pop(0)
        own_ref[...] = exponent_rows(
            stacks[0][0, 0:nfeat, :] / scale_ref[...], 1.0, False
        ).astype(BF16)
    out_ref = refs.pop(0)
    keep_ref = refs.pop(0) if kept else None
    yt_ref = refs.pop(0) if kept < blocks else None
    dirs_ref, acc_ref, *fresh = refs
    acc_ref[...] = jnp.zeros_like(acc_ref)

    def step(b, value):
        rows = exponent_rows(value[0:nfeat, :] / scale_ref[...], LOG2E, True)
        put_dirs(dirs_ref, b, value[nfeat:, :])
        if kept and b < kept:
            fresh[0][b] = rows.T.astype(BF16)
            add_block(fresh[0], b, own_ref, dirs_ref, b, acc_ref, keep_ref, b)
        else:
            yt_ref[b - kept] = rows.T.astype(BF16)
            add_block(yt_ref, b - kept, own_ref, dirs_ref, b, acc_ref)

    each(stacks, step)
    total = folded(acc_ref)
    if not first:
        total = total + sofar_ref[...]
    if amplitude:
        total = amplitude * total + noise_ref[...] * mine_ref[0, nfeat:, :]
    out_ref[...] = total


def over_images(nstacks, table, sofar, form, amplitude, kept, blocks, *refs):
    refs = list(refs)
    table_ref = refs.pop(0) if table else None
    sofar_ref = refs.pop(0) if sofar else None
    if form:
        once_ref, noise_ref, mine_ref = refs.pop(0), refs.pop(0), refs.pop(0)
    keep_ref = refs.pop(0) if kept else None
    own_ref, yt_ref = (refs.pop(0), refs.pop(0)) if kept < blocks else (None, None)
    stacks = refs[:nstacks]
    out_ref, *refs = refs[nstacks:]
    form_ref = refs.pop(0) if form else None
    dirs_ref, acc_ref = refs
    acc_ref[...] = jnp.zeros_like(acc_ref)

    def add(at, slot, is_kept):
        if is_kept:
            add_kept_block(keep_ref, at, dirs_ref, slot, acc_ref)
        else:
            add_block(yt_ref, at - kept, own_ref, dirs_ref, slot, acc_ref)

    if table:
        if nstacks > 1:
            each(stacks, lambda b, value: put_dirs(dirs_ref, b, value))

        def step(s):
            b = table_ref[s]
            if nstacks == 1:
                put_dirs(dirs_ref, s, stacks[0][b])
            add(b, s if nstacks == 1 else b, bool(kept) and 2 * s + 1 < kept)

        repeated(table_ref.shape[0], step)
    else:

        def direct(b, value):
            put_dirs(dirs_ref, b, value)
            add(b, b, bool(kept) and b < kept)

        each(stacks, direct)
    total = folded(acc_ref)
    if sofar:
        total = total + sofar_ref[...]
    if form:
        mine = mine_ref[0]
        twice = once_ref[...] + 2.0 * total
        inner = mine * (amplitude * twice + noise_ref[...] * mine)
        form_ref[...] = jnp.broadcast_to(
            jnp.sum(inner, axis=1, keepdims=True), form_ref.shape
        )
        total = total + once_ref[...]
    out_ref[...] = total


def scalars_kernel(nfeat, count, *refs):
    blocks = refs[:count]
    images = refs[count : 2 * count]
    out_ref = refs[2 * count]
    nothing = jnp.zeros((images[0].shape[1], images[0].shape[2]), F32)

    def walk(function, carry):
        for b_ref, m_ref in zip(blocks, images):

            def block(k, carry, b_ref=b_ref, m_ref=m_ref):
                return function(carry, b_ref[k, nfeat:, :], m_ref[k])

            steps = b_ref.shape[0]
            carry = lax.fori_loop(0, steps, block, carry, unroll=unrolled(steps))
        return carry

    def total(value):
        return jnp.sum(value, axis=1, keepdims=True)

    norm, curv, square = walk(
        lambda c, r, w: (c[0] + r * r, c[1] + r * w, c[2] + w * w), (nothing,) * 3
    )
    norm, curv, square = total(norm), total(curv), total(square)
    alpha = norm / curv

    def left(carry, r, w):
        rest = r - alpha * w
        return carry + rest * rest

    norm_next = total(walk(left, nothing))
    gain = 1.0 + norm_next / norm
    part = gain * (gain * curv - 2.0 * alpha * square)
    for k, value in enumerate((alpha, gain, norm_next, part)):
        out_ref[k] = jnp.broadcast_to(value, out_ref.shape[1:])


def last_kernel(
    nfeat, amplitude, scalars_ref, form_ref, total_ref, noise_ref, mine_ref, image_ref,
    sol_ref, res_ref,
):
    alpha, gain, norm_next, part = [scalars_ref[k][:, 0:1] for k in range(4)]
    alpha_next = norm_next / (part + alpha * alpha * form_ref[:, 0:1])
    rhs = mine_ref[0, nfeat:, :]
    image = image_ref[0]
    twice = amplitude * total_ref[...] + noise_ref[...] * image
    sol_ref[...] = alpha * rhs + alpha_next * (gain * rhs - alpha * image)
    res_ref[...] = (rhs - alpha * image) - alpha_next * (gain * image - alpha * twice)


def shards(features, lengthscale, noise, rhs):
    nfeat, width = features.shape
    nrhs = rhs.shape[0]
    amplitude = 1.0 / math.sqrt(width * lax.axis_size("row"))
    scale = lengthscale[:, None]
    noise = noise[None, :]
    field = jax.ShapeDtypeStruct((nrhs, width), F32)
    small = jax.ShapeDtypeStruct((nrhs, 128), F32)
    smem = pl.BlockSpec(memory_space=pltpu.SMEM)
    vmem = pl.BlockSpec(memory_space=pltpu.VMEM)

    def call(kernel, blocks, work, out_shape, operands, name, table=False, fresh=0):
        entries = work * width * width
        scratch = [
            pltpu.VMEM((blocks, 2 * nrhs, 2 * width), BF16),
            pltpu.VMEM((2 * nrhs, width), F32),
        ]
        if fresh:
            scratch.append(pltpu.VMEM((fresh, width, DEPTH), BF16))
        limit = 4 * MIB + blocks * 512 * width
        return pl.pallas_call(
            kernel,
            out_shape=out_shape,
            in_specs=[smem if table and k == 0 else vmem for k in range(len(operands))],
            scratch_shapes=scratch,
            compiler_params=pltpu.CompilerParams(vmem_limit_bytes=min(limit, 60 * MIB)),
            cost_estimate=pl.CostEstimate(
                flops=2 * entries * 4 * TILE, bytes_accessed=1024 * width, transcendentals=entries
            ),
            name=name,
        )(*operands)

    def amount(stacks):
        return sum(s.shape[0] for s in stacks)

    groups = gathered(jnp.concatenate([features, rhs], axis=0))
    mine = groups[0][0]
    own_shape = jax.ShapeDtypeStruct((DEPTH, width), BF16)
    room = KEPT_ROOM - lax.axis_size("row") * 512 * width
    sizes = [amount(g) for g in groups]
    sizes.append(sizes[3])
    keep = [0] * len(sizes)
    for k in KEPT_ORDER:
        fit = max(room, 0) // (4 * width * width)
        blocks = sizes[k]
        keep[k] = blocks if blocks <= fit else fit // 2 * 2 if blocks <= 4 else 0
        room -= 4 * keep[k] * width * width
    own, total, prepared = None, None, []
    for k, blocks in enumerate(sizes):
        if k == 3:
            groups, total = held_back(groups, total)
        stacks = groups[k]
        final = k == len(sizes) - 1
        made = (own_shape,) * (k == 0) + (field,)
        if keep[k]:
            made += (pltpu.VMEM((keep[k], width // TILE, 2 * width, TILE), BF16),)
        if keep[k] < blocks:
            made += (jax.ShapeDtypeStruct((blocks - keep[k], width, DEPTH), BF16),)
        made = call(
            functools.partial(
                over_points, nfeat, len(stacks), k == 0, amplitude if final else None, keep[k]
            ),
            blocks, blocks, made,
            (scale,) + (() if k == 0 else (own, total)) + ((noise, mine) if final else ())
            + tuple(stacks),
            "blocks_%d" % k, fresh=keep[k],
        )
        if k == 0:
            own, *made = made
        total, *sources = made
        prepared.append(sources)
    images = gathered(total)
    image = images[0][0]

    def again(group, out, name, sofar=(), table=None, form=()):
        stacks = images[group]
        blocks = amount(stacks)
        listed = () if table is None else (table,)
        work = blocks if table is None else table.shape[0]
        sources = list(prepared[group])
        if keep[group]:
            sources[0] = pltpu.with_memory_space_constraint(sources[0], pltpu.VMEM)
        if keep[group] < blocks:
            sources.insert(len(sources) - 1, own)
        return call(
            functools.partial(
                over_images, len(stacks), table is not None, bool(sofar), bool(form), amplitude,
                keep[group], blocks,
            ),
            blocks, work, out,
            listed + tuple(sofar) + tuple(form) + tuple(sources) + tuple(stacks),
            name, table is not None,
        )

    halves, rests = tables()
    once = again(0, field, "own_again")
    once = again(1, field, "line_again", sofar=(once,))
    half = again(2, field, "across_half", table=halves[0])
    images, half = held_back(images, half)
    half = again(3, field, "beside_half", sofar=(half,), table=halves[1])
    total, form = again(
        4, (field, small), "far_half", sofar=(half,), table=halves[2], form=(once, noise, image)
    )
    parts = along_line(form)
    total = again(2, field, "across_rest", sofar=(total,), table=rests[0])
    total = again(3, field, "beside_rest", sofar=(total,), table=rests[1])
    *parts, total = lax.optimization_barrier((*parts, total))
    form = sum(parts, form)
    parts = over_quad(form)
    total = again(4, field, "far_rest", sofar=(total,), table=rests[2])
    *parts, total = lax.optimization_barrier((*parts, total))
    form = sum(parts, form)
    flat = [s for g in groups for s in g]
    flat_images = [s for g in images for s in g]
    scalars = pl.pallas_call(
        functools.partial(scalars_kernel, nfeat, len(flat)),
        out_shape=jax.ShapeDtypeStruct((4, nrhs, 128), F32),
        compiler_params=pltpu.CompilerParams(
            vmem_limit_bytes=4 * MIB + 96 * lax.axis_size("row") * width
        ),
        name="scalars",
    )(*flat, *flat_images)
    return pl.pallas_call(
        functools.partial(last_kernel, nfeat, amplitude),
        out_shape=(field, field),
        compiler_params=pltpu.CompilerParams(vmem_limit_bytes=4 * MIB),
        name="last_update",
    )(scalars, form, total, noise, mine, image)


def solution(mesh):
    in_specs = (P(None, ("grp", "row")), P(), P(("grp", "row")), P(None, ("grp", "row")))
    out_specs = (P(None, ("grp", "row")), P(None, ("grp", "row")))
    return jax.shard_map(shards, mesh=mesh, in_specs=in_specs, out_specs=out_specs, check_vma=False)
```
